128 devices in a mesh: dp: 8 (over y_hi, z), seq: 16 (over x, y_lo, core).
Axes of the slice: x: 4, y: 4 (y_hi: 2, y_lo: 2; y = y_hi * 2 + y_lo), z: 4, core: 2. Of those that a mesh axis runs over, the one named last changes fastest.
Arguments:
- points: bfloat16 [8, 16384, 512], P('dp', 'seq'), may hold values from -6 to 6
- ball_lists: int32 [8, 16384], P('dp', 'seq'), may hold values from 0 to 1023, as said below
- gains: float32 [2, 512], replicated, may hold values from 0.25 to 1.75
- w_qkv: bfloat16 [2, 512, 1536], replicated, may hold values from -0.25 to 0.25
- w_out: bfloat16 [2, 512, 512], replicated, may hold values from -0.25 to 0.25
- cotangent: bfloat16 [8, 16384, 512], P('dp', 'seq'), may hold values from -6 to 6
Outputs:
- mixed: bfloat16 [8, 16384, 512], P('dp', 'seq')
- grad_points: bfloat16 [8, 16384, 512], P('dp', 'seq')
- grad_gains: float32 [2, 512], replicated
- grad_qkv: float32 [2, 512, 1536], replicated
- grad_out: float32 [2, 512, 512], replicated
The draws below stay inside these ranges and needn't reach their ends.
Inputs may be any that keep to these rules, and one draw needn't show every extreme that they name: `ball_lists`: for each snapshot and each index s of seq, its 1024 entries are a permutation of 0 to 1023; so every rotated block of 1024 positions takes exactly 64 points from each index of seq.
All inputs are finite; a program needn't handle non-finite values.
Results may differ from the reference program's by a relative error of at most 0.017.
Values may be sent and summed in bfloat16 or wider, within the bound.
A program may use at most 128 MiB of HBM per device.

```python
import jax
import jax.numpy as jnp
from jax import lax

C = 512
HEADS = 8
BALL = 256
P_DEV = 1024
POINTS = 16384
BLK = 64
SNAPS = 8


def draw_ball_lists(key, part):
    key = jax.random.fold_in(key, 11)
    groups = POINTS // P_DEV
    scores = jax.random.randint(key, (SNAPS, groups, P_DEV), 0, 1 << 16, dtype=jnp.int32) * P_DEV
    scores = scores + jnp.arange(P_DEV, dtype=jnp.int32)
    return jnp.argsort(scores, axis=-1).astype(jnp.int32).reshape(SNAPS, POINTS)


def block_levels(stream_key, dims, split, smallest, largest):
    level, own = 1.0, jax.random.fold_in(stream_key, 6)
    for position, blocks in split:
        heights = jnp.exp(jax.random.uniform(jax.random.fold_in(own, position), (blocks,), jnp.float32, smallest / len(split), largest / len(split)))
        level = level * jnp.repeat(heights, dims[position] // blocks).reshape([-1 if axis == position else 1 for axis in range(len(dims))])
    return level


def noise(own_key, shape, spread, bound, split=(), held_as=jnp.bfloat16):
    drawn = jax.random.normal(own_key, shape, jnp.float32) * spread
    if len(split) > 0:
        drawn = block_levels(own_key, shape, split, -0.22, 0.18) * drawn
    return jnp.clip(drawn, min=-bound, max=bound).astype(held_as)


def setup_inputs(seed: int = 0) -> dict:
    seeds = jax.random.split(jax.random.key(seed), 7)
    points = noise(seeds[0], (SNAPS, POINTS, C), 1.0, 6.0, ((0, 8), (1, 16)))
    ball_lists = draw_ball_lists(jax.random.fold_in(seeds[6], 71), 0)
    gains = jnp.clip(1.0 + 0.15 * jax.random.normal(seeds[2], (2, C), jnp.float32), 0.25, 1.75)
    w_qkv = noise(seeds[3], (2, C, 3 * C), C ** -0.5, 0.25)
    w_out = noise(seeds[4], (2, C, C), C ** -0.5, 0.25)
    cotangent = noise(seeds[5], (SNAPS, POINTS, C), 1.0, 6.0, ((0, 8), (1, 16)))
    return {"points": points, "ball_lists": ball_lists, "gains": gains, "w_qkv": w_qkv, "w_out": w_out, "cotangent": cotangent}


EPS = 1e-05

def norm_rows(x, gain):
    values = x.astype(jnp.float32)
    scale = lax.rsqrt(lax.optimization_barrier(jnp.mean(values * values, axis=-1, keepdims=True)) + EPS)
    return values * scale * gain

def ball_attend(qkv):
    rows = qkv.shape[0]
    width = qkv.shape[1] // 3
    size = width // HEADS
    parts = qkv.reshape(rows // BALL, BALL, 3, HEADS, size)
    query, keys, values = (parts[:, :, 0], parts[:, :, 1], parts[:, :, 2])
    scores = jnp.einsum('bqhd,bkhd->bhqk', query, keys, preferred_element_type=jnp.float32) * size ** (-0.5)
    weights = jax.nn.softmax(scores, axis=-1).astype(jnp.bfloat16)
    out = jnp.einsum('bhqk,bkhd->bqhd', weights, values, preferred_element_type=jnp.float32)
    return out.reshape(rows, width).astype(jnp.bfloat16)

def layer_forward(x, gain, w_qkv, w_out):
    normed, norm_back = jax.vjp(norm_rows, x, gain)
    hidden = normed.astype(jnp.bfloat16)
    qkv = jnp.dot(hidden, w_qkv, preferred_element_type=jnp.float32).astype(jnp.bfloat16)
    att, attend_back = jax.vjp(ball_attend, qkv)
    y = (x.astype(jnp.float32) + jnp.dot(att, w_out, preferred_element_type=jnp.float32)).astype(jnp.bfloat16)
    return (y, (hidden, att, norm_back, attend_back))

def layer_backward(saved, w_qkv, w_out, d_y):
    hidden, att, norm_back, attend_back = saved
    g_out = jnp.einsum('rc,rd->cd', att, d_y, preferred_element_type=jnp.float32)
    d_att = jnp.einsum('rd,cd->rc', d_y, w_out, preferred_element_type=jnp.float32).astype(jnp.bfloat16)
    d_qkv, = attend_back(d_att)
    g_qkv = jnp.einsum('rc,rd->cd', hidden, d_qkv, preferred_element_type=jnp.float32)
    d_h = jnp.einsum('rd,cd->rc', d_qkv, w_qkv, preferred_element_type=jnp.float32)
    d_n, g_gain = norm_back(d_h)
    d_x = (d_y.astype(jnp.float32) + d_n.astype(jnp.float32)).astype(jnp.bfloat16)
    return (d_x, (g_gain, g_qkv, g_out))

def rotation(lists):
    groups = POINTS // P_DEV
    sources = lists.reshape(groups, groups, BLK) + (jnp.arange(groups, dtype=jnp.int32) * P_DEV)[:, None, None]
    return jnp.transpose(sources, (1, 0, 2)).reshape(-1).astype(jnp.int32)

def reference(points, ball_lists, gains, w_qkv, w_out, cotangent):

    def one_snapshot(items):
        start, lists, d_mixed = items
        src = rotation(lists)
        inner, saved_tree = layer_forward(start, gains[0], w_qkv[0], w_out[0])
        outer, saved_rot = layer_forward(inner[src], gains[1], w_qkv[1], w_out[1])
        mixed = jnp.zeros_like(outer).at[src].set(outer)
        d_rot, upper = layer_backward(saved_rot, w_qkv[1], w_out[1], d_mixed[src])
        d_inner = jnp.zeros_like(d_rot).at[src].set(d_rot)
        d_start, lower = layer_backward(saved_tree, w_qkv[0], w_out[0], d_inner)
        stacked = tuple((jnp.stack([lower[i], upper[i]]) for i in range(3)))
        return (mixed, d_start, stacked)
    mixed, grad_points, stacked = lax.map(one_snapshot, (points, ball_lists, cotangent))
    return (mixed, grad_points, lax.optimization_barrier(jnp.sum(stacked[0], axis=0)), lax.optimization_barrier(jnp.sum(stacked[1], axis=0)), lax.optimization_barrier(jnp.sum(stacked[2], axis=0)))
```

```python
import jax
import jax.numpy as jnp
from jax import lax
from jax.experimental import pallas as pl
from jax.experimental.pallas import tpu as pltpu
from jax.sharding import PartitionSpec as P

HEADS = 8
BALL = 256
EPS = 1e-05
F32 = jnp.float32
BF16 = jnp.bfloat16
VMEM_BYTES = 60 * 1024 * 1024


def dot(a, b, ca, cb):
    return lax.dot_general(a, b, (((ca,), (cb,)), ((), ())), preferred_element_type=F32)


def nn(a, b):
    return dot(a, b, 1, 0)


def nt(a, b):
    return dot(a, b, 1, 1)


def tn(a, b):
    return dot(a, b, 0, 0)


def cols(ball):
    return pl.ds(pl.multiple_of(ball * BALL, BALL), BALL)


def norm_scale(x):
    return lax.rsqrt(jnp.mean(x * x, axis=1, keepdims=True) + EPS)


def one_hot_to_rotated(order_row, first):
    rows = order_row.shape[1]
    lane = 128
    held = jnp.broadcast_to(order_row[:, pl.ds(pl.multiple_of(first, lane), lane)], (lane, lane)).T
    row = lax.broadcasted_iota(jnp.int32, (lane, lane), 1)
    parts = [jnp.where(held == row + low, 1.0, 0.0).astype(BF16) for low in range(0, rows, lane)]
    return jnp.concatenate(parts, axis=1)


def one_hot_to_tree(order_row, first, rows):
    tree = lax.broadcasted_iota(jnp.int32, (rows, order_row.shape[1]), 0) + first
    return jnp.where(order_row[...] == tree, 1.0, 0.0).astype(BF16)


def transpose_by_unit(wqkv, wqkv_t):
    unit = jnp.where(
        lax.broadcasted_iota(jnp.int32, (BALL, BALL), 0) == lax.broadcasted_iota(jnp.int32, (BALL, BALL), 1), 1.0, 0.0
    ).astype(BF16)
    for low in range(0, wqkv.shape[1], BALL):
        wqkv_t[low : low + BALL, :] = nt(unit, wqkv[:, low : low + BALL]).astype(BF16)


def forward_ball(ball, x, gain, wqkv_t, wout, h_t, qkv_t, p_t, att_t, inv):
    width = x.shape[1]
    size = width // HEADS
    here = cols(ball)
    values = x.astype(F32)
    hidden = (values * norm_scale(values) * gain).astype(BF16)
    hidden_t = hidden.T
    h_t[:, here] = hidden_t
    qkv_t[:, here] = nn(wqkv_t[...], hidden_t).astype(BF16)
    for head in range(HEADS):
        low = head * size
        q = qkv_t[low : low + size, here] * size ** (-0.5)
        k = qkv_t[width + low : width + low + size, here]
        v = qkv_t[2 * width + low : 2 * width + low + size, here]
        scores = tn(k, q)
        weights = jnp.exp(scores - jnp.max(scores, axis=0, keepdims=True))
        share = 1.0 / jnp.sum(weights, axis=0, keepdims=True)
        weights = weights.astype(BF16)
        p_t[ball, head] = weights
        inv[ball, head : head + 1, :] = share
        att_t[low : low + size, here] = (nn(v, weights) * share).astype(BF16)
    return values + tn(att_t[:, here], wout[...])


def backward_ball(ball, x, gain, dy, wqkv, wout, qkv_t, p_t, att_t, inv, dqkv_t):
    width = x.shape[1]
    size = width // HEADS
    here = cols(ball)
    d_att = nt(wout[...], dy).astype(BF16)
    for head in range(HEADS):
        low = head * size
        q = qkv_t[low : low + size, here] * size ** (-0.5)
        k = qkv_t[width + low : width + low + size, here]
        v = qkv_t[2 * width + low : 2 * width + low + size, here]
        share = inv[ball, head : head + 1, :]
        d_out = d_att[low : low + size].astype(F32) * share
        delta = jnp.sum(d_out * att_t[low : low + size, here].astype(F32), axis=0, keepdims=True)
        d_out = d_out.astype(BF16)
        weights = p_t[ball, head]
        d_scores = (weights.astype(F32) * (tn(v, d_out) - delta)).astype(BF16)
        dqkv_t[low : low + size, here] = (nn(k, d_scores) * size ** (-0.5)).astype(BF16)
        dqkv_t[width + low : width + low + size, here] = nt(q, d_scores).astype(BF16)
        dqkv_t[2 * width + low : 2 * width + low + size, here] = nt(d_out, weights).astype(BF16)
    d_h = nn(wqkv[...], dqkv_t[:, here]).T
    values = x.astype(F32)
    scale = norm_scale(values)
    unit = values * scale
    d_unit = d_h * gain
    d_n = scale * (d_unit - unit * jnp.mean(d_unit * unit, axis=1, keepdims=True))
    d_x = dy.astype(F32) + d_n.astype(BF16).astype(F32)
    return d_x.astype(BF16), jnp.sum(d_h * unit, axis=0, keepdims=True)


TO_X, TO_COT, BACK_R, BACK_D = range(4)
MESH = pl.DeviceIdType.MESH


def kernel(
    points, lists, gains, w_qkv, w_out, cotangent,
    mixed_out, points_out, gain_out, qkv_out, out_out,
    order, x, cot, gain, wqkv, wout, wqkv_t, place, y,
    h0, qkv0, p0, att0, inv0, h1, qkv1, p1, att1, inv1, dqkv, d_y,
    sent, got, mixed, d_x, g_gain, g_qkv, g_out,
    load_sem, store_sem, send_sem, recv_sem,
):
    groups = lax.axis_size("seq")
    me = lax.axis_index("seq")
    rows = x.shape[0]
    block = rows // groups
    balls = rows // BALL
    near = groups // balls
    home = me // near
    seat = me % near

    loads = []

    def load(source, target):
        copy = pltpu.make_async_copy(source, target, load_sem.at[len(loads)])
        copy.start()
        loads.append(copy)
        return copy

    lists_in = load(lists, order)
    cot_in = load(cotangent.at[0], cot)
    x_in = load(points.at[0], x)
    small_in = [load(gains, gain), load(w_qkv.at[0], wqkv.at[0]), load(w_out.at[0], wout.at[0])]
    late_in = [load(w_qkv.at[1], wqkv.at[1]), load(w_out.at[1], wout.at[1])]

    barrier = pltpu.get_barrier_semaphore()
    for step in range(1, groups):
        pl.semaphore_signal(barrier, inc=1, device_id={"seq": (me + step) % groups}, device_id_type=MESH)

    def span(index):
        return pl.ds(pl.multiple_of(index * block, block), block)

    def transfer(kind, source, peer):
        return pltpu.make_async_remote_copy(
            src_ref=sent.at[kind, span(peer), :],
            dst_ref=got.at[kind, span(source), :],
            send_sem=send_sem.at[kind, peer],
            recv_sem=recv_sem.at[kind, source],
            device_id={"seq": peer},
            device_id_type=MESH,
        )

    def send_home(kind):
        got[kind, span(me), :] = sent[kind, span(me), :]
        for step in range(1, near):
            transfer(kind, me, home * near + (seat + step) % near).start()

    def send_away(kind, group):
        for step in range(near):
            transfer(kind, me, group * near + (seat + step) % near).start()

    def arrive_home(kind):
        for step in range(1, near):
            transfer(kind, home * near + (seat + step) % near, me).wait_recv()

    def arrive_away(kind, group):
        for step in range(near):
            transfer(kind, group * near + step, me).wait_recv()

    def gather(kind, source, group):
        sent[kind, cols(group), :] = nn(place[cols(group), :], source[...]).astype(BF16)

    lists_in.wait()

    @pl.loop(0, rows // 128)
    def _(part):
        first = pl.multiple_of(part * 128, 128)
        place[pl.ds(first, 128), :] = one_hot_to_rotated(order, first)

    cot_in.wait()
    pl.semaphore_wait(barrier, groups - 1)
    gather(TO_COT, cot, home)
    send_home(TO_COT)

    @pl.loop(1, balls)
    def _(step):
        group = (home + step) % balls
        gather(TO_COT, cot, group)
        send_away(TO_COT, group)

    x_in.wait()
    for copy in small_in:
        copy.wait()
    transpose_by_unit(wqkv.at[0], wqkv_t.at[0])

    @pl.loop(0, balls)
    def _(ball):
        y[cols(ball), :] = forward_ball(
            ball, x[cols(ball), :], gain[0:1], wqkv_t.at[0], wout.at[0], h0, qkv0, p0, att0, inv0
        ).astype(BF16)

    gather(TO_X, y, home)
    send_home(TO_X)

    @pl.loop(1, balls)
    def _(step):
        group = (home + step) % balls
        gather(TO_X, y, group)
        send_away(TO_X, group)

    for copy in late_in:
        copy.wait()
    transpose_by_unit(wqkv.at[1], wqkv_t.at[1])
    g_gain[...] = jnp.zeros_like(g_gain)

    def forward_rotated(ball):
        sent[BACK_R, cols(ball), :] = forward_ball(
            ball, got[TO_X, cols(ball), :], gain[1:2], wqkv_t.at[1], wout.at[1], h1, qkv1, p1, att1, inv1
        ).astype(BF16)

    def backward_rotated(ball):
        sent[BACK_D, cols(ball), :], gained = backward_ball(
            ball, got[TO_X, cols(ball), :], gain[1:2], got[TO_COT, cols(ball), :],
            wqkv.at[1], wout.at[1], qkv1, p1, att1, inv1, dqkv,
        )
        g_gain[1:2] += gained

    arrive_home(TO_X)
    forward_rotated(home)
    send_home(BACK_R)

    @pl.loop(1, balls)
    def _(step):
        ball = (home + step) % balls
        arrive_away(TO_X, ball)
        forward_rotated(ball)
        send_away(BACK_R, ball)
        arrive_away(TO_COT, ball)
        backward_rotated(ball)
        send_away(BACK_D, ball)

    arrive_home(TO_COT)
    backward_rotated(home)
    send_home(BACK_D)

    stores = []

    def store(source, target):
        copy = pltpu.make_async_copy(source, target, store_sem.at[len(stores)])
        copy.start()
        stores.append(copy)
        return copy

    g_out[...] = nn(att1[...], got[TO_COT])
    out_copy = store(g_out, out_out.at[1])
    g_qkv[...] = nt(h1[...], dqkv[...])
    qkv_copy = store(g_qkv, qkv_out.at[1])

    def arrive(kind):
        arrive_home(kind)

        @pl.loop(1, balls)
        def _(step):
            arrive_away(kind, (home + step) % balls)

    arrive(BACK_R)

    @pl.loop(0, balls)
    def _(ball):
        mixed[cols(ball), :] = nn(one_hot_to_tree(order, ball * BALL, BALL), got[BACK_R]).astype(BF16)

    mixed_copy = store(mixed, mixed_out.at[0])
    arrive(BACK_D)

    @pl.loop(0, balls)
    def _(ball):
        d_y[cols(ball), :] = nn(one_hot_to_tree(order, ball * BALL, BALL), got[BACK_D]).astype(BF16)
        d_x[cols(ball), :], gained = backward_ball(
            ball, x[cols(ball), :], gain[0:1], d_y[cols(ball), :],
            wqkv.at[0], wout.at[0], qkv0, p0, att0, inv0, dqkv,
        )
        g_gain[0:1] += gained

    store(d_x, points_out.at[0])
    store(g_gain, gain_out)
    out_copy.wait()
    g_out[...] = nn(att0[...], d_y[...])
    store(g_out, out_out.at[0])
    qkv_copy.wait()
    g_qkv[...] = nt(h0[...], dqkv[...])
    store(g_qkv, qkv_out.at[0])
    for copy in stores:
        if copy is not out_copy and copy is not qkv_copy:
            copy.wait()

    @pl.loop(1, groups)
    def _(step):
        peer = (me + step) % groups
        for kind in range(4):
            transfer(kind, me, peer).wait_send()


def local(points, ball_lists, gains, w_qkv, w_out, cotangent):
    groups = lax.axis_size("seq")
    rows, width = points.shape[1:]
    balls = rows // BALL
    any_place = pl.BlockSpec(memory_space=pl.ANY)
    saved = [
        pltpu.VMEM((width, rows), BF16),
        pltpu.VMEM((3 * width, rows), BF16),
        pltpu.VMEM((balls, HEADS, BALL, BALL), BF16),
        pltpu.VMEM((width, rows), BF16),
        pltpu.VMEM((balls, HEADS, BALL), F32),
    ]
    token = pltpu.VMEM((rows, width), BF16)
    mixed, d_x, *grads = pl.pallas_call(
        kernel,
        out_shape=[
            jax.ShapeDtypeStruct(points.shape, BF16),
            jax.ShapeDtypeStruct(points.shape, BF16),
            jax.ShapeDtypeStruct(gains.shape, F32),
            jax.ShapeDtypeStruct(w_qkv.shape, F32),
            jax.ShapeDtypeStruct(w_out.shape, F32),
        ],
        in_specs=[any_place] * 6,
        out_specs=[any_place] * 5,
        scratch_shapes=[
            pltpu.VMEM((1, rows), jnp.int32),
            token,
            token,
            pltpu.VMEM(gains.shape, F32),
            pltpu.VMEM(w_qkv.shape, BF16),
            pltpu.VMEM(w_out.shape, BF16),
            pltpu.VMEM((2, 3 * width, width), BF16),
            pltpu.VMEM((rows, rows), BF16),
            token,
            *saved,
            *saved,
            pltpu.VMEM((3 * width, rows), BF16),
            token,
            pltpu.VMEM((4, rows, width), BF16),
            pltpu.VMEM((4, rows, width), BF16),
            token,
            token,
            pltpu.VMEM(gains.shape, F32),
            pltpu.VMEM((width, 3 * width), F32),
            pltpu.VMEM((width, width), F32),
            pltpu.SemaphoreType.DMA((8,)),
            pltpu.SemaphoreType.DMA((8,)),
            pltpu.SemaphoreType.DMA((4, groups)),
            pltpu.SemaphoreType.DMA((4, groups)),
        ],
        compiler_params=pltpu.CompilerParams(
            vmem_limit_bytes=VMEM_BYTES, collective_id=0, has_side_effects=True
        ),
    )(points, ball_lists, gains, w_qkv, w_out, cotangent)
    totals = lax.psum(tuple(grads), ("dp", "seq"))
    return (mixed, d_x, *totals)


def solution(mesh):
    return jax.shard_map(
        local,
        mesh=mesh,
        in_specs=(P("dp", "seq", None), P("dp", "seq"), P(), P(), P(), P("dp", "seq", None)),
        out_specs=(P("dp", "seq", None), P("dp", "seq", None), P(), P(), P()),
        check_vma=False,
    )
```

```python
import jax
import jax.numpy as jnp
from jax import lax
from jax.experimental import pallas as pl
from jax.experimental.pallas import tpu as pltpu
from jax.sharding import PartitionSpec as P

MESH = pl.DeviceIdType.MESH
HEADS = 8
BALL = 256
EPS = 1e-05
F32 = jnp.float32
BF16 = jnp.bfloat16
VMEM_BYTES = 62 * 1024 * 1024


def dot(a, b, ca, cb):
    return lax.dot_general(a, b, (((ca,), (cb,)), ((), ())), preferred_element_type=F32)


def nn(a, b):
    return dot(a, b, 1, 0)


def nt(a, b):
    return dot(a, b, 1, 1)


def tn(a, b):
    return dot(a, b, 0, 0)


def cols(ball):
    return pl.ds(pl.multiple_of(ball * BALL, BALL), BALL)


def norm_scale(x):
    return lax.rsqrt(jnp.mean(x * x, axis=1, keepdims=True) + EPS)


def one_hot_to_rotated(order_row, first):
    rows = order_row.shape[1]
    lane = 128
    held = jnp.broadcast_to(order_row[:, pl.ds(pl.multiple_of(first, lane), lane)], (lane, lane)).T
    row = lax.broadcasted_iota(jnp.int32, (lane, lane), 1)
    parts = [jnp.where(held == row + low, 1.0, 0.0).astype(BF16) for low in range(0, rows, lane)]
    return jnp.concatenate(parts, axis=1)


def one_hot_to_tree(order_row, first, rows):
    tree = lax.broadcasted_iota(jnp.int32, (rows, order_row.shape[1]), 0) + first
    return jnp.where(order_row[...] == tree, 1.0, 0.0).astype(BF16)


def transpose_by_unit(wqkv, wqkv_t):
    unit = jnp.where(
        lax.broadcasted_iota(jnp.int32, (BALL, BALL), 0) == lax.broadcasted_iota(jnp.int32, (BALL, BALL), 1), 1.0, 0.0
    ).astype(BF16)
    for low in range(0, wqkv.shape[1], BALL):
        wqkv_t[low : low + BALL, :] = nt(unit, wqkv[:, low : low + BALL]).astype(BF16)


def forward_ball(ball, keep, x, gain, wqkv_t, wout, h_t, qkv_t, p_t, att_t, inv):
    width = x.shape[1]
    size = width // HEADS
    here = cols(ball)
    values = x.astype(F32)
    hidden = (values * norm_scale(values) * gain).astype(BF16)
    hidden_t = hidden.T
    h_t[:, here] = hidden_t
    qkv_t[:, here] = nn(wqkv_t[...], hidden_t).astype(BF16)
    for head in range(HEADS):
        low = head * size
        q = qkv_t[low : low + size, here] * size ** (-0.5)
        k = qkv_t[width + low : width + low + size, here]
        v = qkv_t[2 * width + low : 2 * width + low + size, here]
        scores = tn(k, q)
        weights = jnp.exp(scores - jnp.max(scores, axis=0, keepdims=True))
        share = 1.0 / jnp.sum(weights, axis=0, keepdims=True)
        weights = weights.astype(BF16)
        p_t[keep, head] = weights
        inv[keep, head : head + 1, :] = share
        att_t[low : low + size, here] = (nn(v, weights) * share).astype(BF16)
    return values + tn(att_t[:, here], wout[...])


def backward_heads(ball, keep, heads, d_att, qkv_t, p_t, att_t, inv, dqkv_t):
    width = d_att.shape[0]
    size = width // HEADS
    here = cols(ball)
    for head in heads:
        low = head * size
        q = qkv_t[low : low + size, here] * size ** (-0.5)
        k = qkv_t[width + low : width + low + size, here]
        v = qkv_t[2 * width + low : 2 * width + low + size, here]
        share = inv[keep, head : head + 1, :]
        d_out = d_att[low : low + size, here].astype(F32) * share
        delta = jnp.sum(d_out * att_t[low : low + size, here].astype(F32), axis=0, keepdims=True)
        d_out = d_out.astype(BF16)
        weights = p_t[keep, head]
        d_scores = (weights.astype(F32) * (tn(v, d_out) - delta)).astype(BF16)
        dqkv_t[low : low + size, here] = (nn(k, d_scores) * size ** (-0.5)).astype(BF16)
        dqkv_t[width + low : width + low + size, here] = nt(q, d_scores).astype(BF16)
        dqkv_t[2 * width + low : 2 * width + low + size, here] = nt(d_out, weights).astype(BF16)


def backward_norm(ball, x, gain, dy, wqkv, dqkv_t):
    d_h = nn(wqkv[...], dqkv_t[:, cols(ball)]).T
    values = x.astype(F32)
    scale = norm_scale(values)
    unit = values * scale
    d_unit = d_h * gain
    d_n = scale * (d_unit - unit * jnp.mean(d_unit * unit, axis=1, keepdims=True))
    d_x = dy.astype(F32) + d_n.astype(BF16).astype(F32)
    return d_x.astype(BF16), jnp.sum(d_h * unit, axis=0, keepdims=True)


class Place:
    def __init__(self):
        dp, seq = lax.axis_index("dp"), lax.axis_index("seq")
        self.at = {"x": seq // 4, "y": dp // 4 * 2 + seq // 2 % 2, "z": dp % 4, "core": seq % 2}
        sizes = {"x": 4, "y": 4, "z": 4, "core": 2}
        self.peers = {
            axis: [(self.at[axis] + step) % size for step in range(1, size)] for axis, size in sizes.items()
        }

    def other(self, axis, value):
        at = {**self.at, axis: value}
        return {"dp": at["y"] // 2 * 4 + at["z"], "seq": at["x"] * 4 + at["y"] % 2 * 2 + at["core"]}


SCATTER = (0, 2, 6)
LAST = 10
GATHER = (22, 18, 14)
SUM_SEMS = 24


class Sum:
    def __init__(self, place, slot, axes, part, total, halves, quarters, pieces, lasts, send_sem, recv_sem):
        self.place, self.slot, self.axes = place, slot, axes
        self.part, self.total = part, total
        self.inboxes, self.lasts = [halves, quarters, pieces], lasts
        self.send_sem, self.recv_sem = send_sem, recv_sem
        rows = part.shape[0]
        self.sizes = [rows, rows // 2, rows // 8, rows // 32]
        self.names = ["core", axes[0], axes[1]]
        base, self.bases = 0, [0]
        for size, name in zip(self.sizes[1:], self.names):
            base = base + place.at[name] * size
            self.bases.append(base)
        self.done = 0

    def span(self, level, coordinate=None):
        base = self.bases[level] if coordinate is None else self.bases[level - 1] + coordinate * self.sizes[level]
        return pl.ds(pl.multiple_of(base, 16), self.sizes[level])

    def hop(self, first, axis, source, target, here, there):
        return pltpu.make_async_remote_copy(
            src_ref=source,
            dst_ref=target,
            send_sem=self.send_sem.at[self.slot, first + there],
            recv_sem=self.recv_sem.at[self.slot, first + here],
            device_id=self.place.other(axis, there),
            device_id_type=MESH,
        )

    def scatter(self, level, here, there):
        axis = self.names[level - 1]
        inbox = self.inboxes[level - 1].at[0 if level == 1 else here]
        return self.hop(SCATTER[level - 1], axis, self.part.at[self.span(level, there), :], inbox, here, there)

    def exchange(self, here, there):
        return self.hop(LAST, self.axes[2], self.lasts.at[here], self.lasts.at[here], here, there)

    def gather(self, level, here, there):
        rows = self.total.at[self.span(level, here), :]
        return self.hop(GATHER[level - 1], self.names[level - 1], rows, rows, here, there)

    def start(self, kind, axis, *level):
        for peer in self.place.peers[axis]:
            kind(*level, self.place.at[axis], peer).start()

    def arrive(self, kind, axis, *level):
        for peer in self.place.peers[axis]:
            kind(*level, peer, self.place.at[axis]).wait_recv()

    def left(self, kind, axis, *level):
        for peer in self.place.peers[axis]:
            kind(*level, self.place.at[axis], peer).wait_send()

    def added(self, level):
        axis = self.names[level - 1]
        self.arrive(self.scatter, axis, level)
        value = self.part[self.span(level), :].astype(F32)
        for peer in self.place.peers[axis]:
            value += self.inboxes[level - 1][0 if level == 1 else peer].astype(F32)
        return value.astype(BF16)

    def step(self):
        step, self.done = self.done, self.done + 1
        last = self.axes[2]
        if step == 0:
            self.start(self.scatter, self.names[0], 1)
        elif step in (1, 2):
            self.part[self.span(step), :] = self.added(step)
            self.start(self.scatter, self.names[step], step + 1)
        elif step == 3:
            self.lasts[self.place.at[last]] = self.added(3)
            self.start(self.exchange, last)
        elif step == 4:
            self.arrive(self.exchange, last)
            value = self.lasts[0].astype(F32)
            for peer in range(1, 4):
                value += self.lasts[peer].astype(F32)
            self.total[self.span(3), :] = value.astype(BF16)
            self.start(self.gather, self.names[2], 3)
        elif step in (5, 6):
            self.arrive(self.gather, self.names[7 - step], 8 - step)
            self.start(self.gather, self.names[6 - step], 7 - step)
        elif step == 7:
            self.arrive(self.gather, self.names[0], 1)

    def clear(self):
        for level in (1, 2, 3):
            self.left(self.scatter, self.names[level - 1], level)
            self.left(self.gather, self.names[level - 1], level)
        self.left(self.exchange, self.axes[2])


class SmallSum:
    axes = ("core", "x", "y", "z")

    def __init__(self, place, boxes, send_sem, recv_sem):
        self.place, self.boxes, self.send_sem, self.recv_sem = place, boxes, send_sem, recv_sem
        self.done = 0

    def hop(self, step, here, there):
        box = self.boxes.at[step, here]
        return pltpu.make_async_remote_copy(
            src_ref=box,
            dst_ref=box,
            send_sem=self.send_sem.at[step, there],
            recv_sem=self.recv_sem.at[step, here],
            device_id=self.place.other(self.axes[step], there),
            device_id_type=MESH,
        )

    def send(self, value):
        axis = self.axes[self.done]
        mine = self.place.at[axis]
        self.boxes[self.done, mine] = value
        for peer in self.place.peers[axis]:
            self.hop(self.done, mine, peer).start()

    def receive(self):
        axis = self.axes[self.done]
        for peer in self.place.peers[axis]:
            self.hop(self.done, peer, self.place.at[axis]).wait_recv()
        value = self.boxes[self.done, 0]
        for peer in range(1, len(self.place.peers[axis]) + 1):
            value += self.boxes[self.done, peer]
        self.done += 1
        return value

    def clear(self):
        for step, axis in enumerate(self.axes):
            for peer in self.place.peers[axis]:
                self.hop(step, self.place.at[axis], peer).wait_send()


TO_X, TO_COT, BACK_R, BACK_D = range(4)
GROUPS = 2
SUMS = (
    (1024, ("x", "z", "y")),
    (1024, ("z", "x", "y")),
    (512, ("z", "x", "y")),
    (768, ("x", "z", "y")),
    (256, ("x", "z", "y")),
    (256, ("z", "y", "x")),
    (256, ("y", "x", "z")),
)


def kernel(
    points, lists, gains, w_qkv, w_out, cotangent,
    mixed_out, points_out, gain_out, qkv_out, out_out,
    order, x, cot, gain, wqkv, wout, wqkv_t, onto, y,
    h0, qkv0, p0, att0, inv0, h1, qkv1, p1, att1, inv1, dqkv, d_att,
    sent, got, d_x, g_gain, *rest,
):
    sum_boxes, rest = rest[: 6 * len(SUMS)], rest[6 * len(SUMS) :]
    boxes, load_sem, store_sem, send_sem, recv_sem, sum_send, sum_recv, small_send, small_recv = rest
    groups = lax.axis_size("seq")
    me = lax.axis_index("seq")
    rows = x.shape[0]
    block = rows // groups
    balls = rows // BALL
    near = groups // balls
    home = me // near
    seat = me % near
    place = Place()
    sums = [
        Sum(place, slot, axes, *sum_boxes[6 * slot : 6 * slot + 6], sum_send, sum_recv)
        for slot, (columns, axes) in enumerate(SUMS)
    ]
    upper, sum_o, sum_q, last = sums[0:2], sums[2], sums[3], sums[4:7]
    small = SmallSum(place, boxes, small_send, small_recv)

    loads = []

    def load(source, target):
        copy = pltpu.make_async_copy(source, target, load_sem.at[len(loads)])
        copy.start()
        loads.append(copy)
        return copy

    lists_in = load(lists, order)
    cot_in = load(cotangent.at[0], cot)
    x_in = load(points.at[0], x)
    small_in = [load(gains, gain), load(w_qkv.at[0], wqkv.at[0]), load(w_out.at[0], wout.at[0])]
    late_in = [load(w_qkv.at[1], wqkv.at[1]), load(w_out.at[1], wout.at[1])]

    barrier = pltpu.get_barrier_semaphore()
    for step in range(1, near):
        pl.semaphore_signal(
            barrier, inc=1, device_id={"seq": home * near + (seat + step) % near}, device_id_type=MESH
        )
    for axis in ("x", "z"):
        for peer in place.peers[axis]:
            pl.semaphore_signal(barrier, inc=1, device_id=place.other(axis, peer), device_id_type=MESH)
    for step in range(2):
        far = (place.at["y"] // 2 * 2 + 2 + step) % 4
        pl.semaphore_signal(barrier, inc=1, device_id=place.other("y", far), device_id_type=MESH)

    def span(index):
        return pl.ds(pl.multiple_of(index * block, block), block)

    others = [(seat + step) % near for step in range(1, near)]

    def transfer(kind, ball, here, there):
        return pltpu.make_async_remote_copy(
            src_ref=sent.at[kind, span(ball * near + there), :],
            dst_ref=got.at[kind, span(ball * near + here), :],
            send_sem=send_sem.at[kind, ball * near + there],
            recv_sem=recv_sem.at[kind, ball * near + here],
            device_id={"seq": home * near + there},
            device_id_type=MESH,
        )

    def send(kind, ball):
        for peer in others:
            transfer(kind, ball, seat, peer).start()
        own = span(ball * near + seat)
        got[kind, own, :] = sent[kind, own, :]

    def arrive(kind, ball):
        for peer in others:
            transfer(kind, ball, peer, seat).wait_recv()

    def gather(kind, source, group):
        sent[kind, cols(group), :] = nn(onto[cols(group), :], source[...]).astype(BF16)

    lists_in.wait()

    @pl.loop(0, rows // 128)
    def _(part):
        first = pl.multiple_of(part * 128, 128)
        onto[pl.ds(first, 128), :] = one_hot_to_rotated(order, first)

    cot_in.wait()
    pl.semaphore_wait(barrier, near - 1 + 8)

    @pl.loop(0, balls)
    def _(ball):
        gather(TO_COT, cot, ball)
        send(TO_COT, ball)

    x_in.wait()
    for copy in small_in:
        copy.wait()
    transpose_by_unit(wqkv.at[0], wqkv_t.at[0])

    @pl.loop(0, balls)
    def _(ball):
        y[cols(ball), :] = forward_ball(
            ball, ball, x[cols(ball), :], gain[0:1], wqkv_t.at[0], wout.at[0], h0, qkv0, p0, att0, inv0
        ).astype(BF16)

    @pl.loop(0, balls)
    def _(ball):
        gather(TO_X, y, ball)
        send(TO_X, ball)

    for copy in late_in:
        copy.wait()
    transpose_by_unit(wqkv.at[1], wqkv_t.at[1])
    g_gain[...] = jnp.zeros_like(g_gain)

    @pl.loop(0, balls)
    def _(ball):
        arrive(TO_X, ball)
        rows_x = got[TO_X, cols(ball), :]
        sent[BACK_R, cols(ball), :] = forward_ball(
            ball, 0, rows_x, gain[1:2], wqkv_t.at[1], wout.at[1], h1, qkv1, p1, att1, inv1
        ).astype(BF16)
        send(BACK_R, ball)
        arrive(TO_COT, ball)
        d_r = got[TO_COT, cols(ball), :]
        d_att[:, cols(ball)] = nt(wout[1], d_r).astype(BF16)
        backward_heads(ball, 0, range(HEADS), d_att, qkv1, p1, att1, inv1, dqkv)
        sent[BACK_D, cols(ball), :], gained = backward_norm(
            ball, got[TO_X, cols(ball), :], gain[1:2], d_r, wqkv.at[1], dqkv
        )
        send(BACK_D, ball)
        g_gain[1:2] += gained

    stores = []

    def store(source, target):
        copy = pltpu.make_async_copy(source, target, store_sem.at[len(stores)])
        copy.start()
        stores.append(copy)
        return copy

    width = x.shape[1]
    first, second = upper[0].part, upper[1].part
    second[:, width:] = nn(att1[...], got[TO_COT]).astype(BF16)
    first[...] = nt(h1[...], dqkv[: 2 * width, :]).astype(BF16)
    second[:, :width] = nt(h1[...], dqkv[2 * width :, :]).astype(BF16)

    def advance(*which):
        for each in which:
            each.step()

    advance(*upper)

    @pl.loop(0, balls)
    def _(ball):
        arrive(BACK_R, ball)

    @pl.loop(0, balls)
    def _(ball):
        cot[cols(ball), :] = nn(one_hot_to_tree(order, ball * BALL, BALL), got[BACK_R]).astype(BF16)

    store(cot, mixed_out.at[0])
    advance(*upper)

    @pl.loop(0, balls)
    def _(ball):
        arrive(BACK_D, ball)

    @pl.loop(0, balls)
    def _(ball):
        y[cols(ball), :] = nn(one_hot_to_tree(order, ball * BALL, BALL), got[BACK_D]).astype(BF16)
        d_att[:, cols(ball)] = nt(wout[0], y[cols(ball), :]).astype(BF16)

    sum_o.part[...] = nn(att0[...], y[...]).astype(BF16)
    advance(sum_o)
    span_q = width // GROUPS
    heads = HEADS // GROUPS
    for group in range(GROUPS):

        @pl.loop(0, balls)
        def _(ball):
            backward_heads(
                ball, ball, range(group * heads, (group + 1) * heads), d_att, qkv0, p0, att0, inv0, dqkv
            )

            @pl.when(ball == 1)
            def _():
                if group == 0:
                    advance(*upper)
                else:
                    advance(*upper, sum_o)

        for kind in range(3):
            low = kind * width + group * span_q
            g = nt(h0[...], dqkv[low : low + span_q, :]).astype(BF16)
            if group == 0:
                sum_q.part[:, kind * span_q : (kind + 1) * span_q] = g
            else:
                last[kind].part[...] = g
                advance(last[kind])
        if group == 0:
            advance(sum_q, sum_o)

    advance(*upper, sum_q)

    @pl.loop(0, balls)
    def _(ball):
        d_x[cols(ball), :], gained = backward_norm(
            ball, x[cols(ball), :], gain[0:1], y[cols(ball), :], wqkv.at[0], dqkv
        )
        g_gain[0:1] += gained

        @pl.when(ball == 1)
        def _():
            advance(sum_o, sum_q, *last)

    store(d_x, points_out.at[0])
    small.send(g_gain[...])
    for step in range(8):
        advance(*sums)
        if small.done < 3:
            small.send(small.receive())
    g_gain[...] = small.receive()
    store(g_gain.at[0:2], gain_out)
    store(upper[0].total, qkv_out.at[1, :, : 2 * width])
    store(upper[1].total.at[:, :width], qkv_out.at[1, :, 2 * width :])
    store(upper[1].total.at[:, width:], out_out.at[1])
    store(sum_o.total, out_out.at[0])
    for kind in range(3):
        low = kind * width
        store(sum_q.total.at[:, kind * span_q : (kind + 1) * span_q], qkv_out.at[0, :, low : low + span_q])
        store(last[kind].total, qkv_out.at[0, :, low + span_q : low + width])
    for copy in stores:
        copy.wait()
    for each in sums:
        each.clear()
    small.clear()

    @pl.loop(0, balls)
    def _(ball):
        for kind in range(4):
            for peer in others:
                transfer(kind, ball, seat, peer).wait_send()


def finish_kernel(mixed, d_x, gain, qkv, out, mixed_out, points_out, gain_out, qkv_out, out_out, *rest):
    mixed_v, d_x_v, gain_v, qkv_v, out_v, qkv_f, out_f, load_sem, store_sem = rest
    rows = BALL
    moves = [(mixed, mixed_v, mixed_v, mixed_out), (d_x, d_x_v, d_x_v, points_out), (gain, gain_v, gain_v, gain_out)]
    for layer in range(qkv.shape[0]):
        for low in range(0, qkv.shape[1], rows):
            at = (layer, pl.ds(low, rows))
            moves.append((qkv.at[at], qkv_v.at[at], qkv_f.at[at], qkv_out.at[at]))
            moves.append((out.at[at], out_v.at[at], out_f.at[at], out_out.at[at]))
    moves = moves[3:] + moves[:3]
    loads = [pltpu.make_async_copy(m[0], m[1], load_sem.at[i]) for i, m in enumerate(moves)]
    stores = [pltpu.make_async_copy(m[2], m[3], store_sem.at[i]) for i, m in enumerate(moves)]
    for copy in loads:
        copy.start()
    for load, store, (_, held, ready, _) in zip(loads, stores, moves):
        load.wait()
        if held is not ready:
            ready[...] = held[...].astype(F32)
        store.start()
    for copy in stores:
        copy.wait()


def local(points, ball_lists, gains, w_qkv, w_out, cotangent):
    groups = lax.axis_size("seq")
    rows, width = points.shape[1:]
    balls = rows // BALL
    any_place = pl.BlockSpec(memory_space=pl.ANY)

    def saved(keep):
        return [
            pltpu.VMEM((width, rows), BF16),
            pltpu.VMEM((3 * width, rows), BF16),
            pltpu.VMEM((keep, HEADS, BALL, BALL), BF16),
            pltpu.VMEM((width, rows), BF16),
            pltpu.VMEM((keep, HEADS, BALL), F32),
        ]

    token = pltpu.VMEM((rows, width), BF16)

    def sums(columns):
        shapes = [(width, columns), (width, columns), (1, width // 2, columns)]
        shapes += [(4, width // 8, columns), (4, width // 32, columns), (4, width // 32, columns)]
        return [pltpu.VMEM(shape, BF16) for shape in shapes]

    parts = pl.pallas_call(
        kernel,
        out_shape=[
            jax.ShapeDtypeStruct(points.shape, BF16),
            jax.ShapeDtypeStruct(points.shape, BF16),
            jax.ShapeDtypeStruct(gains.shape, F32),
            jax.ShapeDtypeStruct(w_qkv.shape, BF16),
            jax.ShapeDtypeStruct(w_out.shape, BF16),
        ],
        in_specs=[any_place] * 6,
        out_specs=[any_place] * 5,
        scratch_shapes=[
            pltpu.VMEM((1, rows), jnp.int32),
            token,
            token,
            pltpu.VMEM(gains.shape, F32),
            pltpu.VMEM(w_qkv.shape, BF16),
            pltpu.VMEM(w_out.shape, BF16),
            pltpu.VMEM((2, 3 * width, width), BF16),
            pltpu.VMEM((rows, rows), BF16),
            token,
            *saved(balls),
            *saved(1),
            pltpu.VMEM((3 * width, rows), BF16),
            pltpu.VMEM((width, rows), BF16),
            pltpu.VMEM((4, rows, width), BF16),
            pltpu.VMEM((4, rows, width), BF16),
            token,
            pltpu.VMEM((8, width), F32),
            *[box for columns, _ in SUMS for box in sums(columns)],
            pltpu.VMEM((4, 4, 8, width), F32),
            pltpu.SemaphoreType.DMA((8,)),
            pltpu.SemaphoreType.DMA((16,)),
            pltpu.SemaphoreType.DMA((4, groups)),
            pltpu.SemaphoreType.DMA((4, groups)),
            pltpu.SemaphoreType.DMA((len(SUMS), SUM_SEMS)),
            pltpu.SemaphoreType.DMA((len(SUMS), SUM_SEMS)),
            pltpu.SemaphoreType.DMA((4, 4)),
            pltpu.SemaphoreType.DMA((4, 4)),
        ],
        compiler_params=pltpu.CompilerParams(
            vmem_limit_bytes=VMEM_BYTES, collective_id=0, has_side_effects=True
        ),
    )(points, ball_lists, gains, w_qkv, w_out, cotangent)
    results = [*parts[:3], *(jax.ShapeDtypeStruct(part.shape, F32) for part in parts[3:])]
    moves = 3 + 4 * width // BALL
    return pl.pallas_call(
        finish_kernel,
        out_shape=[jax.ShapeDtypeStruct(result.shape, result.dtype) for result in results],
        in_specs=[any_place] * 5,
        out_specs=[any_place] * 5,
        scratch_shapes=[
            *[pltpu.VMEM(part.shape, part.dtype) for part in parts],
            *[pltpu.VMEM(part.shape, F32) for part in parts[3:]],
            pltpu.SemaphoreType.DMA((moves,)),
            pltpu.SemaphoreType.DMA((moves,)),
        ],
        compiler_params=pltpu.CompilerParams(vmem_limit_bytes=VMEM_BYTES),
    )(*parts)


def solution(mesh):
    return jax.shard_map(
        local,
        mesh=mesh,
        in_specs=(P("dp", "seq", None), P("dp", "seq"), P(), P(), P(), P("dp", "seq", None)),
        out_specs=(P("dp", "seq", None), P("dp", "seq", None), P(), P(), P()),
        check_vma=False,
    )
```

```python
import jax
import jax.numpy as jnp
from jax import lax
from jax.experimental import pallas as pl
from jax.experimental.pallas import tpu as pltpu
from jax.sharding import PartitionSpec as P

MESH = pl.DeviceIdType.MESH
HEADS = 8
BALL = 256
EPS = 1e-05
F32 = jnp.float32
BF16 = jnp.bfloat16
VMEM_BYTES = 62 * 1024 * 1024


def dot(a, b, ca, cb):
    return lax.dot_general(a, b, (((ca,), (cb,)), ((), ())), preferred_element_type=F32)


def nn(a, b):
    return dot(a, b, 1, 0)


def nt(a, b):
    return dot(a, b, 1, 1)


def tn(a, b):
    return dot(a, b, 0, 0)


def cols(ball):
    return pl.ds(pl.multiple_of(ball * BALL, BALL), BALL)


def norm_scale(x):
    return lax.rsqrt(jnp.mean(x * x, axis=1, keepdims=True) + EPS)


def one_hot_to_rotated(order_row, first):
    rows = order_row.shape[1]
    lane = 128
    held = jnp.broadcast_to(order_row[:, pl.ds(pl.multiple_of(first, lane), lane)], (lane, lane)).T
    row = lax.broadcasted_iota(jnp.int32, (lane, lane), 1)
    parts = [jnp.where(held == row + low, 1.0, 0.0).astype(BF16) for low in range(0, rows, lane)]
    return jnp.concatenate(parts, axis=1)


def one_hot_to_tree(order_row, first, rows):
    tree = lax.broadcasted_iota(jnp.int32, (rows, order_row.shape[1]), 0) + first
    return jnp.where(order_row[...] == tree, 1.0, 0.0).astype(BF16)


def transpose_by_unit(wqkv, wqkv_t):
    unit = jnp.where(
        lax.broadcasted_iota(jnp.int32, (BALL, BALL), 0) == lax.broadcasted_iota(jnp.int32, (BALL, BALL), 1), 1.0, 0.0
    ).astype(BF16)
    for low in range(0, wqkv.shape[1], BALL):
        wqkv_t[low : low + BALL, :] = nt(unit, wqkv[:, low : low + BALL]).astype(BF16)


def forward_ball(ball, keep, x, gain, wqkv_t, wout, h_t, qkv_t, p_t, att_t, inv):
    width = x.shape[1]
    size = width // HEADS
    here = cols(ball)
    values = x.astype(F32)
    hidden = (values * norm_scale(values) * gain).astype(BF16)
    hidden_t = hidden.T
    h_t[:, here] = hidden_t
    qkv_t[:, here] = nn(wqkv_t[...], hidden_t).astype(BF16)

    def score(head):
        low = head * size
        q = qkv_t[low : low + size, here] * size ** (-0.5)
        return tn(qkv_t[width + low : width + low + size, here], q)

    def weigh(head, scores):
        weights = jnp.exp(scores - jnp.max(scores, axis=0, keepdims=True))
        share = 1.0 / jnp.sum(weights, axis=0, keepdims=True)
        weights = weights.astype(BF16)
        p_t[keep, head] = weights
        inv[keep, head : head + 1, :] = share
        return weights, share

    def mix(head, weights, share):
        low = head * size
        v = qkv_t[2 * width + low : 2 * width + low + size, here]
        att_t[low : low + size, here] = (nn(v, weights) * share).astype(BF16)

    staggered(range(HEADS), score, weigh, mix)
    return values + tn(att_t[:, here], wout[...])


def staggered(heads, *stages):
    heads = list(heads)
    held = {}
    for step in range(len(heads) + len(stages) - 1):
        for index, stage in enumerate(stages):
            if 0 <= step - index < len(heads):
                head = heads[step - index]
                given = held.pop((head, index), ())
                result = stage(head, *given)
                held[head, index + 1] = result if isinstance(result, tuple) else (result,)


def backward_heads(ball, keep, heads, d_att, qkv_t, p_t, att_t, inv, dqkv_t):
    width = d_att.shape[0]
    size = width // HEADS
    here = cols(ball)

    def weigh(head):
        low = head * size
        v = qkv_t[2 * width + low : 2 * width + low + size, here]
        d_out = d_att[low : low + size, here].astype(F32) * inv[keep, head : head + 1, :]
        delta = jnp.sum(d_out * att_t[low : low + size, here].astype(F32), axis=0, keepdims=True)
        d_out = d_out.astype(BF16)
        return d_out, delta, tn(v, d_out)

    def score(head, d_out, delta, d_weights):
        weights = p_t[keep, head]
        return d_out, weights, (weights.astype(F32) * (d_weights - delta)).astype(BF16)

    def spread(head, d_out, weights, d_scores):
        low = head * size
        q = qkv_t[low : low + size, here] * size ** (-0.5)
        k = qkv_t[width + low : width + low + size, here]
        dqkv_t[low : low + size, here] = (nn(k, d_scores) * size ** (-0.5)).astype(BF16)
        dqkv_t[width + low : width + low + size, here] = nt(q, d_scores).astype(BF16)
        dqkv_t[2 * width + low : 2 * width + low + size, here] = nt(d_out, weights).astype(BF16)

    staggered(heads, weigh, score, spread)


def backward_norm(ball, x, gain, dy, wqkv, dqkv_t):
    d_h = nn(wqkv[...], dqkv_t[:, cols(ball)]).T
    values = x.astype(F32)
    scale = norm_scale(values)
    unit = values * scale
    d_unit = d_h * gain
    d_n = scale * (d_unit - unit * jnp.mean(d_unit * unit, axis=1, keepdims=True))
    d_x = dy.astype(F32) + d_n.astype(BF16).astype(F32)
    return d_x.astype(BF16), jnp.sum(d_h * unit, axis=0, keepdims=True)


class Place:
    def __init__(self):
        dp, seq = lax.axis_index("dp"), lax.axis_index("seq")
        self.at = {"x": seq // 4, "y": dp // 4 * 2 + seq // 2 % 2, "z": dp % 4, "core": seq % 2}
        sizes = {"x": 4, "y": 4, "z": 4, "core": 2}
        self.peers = {
            axis: [(self.at[axis] + step) % size for step in range(1, size)] for axis, size in sizes.items()
        }

    def other(self, axis, value):
        at = {**self.at, axis: value}
        return {"dp": at["y"] // 2 * 4 + at["z"], "seq": at["x"] * 4 + at["y"] % 2 * 2 + at["core"]}


SCATTER = (0, 2, 6)
LAST = 10
GATHER = (22, 18, 14)
SUM_SEMS = 24


class Sum:
    def __init__(self, place, slot, axes, part, total, halves, quarters, pieces, lasts, send_sem, recv_sem):
        self.place, self.slot, self.axes = place, slot, axes
        self.part, self.total = part, total
        self.inboxes, self.lasts = [halves, quarters, pieces], lasts
        self.send_sem, self.recv_sem = send_sem, recv_sem
        rows = part.shape[0]
        self.sizes = [rows, rows // 2, rows // 8, rows // 32]
        self.names = ["core", axes[0], axes[1]]
        base, self.bases = 0, [0]
        for size, name in zip(self.sizes[1:], self.names):
            base = base + place.at[name] * size
            self.bases.append(base)
        self.done = 0

    def span(self, level, coordinate=None):
        base = self.bases[level] if coordinate is None else self.bases[level - 1] + coordinate * self.sizes[level]
        return pl.ds(pl.multiple_of(base, 16), self.sizes[level])

    def hop(self, first, axis, source, target, here, there):
        return pltpu.make_async_remote_copy(
            src_ref=source,
            dst_ref=target,
            send_sem=self.send_sem.at[self.slot, first + there],
            recv_sem=self.recv_sem.at[self.slot, first + here],
            device_id=self.place.other(axis, there),
            device_id_type=MESH,
        )

    def scatter(self, level, here, there):
        axis = self.names[level - 1]
        inbox = self.inboxes[level - 1].at[0 if level == 1 else here]
        return self.hop(SCATTER[level - 1], axis, self.part.at[self.span(level, there), :], inbox, here, there)

    def exchange(self, here, there):
        return self.hop(LAST, self.axes[2], self.lasts.at[here], self.lasts.at[here], here, there)

    def gather(self, level, here, there):
        rows = self.total.at[self.span(level, here), :]
        return self.hop(GATHER[level - 1], self.names[level - 1], rows, rows, here, there)

    def start(self, kind, axis, *level):
        for peer in self.place.peers[axis]:
            kind(*level, self.place.at[axis], peer).start()

    def arrive(self, kind, axis, *level):
        for peer in self.place.peers[axis]:
            kind(*level, peer, self.place.at[axis]).wait_recv()

    def left(self, kind, axis, *level):
        for peer in self.place.peers[axis]:
            kind(*level, self.place.at[axis], peer).wait_send()

    def added(self, level):
        axis = self.names[level - 1]
        self.arrive(self.scatter, axis, level)
        value = self.part[self.span(level), :].astype(F32)
        for peer in self.place.peers[axis]:
            value += self.inboxes[level - 1][0 if level == 1 else peer].astype(F32)
        return value.astype(BF16)

    def step(self):
        step, self.done = self.done, self.done + 1
        last = self.axes[2]
        if step == 0:
            self.start(self.scatter, self.names[0], 1)
        elif step in (1, 2):
            self.part[self.span(step), :] = self.added(step)
            self.start(self.scatter, self.names[step], step + 1)
        elif step == 3:
            self.lasts[self.place.at[last]] = self.added(3)
            self.start(self.exchange, last)
        elif step == 4:
            self.arrive(self.exchange, last)
            value = self.lasts[0].astype(F32)
            for peer in range(1, 4):
                value += self.lasts[peer].astype(F32)
            self.total[self.span(3), :] = value.astype(BF16)
            self.start(self.gather, self.names[2], 3)
        elif step in (5, 6):
            self.arrive(self.gather, self.names[7 - step], 8 - step)
            self.start(self.gather, self.names[6 - step], 7 - step)
        elif step == 7:
            self.arrive(self.gather, self.names[0], 1)

    def clear(self):
        for level in (1, 2, 3):
            self.left(self.scatter, self.names[level - 1], level)
            self.left(self.gather, self.names[level - 1], level)
        self.left(self.exchange, self.axes[2])


class SmallSum:
    axes = ("core", "x", "y", "z")

    def __init__(self, place, boxes, send_sem, recv_sem):
        self.place, self.boxes, self.send_sem, self.recv_sem = place, boxes, send_sem, recv_sem
        self.done = 0

    def hop(self, step, here, there):
        box = self.boxes.at[step, here]
        return pltpu.make_async_remote_copy(
            src_ref=box,
            dst_ref=box,
            send_sem=self.send_sem.at[step, there],
            recv_sem=self.recv_sem.at[step, here],
            device_id=self.place.other(self.axes[step], there),
            device_id_type=MESH,
        )

    def send(self, value):
        axis = self.axes[self.done]
        mine = self.place.at[axis]
        self.boxes[self.done, mine] = value
        for peer in self.place.peers[axis]:
            self.hop(self.done, mine, peer).start()

    def receive(self):
        axis = self.axes[self.done]
        for peer in self.place.peers[axis]:
            self.hop(self.done, peer, self.place.at[axis]).wait_recv()
        value = self.boxes[self.done, 0]
        for peer in range(1, len(self.place.peers[axis]) + 1):
            value += self.boxes[self.done, peer]
        self.done += 1
        return value

    def clear(self):
        for step, axis in enumerate(self.axes):
            for peer in self.place.peers[axis]:
                self.hop(step, self.place.at[axis], peer).wait_send()


TO_X, TO_COT, BACK_R, BACK_D = range(4)
GROUPS = 2
SUMS = (
    (1024, ("x", "z", "y")),
    (1024, ("z", "x", "y")),
    (512, ("x", "z", "y")),
    (768, ("z", "x", "y")),
    (256, ("x", "y", "z")),
    (256, ("y", "z", "x")),
    (256, ("y", "x", "z")),
)


def kernel(
    points, lists, gains, w_qkv, w_out, cotangent,
    mixed_out, points_out, gain_out, qkv_out, out_out,
    order, x, cot, gain, wqkv, wout, wqkv_t, onto, y,
    h0, qkv0, p0, att0, inv0, h1, qkv1, p1, att1, inv1, dqkv, d_att,
    sent, got, d_x, g_gain, *rest,
):
    sum_boxes, rest = rest[: 6 * len(SUMS)], rest[6 * len(SUMS) :]
    boxes, load_sem, store_sem, send_sem, recv_sem, sum_send, sum_recv, small_send, small_recv = rest
    groups = lax.axis_size("seq")
    me = lax.axis_index("seq")
    rows = x.shape[0]
    block = rows // groups
    balls = rows // BALL
    near = groups // balls
    home = me // near
    seat = me % near
    place = Place()
    sums = [
        Sum(place, slot, axes, *sum_boxes[6 * slot : 6 * slot + 6], sum_send, sum_recv)
        for slot, (columns, axes) in enumerate(SUMS)
    ]
    upper, sum_o, sum_q, last = sums[0:2], sums[2], sums[3], sums[4:7]
    small = SmallSum(place, boxes, small_send, small_recv)

    loads = []

    def load(source, target):
        copy = pltpu.make_async_copy(source, target, load_sem.at[len(loads)])
        copy.start()
        loads.append(copy)
        return copy

    lists_in = load(lists, order)
    cot_in = load(cotangent.at[0], cot)
    x_in = load(points.at[0], x)
    small_in = [load(gains, gain), load(w_qkv.at[0], wqkv.at[0]), load(w_out.at[0], wout.at[0])]
    late_in = [load(w_qkv.at[1], wqkv.at[1]), load(w_out.at[1], wout.at[1])]

    barrier = pltpu.get_barrier_semaphore()
    for step in range(1, near):
        pl.semaphore_signal(
            barrier, inc=1, device_id={"seq": home * near + (seat + step) % near}, device_id_type=MESH
        )
    for axis in ("x", "z"):
        for peer in place.peers[axis]:
            pl.semaphore_signal(barrier, inc=1, device_id=place.other(axis, peer), device_id_type=MESH)
    for step in range(2):
        far = (place.at["y"] // 2 * 2 + 2 + step) % 4
        pl.semaphore_signal(barrier, inc=1, device_id=place.other("y", far), device_id_type=MESH)

    def span(index):
        return pl.ds(pl.multiple_of(index * block, block), block)

    others = [(seat + step) % near for step in range(1, near)]

    def transfer(kind, ball, here, there):
        return pltpu.make_async_remote_copy(
            src_ref=sent.at[kind, span(ball * near + there), :],
            dst_ref=got.at[kind, span(ball * near + here), :],
            send_sem=send_sem.at[kind, ball * near + there],
            recv_sem=recv_sem.at[kind, ball * near + here],
            device_id={"seq": home * near + there},
            device_id_type=MESH,
        )

    def send(kind, ball):
        for peer in others:
            transfer(kind, ball, seat, peer).start()
        own = span(ball * near + seat)
        got[kind, own, :] = sent[kind, own, :]

    def arrive(kind, ball):
        for peer in others:
            transfer(kind, ball, peer, seat).wait_recv()

    def gather(kind, source, group):
        sent[kind, cols(group), :] = nn(onto[cols(group), :], source[...]).astype(BF16)

    lists_in.wait()

    @pl.loop(0, rows // 128)
    def _(part):
        first = pl.multiple_of(part * 128, 128)
        onto[pl.ds(first, 128), :] = one_hot_to_rotated(order, first)

    cot_in.wait()
    pl.semaphore_wait(barrier, near - 1 + 8)

    @pl.loop(0, balls)
    def _(ball):
        gather(TO_COT, cot, ball)
        send(TO_COT, ball)

    x_in.wait()
    for copy in small_in:
        copy.wait()
    transpose_by_unit(wqkv.at[0], wqkv_t.at[0])

    @pl.loop(0, balls)
    def _(ball):
        y[cols(ball), :] = forward_ball(
            ball, ball, x[cols(ball), :], gain[0:1], wqkv_t.at[0], wout.at[0], h0, qkv0, p0, att0, inv0
        ).astype(BF16)

    @pl.loop(0, balls)
    def _(ball):
        gather(TO_X, y, ball)
        send(TO_X, ball)

    for copy in late_in:
        copy.wait()
    transpose_by_unit(wqkv.at[1], wqkv_t.at[1])
    g_gain[...] = jnp.zeros_like(g_gain)

    @pl.loop(0, balls)
    def _(ball):
        arrive(TO_X, ball)
        rows_x = got[TO_X, cols(ball), :]
        sent[BACK_R, cols(ball), :] = forward_ball(
            ball, 0, rows_x, gain[1:2], wqkv_t.at[1], wout.at[1], h1, qkv1, p1, att1, inv1
        ).astype(BF16)
        arrive(TO_COT, ball)
        d_r = got[TO_COT, cols(ball), :]
        d_att[:, cols(ball)] = nt(wout[1], d_r).astype(BF16)
        backward_heads(ball, 0, range(HEADS), d_att, qkv1, p1, att1, inv1, dqkv)
        sent[BACK_D, cols(ball), :], gained = backward_norm(
            ball, got[TO_X, cols(ball), :], gain[1:2], d_r, wqkv.at[1], dqkv
        )
        send(BACK_D, ball)
        g_gain[1:2] += gained

    @pl.loop(0, balls)
    def _(ball):
        send(BACK_R, ball)

    stores = []

    def store(source, target):
        copy = pltpu.make_async_copy(source, target, store_sem.at[len(stores)])
        copy.start()
        stores.append(copy)
        return copy

    width = x.shape[1]
    first, second = upper[0].part, upper[1].part
    second[:, width:] = nn(att1[...], got[TO_COT]).astype(BF16)
    first[...] = nt(h1[...], dqkv[: 2 * width, :]).astype(BF16)
    second[:, :width] = nt(h1[...], dqkv[2 * width :, :]).astype(BF16)

    def advance(*which):
        for each in which:
            each.step()

    advance(*upper)

    @pl.loop(0, balls)
    def _(ball):
        arrive(BACK_D, ball)

    @pl.loop(0, balls)
    def _(ball):
        y[cols(ball), :] = nn(one_hot_to_tree(order, ball * BALL, BALL), got[BACK_D]).astype(BF16)
        d_att[:, cols(ball)] = nt(wout[0], y[cols(ball), :]).astype(BF16)

    advance(*upper)
    sum_o.part[...] = nn(att0[...], y[...]).astype(BF16)
    advance(sum_o)
    span_q = width // GROUPS
    heads = HEADS // GROUPS
    for group in range(GROUPS):

        @pl.loop(0, balls)
        def _(ball):
            backward_heads(
                ball, ball, range(group * heads, (group + 1) * heads), d_att, qkv0, p0, att0, inv0, dqkv
            )

            if group == 1:

                @pl.when(ball == 2)
                def _():
                    advance(*upper)

        for kind in range(3):
            low = kind * width + group * span_q
            g = nt(h0[...], dqkv[low : low + span_q, :]).astype(BF16)
            if group == 0:
                sum_q.part[:, kind * span_q : (kind + 1) * span_q] = g
            else:
                last[kind].part[...] = g
                advance(last[kind])
        if group == 0:
            advance(sum_q, sum_o)

    advance(sum_q, *upper)

    @pl.loop(0, balls)
    def _(ball):
        d_x[cols(ball), :], gained = backward_norm(
            ball, x[cols(ball), :], gain[0:1], y[cols(ball), :], wqkv.at[0], dqkv
        )
        g_gain[0:1] += gained

        @pl.when(ball == 0)
        def _():
            advance(sum_o)

        @pl.when(ball == 1)
        def _():
            advance(*upper, *last)

        @pl.when(ball == 2)
        def _():
            advance(sum_q, sum_o)

    small.send(g_gain[...])
    advance(*upper)
    store(d_x, points_out.at[0])

    @pl.loop(0, balls)
    def _(ball):
        arrive(BACK_R, ball)

    @pl.loop(0, balls)
    def _(ball):
        cot[cols(ball), :] = nn(one_hot_to_tree(order, ball * BALL, BALL), got[BACK_R]).astype(BF16)

    store(cot, mixed_out.at[0])
    for step in range(8):
        advance(*sums)
        if small.done < 3:
            small.send(small.receive())
    g_gain[...] = small.receive()
    store(g_gain.at[0:2], gain_out)
    store(upper[0].total, qkv_out.at[1, :, : 2 * width])
    store(upper[1].total.at[:, :width], qkv_out.at[1, :, 2 * width :])
    store(upper[1].total.at[:, width:], out_out.at[1])
    store(sum_o.total, out_out.at[0])
    for kind in range(3):
        low = kind * width
        store(sum_q.total.at[:, kind * span_q : (kind + 1) * span_q], qkv_out.at[0, :, low : low + span_q])
        store(last[kind].total, qkv_out.at[0, :, low + span_q : low + width])
    for copy in stores:
        copy.wait()
    for each in sums:
        each.clear()
    small.clear()

    @pl.loop(0, balls)
    def _(ball):
        for kind in range(4):
            for peer in others:
                transfer(kind, ball, seat, peer).wait_send()


def finish_kernel(mixed, d_x, gain, qkv, out, mixed_out, points_out, gain_out, qkv_out, out_out, *rest):
    mixed_v, d_x_v, gain_v, qkv_v, out_v, qkv_f, out_f, load_sem, store_sem = rest
    rows = BALL
    moves = [(mixed, mixed_v, mixed_v, mixed_out), (d_x, d_x_v, d_x_v, points_out), (gain, gain_v, gain_v, gain_out)]
    for layer in range(qkv.shape[0]):
        for low in range(0, qkv.shape[1], rows):
            at = (layer, pl.ds(low, rows))
            moves.append((qkv.at[at], qkv_v.at[at], qkv_f.at[at], qkv_out.at[at]))
            moves.append((out.at[at], out_v.at[at], out_f.at[at], out_out.at[at]))
    moves = moves[3:] + moves[:3]
    loads = [pltpu.make_async_copy(m[0], m[1], load_sem.at[i]) for i, m in enumerate(moves)]
    stores = [pltpu.make_async_copy(m[2], m[3], store_sem.at[i]) for i, m in enumerate(moves)]
    for copy in loads:
        copy.start()
    for load, store, (_, held, ready, _) in zip(loads, stores, moves):
        load.wait()
        if held is not ready:
            ready[...] = held[...].astype(F32)
        store.start()
    for copy in stores:
        copy.wait()


def local(points, ball_lists, gains, w_qkv, w_out, cotangent):
    groups = lax.axis_size("seq")
    rows, width = points.shape[1:]
    balls = rows // BALL
    any_place = pl.BlockSpec(memory_space=pl.ANY)

    def saved(keep):
        return [
            pltpu.VMEM((width, rows), BF16),
            pltpu.VMEM((3 * width, rows), BF16),
            pltpu.VMEM((keep, HEADS, BALL, BALL), BF16),
            pltpu.VMEM((width, rows), BF16),
            pltpu.VMEM((keep, HEADS, BALL), F32),
        ]

    token = pltpu.VMEM((rows, width), BF16)

    def sums(columns):
        shapes = [(width, columns), (width, columns), (1, width // 2, columns)]
        shapes += [(4, width // 8, columns), (4, width // 32, columns), (4, width // 32, columns)]
        return [pltpu.VMEM(shape, BF16) for shape in shapes]

    parts = pl.pallas_call(
        kernel,
        out_shape=[
            jax.ShapeDtypeStruct(points.shape, BF16),
            jax.ShapeDtypeStruct(points.shape, BF16),
            jax.ShapeDtypeStruct(gains.shape, F32),
            jax.ShapeDtypeStruct(w_qkv.shape, BF16),
            jax.ShapeDtypeStruct(w_out.shape, BF16),
        ],
        in_specs=[any_place] * 6,
        out_specs=[any_place] * 5,
        scratch_shapes=[
            pltpu.VMEM((1, rows), jnp.int32),
            token,
            token,
            pltpu.VMEM(gains.shape, F32),
            pltpu.VMEM(w_qkv.shape, BF16),
            pltpu.VMEM(w_out.shape, BF16),
            pltpu.VMEM((2, 3 * width, width), BF16),
            pltpu.VMEM((rows, rows), BF16),
            token,
            *saved(balls),
            *saved(1),
            pltpu.VMEM((3 * width, rows), BF16),
            pltpu.VMEM((width, rows), BF16),
            pltpu.VMEM((4, rows, width), BF16),
            pltpu.VMEM((4, rows, width), BF16),
            token,
            pltpu.VMEM((8, width), F32),
            *[box for columns, _ in SUMS for box in sums(columns)],
            pltpu.VMEM((4, 4, 8, width), F32),
            pltpu.SemaphoreType.DMA((8,)),
            pltpu.SemaphoreType.DMA((16,)),
            pltpu.SemaphoreType.DMA((4, groups)),
            pltpu.SemaphoreType.DMA((4, groups)),
            pltpu.SemaphoreType.DMA((len(SUMS), SUM_SEMS)),
            pltpu.SemaphoreType.DMA((len(SUMS), SUM_SEMS)),
            pltpu.SemaphoreType.DMA((4, 4)),
            pltpu.SemaphoreType.DMA((4, 4)),
        ],
        compiler_params=pltpu.CompilerParams(
            vmem_limit_bytes=VMEM_BYTES, collective_id=0, has_side_effects=True
        ),
    )(points, ball_lists, gains, w_qkv, w_out, cotangent)
    results = [*parts[:3], *(jax.ShapeDtypeStruct(part.shape, F32) for part in parts[3:])]
    moves = 3 + 4 * width // BALL
    return pl.pallas_call(
        finish_kernel,
        out_shape=[jax.ShapeDtypeStruct(result.shape, result.dtype) for result in results],
        in_specs=[any_place] * 5,
        out_specs=[any_place] * 5,
        scratch_shapes=[
            *[pltpu.VMEM(part.shape, part.dtype) for part in parts],
            *[pltpu.VMEM(part.shape, F32) for part in parts[3:]],
            pltpu.SemaphoreType.DMA((moves,)),
            pltpu.SemaphoreType.DMA((moves,)),
        ],
        compiler_params=pltpu.CompilerParams(vmem_limit_bytes=VMEM_BYTES),
    )(*parts)


def solution(mesh):
    return jax.shard_map(
        local,
        mesh=mesh,
        in_specs=(P("dp", "seq", None), P("dp", "seq"), P(), P(), P(), P("dp", "seq", None)),
        out_specs=(P("dp", "seq", None), P("dp", "seq", None), P(), P(), P()),
        check_vma=False,
    )
```

```python
import jax
import jax.numpy as jnp
from jax import lax
from jax.experimental import pallas as pl
from jax.experimental.pallas import tpu as pltpu
from jax.sharding import PartitionSpec as P

MESH = pl.DeviceIdType.MESH
HEADS = 8
BALL = 256
EPS = 1e-05
F32 = jnp.float32
BF16 = jnp.bfloat16
VMEM_BYTES = 62 * 1024 * 1024


def dot(a, b, ca, cb):
    return lax.dot_general(a, b, (((ca,), (cb,)), ((), ())), preferred_element_type=F32)


def nn(a, b):
    return dot(a, b, 1, 0)


def nt(a, b):
    return dot(a, b, 1, 1)


def tn(a, b):
    return dot(a, b, 0, 0)


def cols(ball, count=1):
    return pl.ds(pl.multiple_of(ball * BALL, BALL), count * BALL)


def norm_scale(x):
    return lax.rsqrt(jnp.mean(x * x, axis=1, keepdims=True) + EPS)


def one_hot_to_rotated(order_row, first):
    rows = order_row.shape[1]
    lane = 128
    held = jnp.broadcast_to(order_row[:, pl.ds(pl.multiple_of(first, lane), lane)], (lane, lane)).T
    row = lax.broadcasted_iota(jnp.int32, (lane, lane), 1)
    parts = [jnp.where(held == row + low, 1.0, 0.0).astype(BF16) for low in range(0, rows, lane)]
    return jnp.concatenate(parts, axis=1)


def one_hot_to_tree(order_row, first, rows):
    tree = lax.broadcasted_iota(jnp.int32, (rows, order_row.shape[1]), 0) + first
    return jnp.where(order_row[...] == tree, 1.0, 0.0).astype(BF16)


def transpose_by_unit(wqkv, wqkv_t):
    unit = jnp.where(
        lax.broadcasted_iota(jnp.int32, (BALL, BALL), 0) == lax.broadcasted_iota(jnp.int32, (BALL, BALL), 1), 1.0, 0.0
    ).astype(BF16)
    for low in range(0, wqkv.shape[1], BALL):
        wqkv_t[low : low + BALL, :] = nt(unit, wqkv[:, low : low + BALL]).astype(BF16)


def forward_balls(ball, count, keep, x, gain, wqkv_t, wout, h_t, qkv_t, p_t, att_t, inv):
    width = x.shape[1]
    size = width // HEADS
    here = cols(ball, count)
    values = x.astype(F32)
    hidden = (values * norm_scale(values) * gain).astype(BF16)
    hidden_t = hidden.T
    h_t[:, here] = hidden_t
    qkv_t[:, here] = nn(wqkv_t[...], hidden_t).astype(BF16)

    def score(item):
        nth, head = item
        low = head * size
        q = qkv_t[low : low + size, cols(ball + nth)] * size ** (-0.5)
        return tn(qkv_t[width + low : width + low + size, cols(ball + nth)], q)

    def weigh(item, scores):
        nth, head = item
        weights = jnp.exp(scores - jnp.max(scores, axis=0, keepdims=True))
        share = 1.0 / jnp.sum(weights, axis=0, keepdims=True)
        weights = weights.astype(BF16)
        p_t[keep + nth, head] = weights
        inv[keep + nth, head : head + 1, :] = share
        return weights, share

    def mix(item, weights, share):
        nth, head = item
        low = head * size
        v = qkv_t[2 * width + low : 2 * width + low + size, cols(ball + nth)]
        att_t[low : low + size, cols(ball + nth)] = (nn(v, weights) * share).astype(BF16)

    staggered([(nth, head) for nth in range(count) for head in range(HEADS)], score, weigh, mix)
    return values + tn(att_t[:, here], wout[...])


def staggered(heads, *stages):
    heads = list(heads)
    held = {}
    for step in range(len(heads) + len(stages) - 1):
        for index, stage in enumerate(stages):
            if 0 <= step - index < len(heads):
                head = heads[step - index]
                given = held.pop((head, index), ())
                result = stage(head, *given)
                held[head, index + 1] = result if isinstance(result, tuple) else (result,)


def backward_heads(ball, keep, heads, d_att, qkv_t, p_t, att_t, inv, dqkv_t):
    width = d_att.shape[0]
    size = width // HEADS
    here = cols(ball)

    def weigh(head):
        low = head * size
        v = qkv_t[2 * width + low : 2 * width + low + size, here]
        d_out = d_att[low : low + size, here].astype(F32) * inv[keep, head : head + 1, :]
        delta = jnp.sum(d_out * att_t[low : low + size, here].astype(F32), axis=0, keepdims=True)
        d_out = d_out.astype(BF16)
        return d_out, delta, tn(v, d_out)

    def score(head, d_out, delta, d_weights):
        weights = p_t[keep, head]
        return d_out, weights, (weights.astype(F32) * (d_weights - delta)).astype(BF16)

    def spread(head, d_out, weights, d_scores):
        low = head * size
        q = qkv_t[low : low + size, here] * size ** (-0.5)
        k = qkv_t[width + low : width + low + size, here]
        dqkv_t[low : low + size, here] = (nn(k, d_scores) * size ** (-0.5)).astype(BF16)
        dqkv_t[width + low : width + low + size, here] = nt(q, d_scores).astype(BF16)
        dqkv_t[2 * width + low : 2 * width + low + size, here] = nt(d_out, weights).astype(BF16)

    staggered(heads, weigh, score, spread)


def backward_norm(ball, count, x, gain, dy, wqkv, dqkv_t):
    d_h = nn(wqkv[...], dqkv_t[:, cols(ball, count)]).T
    values = x.astype(F32)
    scale = norm_scale(values)
    unit = values * scale
    d_unit = d_h * gain
    d_n = scale * (d_unit - unit * jnp.mean(d_unit * unit, axis=1, keepdims=True))
    d_x = dy.astype(F32) + d_n.astype(BF16).astype(F32)
    return d_x.astype(BF16), jnp.sum(d_h * unit, axis=0, keepdims=True)


class Place:
    def __init__(self):
        dp, seq = lax.axis_index("dp"), lax.axis_index("seq")
        self.at = {"x": seq // 4, "y": dp // 4 * 2 + seq // 2 % 2, "z": dp % 4, "core": seq % 2}
        sizes = {"x": 4, "y": 4, "z": 4, "core": 2}
        self.peers = {
            axis: [(self.at[axis] + step) % size for step in range(1, size)] for axis, size in sizes.items()
        }
        self.devices = {
            axis: [(peer, self.other(axis, peer)) for peer in peers] for axis, peers in self.peers.items()
        }

    def device(self, axis, peer):
        for known, device in self.devices[axis]:
            if known is peer:
                return device
        return self.other(axis, peer)

    def other(self, axis, value):
        at = {**self.at, axis: value}
        return {"dp": at["y"] // 2 * 4 + at["z"], "seq": at["x"] * 4 + at["y"] % 2 * 2 + at["core"]}


HALVES, TURN, PASS, SPREAD, LAST, COLLECT, SHARE, RELAY, BACK = range(9)


class Sum:
    def __init__(self, place, slot, axes, part, total, halves, turns, quarters, pieces, lasts, send_sem, recv_sem):
        self.place, self.slot, self.axes = place, slot, axes
        self.part, self.total = part, total
        self.halves, self.turns, self.quarters, self.pieces, self.lasts = halves, turns, quarters, pieces, lasts
        self.send_sem, self.recv_sem = send_sem, recv_sem
        rows, columns = part.shape
        self.sizes = [rows, rows // 2, rows // 8, rows // 32]
        base, self.bases = 0, [0]
        for size, name in zip(self.sizes[1:], ("core", *axes)):
            base = base + place.at[name] * size
            self.bases.append(base)
        self.right, self.far, self.left = place.peers[axes[0]]
        self.sides = (pl.ds(0, columns // 2), pl.ds(columns // 2, columns // 2))
        self.done = 0

    def span(self, level, coordinate=None):
        base = self.bases[level] if coordinate is None else self.bases[level - 1] + coordinate * self.sizes[level]
        return pl.ds(pl.multiple_of(base, 16), self.sizes[level])

    def copy(self, source, target, send, recv, axis, peer):
        return pltpu.make_async_remote_copy(
            src_ref=source,
            dst_ref=target,
            send_sem=self.send_sem.at[self.slot, send],
            recv_sem=self.recv_sem.at[self.slot, recv],
            device_id=self.place.device(axis, peer),
            device_id_type=MESH,
        )

    def partner(self, kind):
        peer = self.place.peers["core"][0]
        if kind == HALVES:
            return self.copy(self.part.at[self.span(1, peer), :], self.halves, 0, kind, "core", peer)
        rows = self.total.at[self.span(1), :]
        return self.copy(rows, rows, 0, kind, "core", peer)

    def around(self, kind, way):
        peer = (self.right, self.left)[way]
        other = (self.left, self.right)[way]
        side = self.sides[way]
        if kind == TURN:
            source, target = self.part.at[self.span(2, self.far), side], self.turns.at[way]
        elif kind == PASS:
            source, target = self.part.at[self.span(2, peer), :], self.quarters.at[way]
        elif kind == SHARE:
            source = target = self.total.at[self.span(2), :]
        else:
            source = target = self.total.at[self.span(2, other), side]
        return self.copy(source, target, 1, kind, self.axes[0], peer)

    def along(self, kind, here, there):
        axis = self.axes[2] if kind == LAST else self.axes[1]
        if kind == SPREAD:
            source, target = self.part.at[self.span(3, there), :], self.pieces.at[here]
        elif kind == LAST:
            source = target = self.lasts.at[here]
        else:
            source = target = self.total.at[self.span(3, here), :]
        return self.copy(source, target, 2, kind, axis, there)

    def start_around(self, kind):
        for way in range(2):
            self.around(kind, way).start()

    def start_along(self, kind):
        axis = self.axes[2] if kind == LAST else self.axes[1]
        for peer in self.place.peers[axis]:
            self.along(kind, self.place.at[axis], peer).start()

    def arrive(self, kind):
        rows = self.part.shape[0]
        eighth, last = rows // 8, rows // 32
        held = {
            HALVES: self.halves,
            TURN: self.turns,
            PASS: self.quarters,
            SPREAD: self.pieces.at[pl.ds(0, 3)],
            LAST: self.lasts.at[pl.ds(0, 3)],
            COLLECT: self.total.at[pl.ds(0, 3 * last), :],
            SHARE: self.total.at[pl.ds(0, 2 * eighth), :],
            RELAY: self.total.at[pl.ds(0, eighth), :],
            BACK: self.total.at[pl.ds(0, rows // 2), :],
        }[kind]
        pltpu.make_async_copy(held, held, self.recv_sem.at[self.slot, kind]).wait()

    def add(self, rows, side, *arrived):
        value = self.part[rows, side].astype(F32)
        for each in arrived:
            value += each.astype(F32)
        return value.astype(BF16)

    def step(self):
        step, self.done = self.done, self.done + 1
        everything = pl.ds(0, self.part.shape[1])
        if step == 0:
            self.partner(HALVES).start()
        elif step == 1:
            self.arrive(HALVES)
            self.part[self.span(1), :] = self.add(self.span(1), everything, self.halves[...])
            self.start_around(TURN)
        elif step == 2:
            self.arrive(TURN)
            for way, peer in enumerate((self.right, self.left)):
                rows, side = self.span(2, peer), self.sides[way]
                self.part[rows, side] = self.add(rows, side, self.turns[way])
            self.start_around(PASS)
        elif step == 3:
            self.arrive(PASS)
            self.part[self.span(2), :] = self.add(self.span(2), everything, self.quarters[0], self.quarters[1])
            self.start_along(SPREAD)
        elif step == 4:
            self.arrive(SPREAD)
            mine = self.place.at[self.axes[2]]
            peers = self.place.peers[self.axes[1]]
            self.lasts[mine] = self.add(self.span(3), everything, *[self.pieces[peer] for peer in peers])
            self.start_along(LAST)
        elif step == 5:
            self.arrive(LAST)
            value = self.lasts[0].astype(F32)
            for peer in range(1, 4):
                value += self.lasts[peer].astype(F32)
            self.total[self.span(3), :] = value.astype(BF16)
            self.start_along(COLLECT)
        elif step == 6:
            self.arrive(COLLECT)
            self.start_around(SHARE)
        elif step == 7:
            self.arrive(SHARE)
            self.start_around(RELAY)
        elif step == 8:
            self.arrive(RELAY)
            self.partner(BACK).start()
        elif step == 9:
            self.arrive(BACK)

    def clear(self):
        rows = self.part.shape[0]
        for index, sent in enumerate((rows, 6 * rows // 8, 9 * rows // 32)):
            held = self.part.at[pl.ds(0, sent), :]
            pltpu.make_async_copy(held, held, self.send_sem.at[self.slot, index]).wait()


class SmallSum:
    axes = ("core", "x", "y", "z")

    def __init__(self, place, boxes, send_sem, recv_sem):
        self.place, self.boxes, self.send_sem, self.recv_sem = place, boxes, send_sem, recv_sem
        self.done = 0

    def hop(self, step, here, there):
        box = self.boxes.at[step, here]
        return pltpu.make_async_remote_copy(
            src_ref=box,
            dst_ref=box,
            send_sem=self.send_sem.at[step],
            recv_sem=self.recv_sem.at[step],
            device_id=self.place.device(self.axes[step], there),
            device_id_type=MESH,
        )

    def send(self, value):
        axis = self.axes[self.done]
        mine = self.place.at[axis]
        self.boxes[self.done, mine] = value
        for peer in self.place.peers[axis]:
            self.hop(self.done, mine, peer).start()

    def receive(self):
        axis = self.axes[self.done]
        self.wait(self.done, self.recv_sem)
        value = self.boxes[self.done, 0]
        for peer in range(1, len(self.place.peers[axis]) + 1):
            value += self.boxes[self.done, peer]
        self.done += 1
        return value

    def wait(self, step, sem):
        held = self.boxes.at[step, pl.ds(0, len(self.place.peers[self.axes[step]]))]
        pltpu.make_async_copy(held, held, sem.at[step]).wait()

    def clear(self):
        for step in range(len(self.axes)):
            self.wait(step, self.send_sem)


TO_X, TO_COT, BACK_R, BACK_D = range(4)
GROUPS = 2
PAIR = 2
SUMS = (
    (1024, ("x", "z", "y")),
    (1024, ("z", "x", "y")),
    (512, ("x", "z", "y")),
    (768, ("z", "x", "y")),
    (256, ("x", "y", "z")),
    (256, ("z", "y", "x")),
    (256, ("y", "x", "z")),
)


def kernel(
    points, lists, gains, w_qkv, w_out, cotangent,
    mixed_out, points_out, gain_out, qkv_out, out_out,
    order, x, cot, gain, wqkv, wout, wqkv_t, onto, y,
    h0, qkv0, p0, att0, inv0, h1, qkv1, p1, att1, inv1, dqkv, d_att,
    sent, got, d_x, g_gain, *rest,
):
    sum_boxes, rest = rest[: 7 * len(SUMS)], rest[7 * len(SUMS) :]
    boxes, load_sem, store_sem, send_sem, recv_sem, sum_send, sum_recv, small_send, small_recv = rest
    groups = lax.axis_size("seq")
    me = lax.axis_index("seq")
    rows = x.shape[0]
    block = rows // groups
    balls = rows // BALL
    near = groups // balls
    home = me // near
    seat = me % near
    place = Place()
    sums = [
        Sum(place, slot, axes, *sum_boxes[7 * slot : 7 * slot + 7], sum_send, sum_recv)
        for slot, (columns, axes) in enumerate(SUMS)
    ]
    upper, sum_o, sum_q, last = sums[0:2], sums[2], sums[3], sums[4:7]
    small = SmallSum(place, boxes, small_send, small_recv)

    loads = []

    def load(source, target):
        copy = pltpu.make_async_copy(source, target, load_sem.at[len(loads)])
        copy.start()
        loads.append(copy)
        return copy

    lists_in = load(lists, order)
    cot_in = load(cotangent.at[0], cot)
    x_in = load(points.at[0], x)
    small_in = [load(gains, gain), load(w_qkv.at[0], wqkv.at[0]), load(w_out.at[0], wout.at[0])]
    late_in = [load(w_qkv.at[1], wqkv.at[1]), load(w_out.at[1], wout.at[1])]

    barrier = pltpu.get_barrier_semaphore()
    for step in range(1, near):
        pl.semaphore_signal(
            barrier, inc=1, device_id={"seq": home * near + (seat + step) % near}, device_id_type=MESH
        )
    for axis in ("x", "z"):
        for peer in place.peers[axis]:
            pl.semaphore_signal(barrier, inc=1, device_id=place.other(axis, peer), device_id_type=MESH)
    for step in range(2):
        far = (place.at["y"] // 2 * 2 + 2 + step) % 4
        pl.semaphore_signal(barrier, inc=1, device_id=place.other("y", far), device_id_type=MESH)

    def span(index):
        return pl.ds(pl.multiple_of(index * block, block), block)

    others = [(seat + step) % near for step in range(1, near)]

    def transfer(kind, ball, here, there):
        return pltpu.make_async_remote_copy(
            src_ref=sent.at[kind, span(ball * near + there), :],
            dst_ref=got.at[kind, span(ball * near + here), :],
            send_sem=send_sem.at[kind],
            recv_sem=recv_sem.at[kind, ball],
            device_id={"seq": home * near + there},
            device_id_type=MESH,
        )

    def send(kind, ball):
        for peer in others:
            transfer(kind, ball, seat, peer).start()
        own = span(ball * near + seat)
        got[kind, own, :] = sent[kind, own, :]

    def arrive(kind, ball):
        held = got.at[kind, pl.ds(0, (near - 1) * block), :]
        pltpu.make_async_copy(held, held, recv_sem.at[kind, ball]).wait()

    def gather(kind, source, ball):
        sent[kind, cols(ball, PAIR), :] = nn(onto[cols(ball, PAIR), :], source[...]).astype(BF16)

    lists_in.wait()

    @pl.loop(0, rows // 128)
    def _(part):
        first = pl.multiple_of(part * 128, 128)
        onto[pl.ds(first, 128), :] = one_hot_to_rotated(order, first)

    cot_in.wait()
    pl.semaphore_wait(barrier, near - 1 + 8)

    @pl.loop(0, balls, step=PAIR)
    def _(ball):
        gather(TO_COT, cot, ball)
        for nth in range(PAIR):
            send(TO_COT, ball + nth)

    x_in.wait()
    for copy in small_in:
        copy.wait()
    transpose_by_unit(wqkv.at[0], wqkv_t.at[0])

    @pl.loop(0, balls, step=PAIR)
    def _(ball):
        here = cols(ball, PAIR)
        y[here, :] = forward_balls(
            ball, PAIR, ball, x[here, :], gain[0:1], wqkv_t.at[0], wout.at[0], h0, qkv0, p0, att0, inv0
        ).astype(BF16)

    @pl.loop(0, balls, step=PAIR)
    def _(ball):
        gather(TO_X, y, ball)
        for nth in range(PAIR):
            send(TO_X, ball + nth)

    for copy in late_in:
        copy.wait()
    transpose_by_unit(wqkv.at[1], wqkv_t.at[1])
    g_gain[...] = jnp.zeros_like(g_gain)

    @pl.loop(0, balls)
    def _(ball):
        arrive(TO_X, ball)
        rows_x = got[TO_X, cols(ball), :]
        sent[BACK_R, cols(ball), :] = forward_balls(
            ball, 1, 0, rows_x, gain[1:2], wqkv_t.at[1], wout.at[1], h1, qkv1, p1, att1, inv1
        ).astype(BF16)
        arrive(TO_COT, ball)
        d_r = got[TO_COT, cols(ball), :]
        d_att[:, cols(ball)] = nt(wout[1], d_r).astype(BF16)
        backward_heads(ball, 0, range(HEADS), d_att, qkv1, p1, att1, inv1, dqkv)
        sent[BACK_D, cols(ball), :], gained = backward_norm(
            ball, 1, got[TO_X, cols(ball), :], gain[1:2], d_r, wqkv.at[1], dqkv
        )
        send(BACK_D, ball)
        g_gain[1:2] += gained

    @pl.loop(0, balls)
    def _(ball):
        send(BACK_R, ball)

    stores = []

    def store(source, target):
        copy = pltpu.make_async_copy(source, target, store_sem.at[len(stores)])
        copy.start()
        stores.append(copy)
        return copy

    width = x.shape[1]
    first, second = upper[0].part, upper[1].part
    second[:, width:] = nn(att1[...], got[TO_COT]).astype(BF16)
    first[...] = nt(h1[...], dqkv[: 2 * width, :]).astype(BF16)
    second[:, :width] = nt(h1[...], dqkv[2 * width :, :]).astype(BF16)

    def advance(*which):
        for each in which:
            each.step()

    advance(*upper)

    @pl.loop(0, balls)
    def _(ball):
        arrive(BACK_D, ball)

    @pl.loop(0, balls, step=PAIR)
    def _(ball):
        here = cols(ball, PAIR)
        y[here, :] = nn(one_hot_to_tree(order, ball * BALL, PAIR * BALL), got[BACK_D]).astype(BF16)
        d_att[:, here] = nt(wout[0], y[here, :]).astype(BF16)

        @pl.when(ball == 0)
        def _():
            advance(*upper)

    sum_o.part[...] = nn(att0[...], y[...]).astype(BF16)
    advance(sum_o)
    span_q = width // GROUPS
    heads = HEADS // GROUPS
    for group in range(GROUPS):

        @pl.loop(0, balls)
        def _(ball):
            backward_heads(
                ball, ball, range(group * heads, (group + 1) * heads), d_att, qkv0, p0, att0, inv0, dqkv
            )

            @pl.when(ball == 0)
            def _():
                advance(*upper)

            @pl.when(ball == 2)
            def _():
                if group == 0:
                    advance(sum_o)
                else:
                    advance(sum_q, sum_o)

        for kind in range(3):
            low = kind * width + group * span_q
            g = nt(h0[...], dqkv[low : low + span_q, :]).astype(BF16)
            if group == 0:
                sum_q.part[:, kind * span_q : (kind + 1) * span_q] = g
            else:
                last[kind].part[...] = g
                advance(last[kind])
        if group == 0:
            advance(sum_q)
        else:
            advance(*upper)

    @pl.loop(0, balls, step=PAIR)
    def _(ball):
        here = cols(ball, PAIR)
        d_x[here, :], gained = backward_norm(
            ball, PAIR, x[here, :], gain[0:1], y[here, :], wqkv.at[0], dqkv
        )
        g_gain[0:1] += gained

        @pl.when(ball == 0)
        def _():
            advance(sum_q, sum_o, *upper, *last)

    advance(sum_q, sum_o, *last)
    small.send(g_gain[...])
    advance(*upper, *last)
    store(d_x, points_out.at[0])

    @pl.loop(0, balls)
    def _(ball):
        arrive(BACK_R, ball)

    @pl.loop(0, balls, step=PAIR)
    def _(ball):
        here = cols(ball, PAIR)
        cot[here, :] = nn(one_hot_to_tree(order, ball * BALL, PAIR * BALL), got[BACK_R]).astype(BF16)

        @pl.when(ball == 0)
        def _():
            advance(sum_q, sum_o)

    store(cot, mixed_out.at[0])
    for step in range(10):
        advance(*sums)
        if small.done < 3:
            small.send(small.receive())
    g_gain[...] = small.receive()
    store(g_gain.at[0:2], gain_out)
    store(upper[0].total, qkv_out.at[1, :, : 2 * width])
    store(upper[1].total.at[:, :width], qkv_out.at[1, :, 2 * width :])
    store(upper[1].total.at[:, width:], out_out.at[1])
    store(sum_o.total, out_out.at[0])
    for kind in range(3):
        low = kind * width
        store(sum_q.total.at[:, kind * span_q : (kind + 1) * span_q], qkv_out.at[0, :, low : low + span_q])
        store(last[kind].total, qkv_out.at[0, :, low + span_q : low + width])
    for copy in stores:
        copy.wait()
    for each in sums:
        each.clear()
    small.clear()

    for kind in range(4):
        held = sent.at[kind, pl.ds(0, balls * (near - 1) * block), :]
        pltpu.make_async_copy(held, held, send_sem.at[kind]).wait()


def finish_kernel(mixed, d_x, gain, qkv, out, mixed_out, points_out, gain_out, qkv_out, out_out, *rest):
    mixed_v, d_x_v, gain_v, qkv_v, out_v, qkv_f, out_f, load_sem, store_sem = rest
    rows = BALL
    moves = [(mixed, mixed_v, mixed_v, mixed_out), (d_x, d_x_v, d_x_v, points_out), (gain, gain_v, gain_v, gain_out)]
    for layer in range(qkv.shape[0]):
        for low in range(0, qkv.shape[1], rows):
            at = (layer, pl.ds(low, rows))
            moves.append((qkv.at[at], qkv_v.at[at], qkv_f.at[at], qkv_out.at[at]))
            moves.append((out.at[at], out_v.at[at], out_f.at[at], out_out.at[at]))
    moves = moves[3:] + moves[:3]
    loads = [pltpu.make_async_copy(m[0], m[1], load_sem.at[i]) for i, m in enumerate(moves)]
    stores = [pltpu.make_async_copy(m[2], m[3], store_sem.at[i]) for i, m in enumerate(moves)]
    for copy in loads:
        copy.start()
    for load, store, (_, held, ready, _) in zip(loads, stores, moves):
        load.wait()
        if held is not ready:
            ready[...] = held[...].astype(F32)
        store.start()
    for copy in stores:
        copy.wait()


def local(points, ball_lists, gains, w_qkv, w_out, cotangent):
    groups = lax.axis_size("seq")
    rows, width = points.shape[1:]
    balls = rows // BALL
    any_place = pl.BlockSpec(memory_space=pl.ANY)

    def saved(keep):
        return [
            pltpu.VMEM((width, rows), BF16),
            pltpu.VMEM((3 * width, rows), BF16),
            pltpu.VMEM((keep, HEADS, BALL, BALL), BF16),
            pltpu.VMEM((width, rows), BF16),
            pltpu.VMEM((keep, HEADS, BALL), F32),
        ]

    token = pltpu.VMEM((rows, width), BF16)

    def sums(columns):
        shapes = [(width, columns), (width, columns), (width // 2, columns), (2, width // 8, columns // 2)]
        shapes += [(2, width // 8, columns), (4, width // 32, columns), (4, width // 32, columns)]
        return [pltpu.VMEM(shape, BF16) for shape in shapes]

    parts = pl.pallas_call(
        kernel,
        out_shape=[
            jax.ShapeDtypeStruct(points.shape, BF16),
            jax.ShapeDtypeStruct(points.shape, BF16),
            jax.ShapeDtypeStruct(gains.shape, F32),
            jax.ShapeDtypeStruct(w_qkv.shape, BF16),
            jax.ShapeDtypeStruct(w_out.shape, BF16),
        ],
        in_specs=[any_place] * 6,
        out_specs=[any_place] * 5,
        scratch_shapes=[
            pltpu.VMEM((1, rows), jnp.int32),
            token,
            token,
            pltpu.VMEM(gains.shape, F32),
            pltpu.VMEM(w_qkv.shape, BF16),
            pltpu.VMEM(w_out.shape, BF16),
            pltpu.VMEM((2, 3 * width, width), BF16),
            pltpu.VMEM((rows, rows), BF16),
            token,
            *saved(balls),
            *saved(1),
            pltpu.VMEM((3 * width, rows), BF16),
            pltpu.VMEM((width, rows), BF16),
            pltpu.VMEM((4, rows, width), BF16),
            pltpu.VMEM((4, rows, width), BF16),
            token,
            pltpu.VMEM((8, width), F32),
            *[box for columns, _ in SUMS for box in sums(columns)],
            pltpu.VMEM((4, 4, 8, width), F32),
            pltpu.SemaphoreType.DMA((8,)),
            pltpu.SemaphoreType.DMA((16,)),
            pltpu.SemaphoreType.DMA((4,)),
            pltpu.SemaphoreType.DMA((4, balls)),
            pltpu.SemaphoreType.DMA((len(SUMS), 3)),
            pltpu.SemaphoreType.DMA((len(SUMS), 9)),
            pltpu.SemaphoreType.DMA((4,)),
            pltpu.SemaphoreType.DMA((4,)),
        ],
        compiler_params=pltpu.CompilerParams(
            vmem_limit_bytes=VMEM_BYTES, collective_id=0, has_side_effects=True
        ),
    )(points, ball_lists, gains, w_qkv, w_out, cotangent)
    results = [*parts[:3], *(jax.ShapeDtypeStruct(part.shape, F32) for part in parts[3:])]
    moves = 3 + 4 * width // BALL
    return pl.pallas_call(
        finish_kernel,
        out_shape=[jax.ShapeDtypeStruct(result.shape, result.dtype) for result in results],
        in_specs=[any_place] * 5,
        out_specs=[any_place] * 5,
        scratch_shapes=[
            *[pltpu.VMEM(part.shape, part.dtype) for part in parts],
            *[pltpu.VMEM(part.shape, F32) for part in parts[3:]],
            pltpu.SemaphoreType.DMA((moves,)),
            pltpu.SemaphoreType.DMA((moves,)),
        ],
        compiler_params=pltpu.CompilerParams(vmem_limit_bytes=VMEM_BYTES),
    )(*parts)


def solution(mesh):
    return jax.shard_map(
        local,
        mesh=mesh,
        in_specs=(P("dp", "seq", None), P("dp", "seq"), P(), P(), P(), P("dp", "seq", None)),
        out_specs=(P("dp", "seq", None), P("dp", "seq", None), P(), P(), P()),
        check_vma=False,
    )
```

```python
import jax
import jax.numpy as jnp
from jax import lax
from jax.experimental import pallas as pl
from jax.experimental.pallas import tpu as pltpu
from jax.sharding import PartitionSpec as P

MESH = pl.DeviceIdType.MESH
HEADS = 8
BALL = 256
EPS = 1e-05
F32 = jnp.float32
BF16 = jnp.bfloat16
VMEM_BYTES = 62 * 1024 * 1024


def dot(a, b, ca, cb):
    return lax.dot_general(a, b, (((ca,), (cb,)), ((), ())), preferred_element_type=F32)


def nn(a, b):
    return dot(a, b, 1, 0)


def nt(a, b):
    return dot(a, b, 1, 1)


def tn(a, b):
    return dot(a, b, 0, 0)


def cols(ball, count=1):
    return pl.ds(pl.multiple_of(ball * BALL, BALL), count * BALL)


def norm_scale(x):
    return lax.rsqrt(jnp.mean(x * x, axis=1, keepdims=True) + EPS)


def one_hot_to_rotated(order_row, first):
    rows = order_row.shape[1]
    lane = 128
    held = jnp.broadcast_to(order_row[:, pl.ds(pl.multiple_of(first, lane), lane)], (lane, lane)).T
    row = lax.broadcasted_iota(jnp.int32, (lane, lane), 1)
    parts = [jnp.where(held == row + low, 1.0, 0.0).astype(BF16) for low in range(0, rows, lane)]
    return jnp.concatenate(parts, axis=1)


def one_hot_to_tree(order_row, first, rows):
    tree = lax.broadcasted_iota(jnp.int32, (rows, order_row.shape[1]), 0) + first
    return jnp.where(order_row[...] == tree, 1.0, 0.0).astype(BF16)


def transpose_by_unit(wqkv, wqkv_t):
    unit = jnp.where(
        lax.broadcasted_iota(jnp.int32, (BALL, BALL), 0) == lax.broadcasted_iota(jnp.int32, (BALL, BALL), 1), 1.0, 0.0
    ).astype(BF16)
    for low in range(0, wqkv.shape[1], BALL):
        wqkv_t[low : low + BALL, :] = nt(unit, wqkv[:, low : low + BALL]).astype(BF16)


def forward_balls(ball, count, keep, x, gain, wqkv_t, wout, h_t, qkv_t, p_t, att_t, inv):
    width = x.shape[1]
    size = width // HEADS
    here = cols(ball, count)
    values = x.astype(F32)
    hidden = (values * norm_scale(values) * gain).astype(BF16)
    hidden_t = hidden.T
    h_t[:, here] = hidden_t
    qkv_t[:, here] = nn(wqkv_t[...], hidden_t).astype(BF16)

    def score(item):
        nth, head = item
        low = head * size
        q = qkv_t[low : low + size, cols(ball + nth)] * size ** (-0.5)
        return tn(qkv_t[width + low : width + low + size, cols(ball + nth)], q)

    def weigh(item, scores):
        nth, head = item
        weights = jnp.exp(scores - jnp.max(scores, axis=0, keepdims=True))
        share = 1.0 / jnp.sum(weights, axis=0, keepdims=True)
        weights = weights.astype(BF16)
        p_t[keep + nth, head] = weights
        inv[keep + nth, head : head + 1, :] = share
        return weights, share

    def mix(item, weights, share):
        nth, head = item
        low = head * size
        v = qkv_t[2 * width + low : 2 * width + low + size, cols(ball + nth)]
        att_t[low : low + size, cols(ball + nth)] = (nn(v, weights) * share).astype(BF16)

    staggered([(nth, head) for nth in range(count) for head in range(HEADS)], score, weigh, mix)
    return values + tn(att_t[:, here], wout[...])


def staggered(heads, *stages):
    heads = list(heads)
    held = {}
    for step in range(len(heads) + len(stages) - 1):
        for index, stage in enumerate(stages):
            if 0 <= step - index < len(heads):
                head = heads[step - index]
                given = held.pop((head, index), ())
                result = stage(head, *given)
                held[head, index + 1] = result if isinstance(result, tuple) else (result,)


def backward_heads(ball, keep, heads, d_att, qkv_t, p_t, att_t, inv, dqkv_t):
    width = d_att.shape[0]
    size = width // HEADS
    here = cols(ball)

    def weigh(head):
        low = head * size
        v = qkv_t[2 * width + low : 2 * width + low + size, here]
        d_out = d_att[low : low + size, here].astype(F32) * inv[keep, head : head + 1, :]
        delta = jnp.sum(d_out * att_t[low : low + size, here].astype(F32), axis=0, keepdims=True)
        d_out = d_out.astype(BF16)
        return d_out, delta, tn(v, d_out)

    def score(head, d_out, delta, d_weights):
        weights = p_t[keep, head]
        return d_out, weights, (weights.astype(F32) * (d_weights - delta)).astype(BF16)

    def spread(head, d_out, weights, d_scores):
        low = head * size
        q = qkv_t[low : low + size, here] * size ** (-0.5)
        k = qkv_t[width + low : width + low + size, here]
        dqkv_t[low : low + size, here] = (nn(k, d_scores) * size ** (-0.5)).astype(BF16)
        dqkv_t[width + low : width + low + size, here] = nt(q, d_scores).astype(BF16)
        dqkv_t[2 * width + low : 2 * width + low + size, here] = nt(d_out, weights).astype(BF16)

    staggered(heads, weigh, score, spread)


def backward_norm(ball, count, x, gain, dy, wqkv, dqkv_t):
    d_h = nn(wqkv[...], dqkv_t[:, cols(ball, count)]).T
    values = x.astype(F32)
    scale = norm_scale(values)
    unit = values * scale
    d_unit = d_h * gain
    d_n = scale * (d_unit - unit * jnp.mean(d_unit * unit, axis=1, keepdims=True))
    d_x = dy.astype(F32) + d_n.astype(BF16).astype(F32)
    return d_x.astype(BF16), jnp.sum(d_h * unit, axis=0, keepdims=True)


class Place:
    def __init__(self):
        dp, seq = lax.axis_index("dp"), lax.axis_index("seq")
        self.at = {"x": seq // 4, "y": dp // 4 * 2 + seq // 2 % 2, "z": dp % 4, "core": seq % 2}
        sizes = {"x": 4, "y": 4, "z": 4, "core": 2}
        self.peers = {
            axis: [(self.at[axis] + step) % size for step in range(1, size)] for axis, size in sizes.items()
        }
        self.devices = {
            axis: [(peer, self.other(axis, peer)) for peer in peers] for axis, peers in self.peers.items()
        }

    def device(self, axis, peer):
        for known, device in self.devices[axis]:
            if known is peer:
                return device
        return self.other(axis, peer)

    def other(self, axis, value):
        at = {**self.at, axis: value}
        return {"dp": at["y"] // 2 * 4 + at["z"], "seq": at["x"] * 4 + at["y"] % 2 * 2 + at["core"]}


STEPS = 10
HALVES, TURN, PASS, SPREAD, LAST, COLLECT, SHARE, RELAY, BACK = range(9)


class Sum:
    def __init__(self, place, slot, axes, part, total, halves, turns, quarters, pieces, lasts, send_sem, recv_sem):
        self.place, self.slot, self.axes = place, slot, axes
        self.part, self.total = part, total
        self.halves, self.turns, self.quarters, self.pieces, self.lasts = halves, turns, quarters, pieces, lasts
        self.send_sem, self.recv_sem = send_sem, recv_sem
        rows, columns = part.shape
        self.sizes = [rows, rows // 2, rows // 8, rows // 32]
        base, self.bases = 0, [0]
        for size, name in zip(self.sizes[1:], ("core", *axes)):
            base = base + place.at[name] * size
            self.bases.append(base)
        self.right, self.far, self.left = place.peers[axes[0]]
        self.sides = (pl.ds(0, columns // 2), pl.ds(columns // 2, columns // 2))
        self.done = 0

    def span(self, level, coordinate=None):
        base = self.bases[level] if coordinate is None else self.bases[level - 1] + coordinate * self.sizes[level]
        return pl.ds(pl.multiple_of(base, 16), self.sizes[level])

    def copy(self, source, target, send, recv, axis, peer):
        return pltpu.make_async_remote_copy(
            src_ref=source,
            dst_ref=target,
            send_sem=self.send_sem.at[self.slot, send],
            recv_sem=self.recv_sem.at[self.slot, recv],
            device_id=self.place.device(axis, peer),
            device_id_type=MESH,
        )

    def partner(self, kind):
        peer = self.place.peers["core"][0]
        if kind == HALVES:
            return self.copy(self.part.at[self.span(1, peer), :], self.halves, 0, kind, "core", peer)
        rows = self.total.at[self.span(1), :]
        return self.copy(rows, rows, 0, kind, "core", peer)

    def around(self, kind, way):
        peer = (self.right, self.left)[way]
        other = (self.left, self.right)[way]
        side = self.sides[way]
        if kind == TURN:
            source, target = self.part.at[self.span(2, self.far), side], self.turns.at[way]
        elif kind == PASS:
            source, target = self.part.at[self.span(2, peer), :], self.quarters.at[way]
        elif kind == SHARE:
            source = target = self.total.at[self.span(2), :]
        else:
            source = target = self.total.at[self.span(2, other), side]
        return self.copy(source, target, 1, kind, self.axes[0], peer)

    def along(self, kind, here, there):
        axis = self.axes[2] if kind == LAST else self.axes[1]
        if kind == SPREAD:
            source, target = self.part.at[self.span(3, there), :], self.pieces.at[here]
        elif kind == LAST:
            source = target = self.lasts.at[here]
        else:
            source = target = self.total.at[self.span(3, here), :]
        return self.copy(source, target, 2, kind, axis, there)

    def start_around(self, kind):
        for way in range(2):
            self.around(kind, way).start()

    def start_along(self, kind):
        axis = self.axes[2] if kind == LAST else self.axes[1]
        for peer in self.place.peers[axis]:
            self.along(kind, self.place.at[axis], peer).start()

    def arrive(self, kind):
        rows = self.part.shape[0]
        eighth, last = rows // 8, rows // 32
        held = {
            HALVES: self.halves,
            TURN: self.turns,
            PASS: self.quarters,
            SPREAD: self.pieces.at[pl.ds(0, 3)],
            LAST: self.lasts.at[pl.ds(0, 3)],
            COLLECT: self.total.at[pl.ds(0, 3 * last), :],
            SHARE: self.total.at[pl.ds(0, 2 * eighth), :],
            RELAY: self.total.at[pl.ds(0, eighth), :],
            BACK: self.total.at[pl.ds(0, rows // 2), :],
        }[kind]
        pltpu.make_async_copy(held, held, self.recv_sem.at[self.slot, kind]).wait()

    def add(self, rows, side, *arrived):
        value = self.part[rows, side].astype(F32)
        for each in arrived:
            value += each.astype(F32)
        return value.astype(BF16)

    def step(self):
        step, self.done = self.done, self.done + 1
        everything = pl.ds(0, self.part.shape[1])
        if step == 0:
            self.partner(HALVES).start()
        elif step == 1:
            self.arrive(HALVES)
            self.part[self.span(1), :] = self.add(self.span(1), everything, self.halves[...])
            self.start_around(TURN)
        elif step == 2:
            self.arrive(TURN)
            for way, peer in enumerate((self.right, self.left)):
                rows, side = self.span(2, peer), self.sides[way]
                self.part[rows, side] = self.add(rows, side, self.turns[way])
            self.start_around(PASS)
        elif step == 3:
            self.arrive(PASS)
            self.part[self.span(2), :] = self.add(self.span(2), everything, self.quarters[0], self.quarters[1])
            self.start_along(SPREAD)
        elif step == 4:
            self.arrive(SPREAD)
            mine = self.place.at[self.axes[2]]
            peers = self.place.peers[self.axes[1]]
            self.lasts[mine] = self.add(self.span(3), everything, *[self.pieces[peer] for peer in peers])
            self.start_along(LAST)
        elif step == 5:
            self.arrive(LAST)
            value = self.lasts[0].astype(F32)
            for peer in range(1, 4):
                value += self.lasts[peer].astype(F32)
            self.total[self.span(3), :] = value.astype(BF16)
            self.start_along(COLLECT)
        elif step == 6:
            self.arrive(COLLECT)
            self.start_around(SHARE)
        elif step == 7:
            self.arrive(SHARE)
            self.start_around(RELAY)
        elif step == 8:
            self.arrive(RELAY)
            self.partner(BACK).start()
        elif step == 9:
            self.arrive(BACK)

    def clear(self):
        rows = self.part.shape[0]
        for index, sent in enumerate((rows, 6 * rows // 8, 9 * rows // 32)):
            held = self.part.at[pl.ds(0, sent), :]
            pltpu.make_async_copy(held, held, self.send_sem.at[self.slot, index]).wait()


class SmallSum:
    axes = ("core", "x", "y", "z")

    def __init__(self, place, boxes, send_sem, recv_sem):
        self.place, self.boxes, self.send_sem, self.recv_sem = place, boxes, send_sem, recv_sem
        self.done = 0

    def hop(self, step, here, there):
        box = self.boxes.at[step, here]
        return pltpu.make_async_remote_copy(
            src_ref=box,
            dst_ref=box,
            send_sem=self.send_sem.at[step],
            recv_sem=self.recv_sem.at[step],
            device_id=self.place.device(self.axes[step], there),
            device_id_type=MESH,
        )

    def send(self, value):
        axis = self.axes[self.done]
        mine = self.place.at[axis]
        self.boxes[self.done, mine] = value
        for peer in self.place.peers[axis]:
            self.hop(self.done, mine, peer).start()

    def receive(self):
        axis = self.axes[self.done]
        self.wait(self.done, self.recv_sem)
        value = self.boxes[self.done, 0]
        for peer in range(1, len(self.place.peers[axis]) + 1):
            value += self.boxes[self.done, peer]
        self.done += 1
        return value

    def wait(self, step, sem):
        held = self.boxes.at[step, pl.ds(0, len(self.place.peers[self.axes[step]]))]
        pltpu.make_async_copy(held, held, sem.at[step]).wait()

    def clear(self):
        for step in range(len(self.axes)):
            self.wait(step, self.send_sem)


TO_X, TO_COT, BACK_R, BACK_D = range(4)
GROUPS = 2
PAIR = 2
SUMS = (
    (1024, ("x", "z", "y")),
    (1024, ("z", "x", "y")),
    (512, ("x", "z", "y")),
    (768, ("z", "x", "y")),
    (256, ("x", "y", "z")),
    (256, ("z", "y", "x")),
    (256, ("y", "x", "z")),
)


def kernel(
    points, lists, gains, w_qkv, w_out, cotangent,
    mixed_out, points_out, gain_out, qkv_out, out_out,
    order, x, cot, gain, wqkv, wout, wqkv_t, onto, y,
    h0, qkv0, p0, att0, inv0, h1, qkv1, p1, att1, inv1, dqkv, d_att,
    sent, got, d_x, g_gain, *rest,
):
    sum_boxes, rest = rest[: 7 * len(SUMS)], rest[7 * len(SUMS) :]
    boxes, load_sem, store_sem, send_sem, recv_sem, sum_send, sum_recv, small_send, small_recv = rest
    groups = lax.axis_size("seq")
    me = lax.axis_index("seq")
    rows = x.shape[0]
    block = rows // groups
    balls = rows // BALL
    near = groups // balls
    home = me // near
    seat = me % near
    place = Place()
    sums = [
        Sum(place, slot, axes, *sum_boxes[7 * slot : 7 * slot + 7], sum_send, sum_recv)
        for slot, (columns, axes) in enumerate(SUMS)
    ]
    upper, sum_o, sum_q, last = sums[0:2], sums[2], sums[3], sums[4:7]
    small = SmallSum(place, boxes, small_send, small_recv)

    loads = []

    def load(source, target):
        copy = pltpu.make_async_copy(source, target, load_sem.at[len(loads)])
        copy.start()
        loads.append(copy)
        return copy

    lists_in = load(lists, order)
    cot_in = load(cotangent.at[0], cot)
    x_in = load(points.at[0], x)
    small_in = [load(gains, gain), load(w_qkv.at[0], wqkv.at[0]), load(w_out.at[0], wout.at[0])]
    late_in = [load(w_qkv.at[1], wqkv.at[1]), load(w_out.at[1], wout.at[1])]

    barrier = pltpu.get_barrier_semaphore()
    for step in range(1, near):
        pl.semaphore_signal(
            barrier, inc=1, device_id={"seq": home * near + (seat + step) % near}, device_id_type=MESH
        )
    for axis in ("x", "z"):
        for peer in place.peers[axis]:
            pl.semaphore_signal(barrier, inc=1, device_id=place.other(axis, peer), device_id_type=MESH)
    for step in range(2):
        far = (place.at["y"] // 2 * 2 + 2 + step) % 4
        pl.semaphore_signal(barrier, inc=1, device_id=place.other("y", far), device_id_type=MESH)

    def span(index):
        return pl.ds(pl.multiple_of(index * block, block), block)

    others = [(seat + step) % near for step in range(1, near)]

    def transfer(kind, ball, here, there):
        return pltpu.make_async_remote_copy(
            src_ref=sent.at[kind, span(ball * near + there), :],
            dst_ref=got.at[kind, span(ball * near + here), :],
            send_sem=send_sem.at[kind],
            recv_sem=recv_sem.at[kind, ball],
            device_id={"seq": home * near + there},
            device_id_type=MESH,
        )

    def send(kind, ball):
        for peer in others:
            transfer(kind, ball, seat, peer).start()
        own = span(ball * near + seat)
        got[kind, own, :] = sent[kind, own, :]

    def arrive(kind, ball):
        held = got.at[kind, pl.ds(0, (near - 1) * block), :]
        pltpu.make_async_copy(held, held, recv_sem.at[kind, ball]).wait()

    def gather(kind, source, ball):
        sent[kind, cols(ball, PAIR), :] = nn(onto[cols(ball, PAIR), :], source[...]).astype(BF16)

    lists_in.wait()

    @pl.loop(0, rows // 128)
    def _(part):
        first = pl.multiple_of(part * 128, 128)
        onto[pl.ds(first, 128), :] = one_hot_to_rotated(order, first)

    cot_in.wait()
    pl.semaphore_wait(barrier, near - 1 + 8)

    @pl.loop(0, balls, step=PAIR)
    def _(ball):
        gather(TO_COT, cot, ball)
        for nth in range(PAIR):
            send(TO_COT, ball + nth)

    x_in.wait()
    for copy in small_in:
        copy.wait()
    transpose_by_unit(wqkv.at[0], wqkv_t.at[0])

    @pl.loop(0, balls, step=PAIR)
    def _(ball):
        here = cols(ball, PAIR)
        y[here, :] = forward_balls(
            ball, PAIR, ball, x[here, :], gain[0:1], wqkv_t.at[0], wout.at[0], h0, qkv0, p0, att0, inv0
        ).astype(BF16)

    @pl.loop(0, balls, step=PAIR)
    def _(ball):
        gather(TO_X, y, ball)
        for nth in range(PAIR):
            send(TO_X, ball + nth)

    for copy in late_in:
        copy.wait()
    transpose_by_unit(wqkv.at[1], wqkv_t.at[1])
    g_gain[...] = jnp.zeros_like(g_gain)

    @pl.loop(0, balls)
    def _(ball):
        arrive(TO_X, ball)
        rows_x = got[TO_X, cols(ball), :]
        sent[BACK_R, cols(ball), :] = forward_balls(
            ball, 1, 0, rows_x, gain[1:2], wqkv_t.at[1], wout.at[1], h1, qkv1, p1, att1, inv1
        ).astype(BF16)
        arrive(TO_COT, ball)
        d_r = got[TO_COT, cols(ball), :]
        d_att[:, cols(ball)] = nt(wout[1], d_r).astype(BF16)
        backward_heads(ball, 0, range(HEADS), d_att, qkv1, p1, att1, inv1, dqkv)
        sent[BACK_D, cols(ball), :], gained = backward_norm(
            ball, 1, got[TO_X, cols(ball), :], gain[1:2], d_r, wqkv.at[1], dqkv
        )
        send(BACK_D, ball)
        g_gain[1:2] += gained

    @pl.loop(0, balls)
    def _(ball):
        send(BACK_R, ball)

    stores = []

    def store(source, target):
        copy = pltpu.make_async_copy(source, target, store_sem.at[len(stores)])
        copy.start()
        stores.append(copy)
        return copy

    width = x.shape[1]
    first, second = upper[0].part, upper[1].part
    second[:, width:] = nn(att1[...], got[TO_COT]).astype(BF16)
    first[...] = nt(h1[...], dqkv[: 2 * width, :]).astype(BF16)
    second[:, :width] = nt(h1[...], dqkv[2 * width :, :]).astype(BF16)

    def advance(*which):
        for each in which:
            each.step()

    advance(*upper)

    @pl.loop(0, balls)
    def _(ball):
        arrive(BACK_D, ball)

    @pl.loop(0, balls, step=PAIR)
    def _(ball):
        here = cols(ball, PAIR)
        y[here, :] = nn(one_hot_to_tree(order, ball * BALL, PAIR * BALL), got[BACK_D]).astype(BF16)
        d_att[:, here] = nt(wout[0], y[here, :]).astype(BF16)

        @pl.when(ball == 0)
        def _():
            advance(*upper)

    sum_o.part[...] = nn(att0[...], y[...]).astype(BF16)
    advance(sum_o)
    span_q = width // GROUPS
    heads = HEADS // GROUPS
    for group in range(GROUPS):

        @pl.loop(0, balls)
        def _(ball):
            backward_heads(
                ball, ball, range(group * heads, (group + 1) * heads), d_att, qkv0, p0, att0, inv0, dqkv
            )

            @pl.when(ball == 2)
            def _():
                advance(sum_o)

        for kind in range(3):
            low = kind * width + group * span_q
            g = nt(h0[...], dqkv[low : low + span_q, :]).astype(BF16)
            if group == 0:
                sum_q.part[:, kind * span_q : (kind + 1) * span_q] = g
            else:
                last[kind].part[...] = g
                advance(last[kind])
        advance(*upper, sum_q)

    @pl.loop(0, balls, step=PAIR)
    def _(ball):
        here = cols(ball, PAIR)
        d_x[here, :], gained = backward_norm(
            ball, PAIR, x[here, :], gain[0:1], y[here, :], wqkv.at[0], dqkv
        )
        g_gain[0:1] += gained

        @pl.when(ball == 0)
        def _():
            advance(*last, sum_q, sum_o)

    small.send(g_gain[...])
    advance(*last, sum_q, *upper, sum_o)
    store(d_x, points_out.at[0])

    @pl.loop(0, balls)
    def _(ball):
        arrive(BACK_R, ball)

    @pl.loop(0, balls, step=PAIR)
    def _(ball):
        here = cols(ball, PAIR)
        cot[here, :] = nn(one_hot_to_tree(order, ball * BALL, PAIR * BALL), got[BACK_R]).astype(BF16)

        @pl.when(ball == 0)
        def _():
            advance(*last, sum_q, sum_o, *upper)

    store(cot, mixed_out.at[0])

    def store_total(each):
        if each is upper[0]:
            store(each.total, qkv_out.at[1, :, : 2 * width])
        elif each is upper[1]:
            store(each.total.at[:, :width], qkv_out.at[1, :, 2 * width :])
            store(each.total.at[:, width:], out_out.at[1])
        elif each is sum_o:
            store(each.total, out_out.at[0])
        elif each is sum_q:
            for kind in range(3):
                columns = pl.ds(kind * width, span_q)
                store(each.total.at[:, kind * span_q : (kind + 1) * span_q], qkv_out.at[0, :, columns])
        else:
            columns = pl.ds(last.index(each) * width + span_q, span_q)
            store(each.total, qkv_out.at[0, :, columns])

    while any(each.done < STEPS for each in sums):
        for each in (*last, sum_q, *upper, sum_o):
            if each.done < STEPS:
                each.step()
                if each.done == STEPS:
                    store_total(each)
        if small.done < 3:
            small.send(small.receive())
        elif small.done == 3:
            g_gain[...] = small.receive()
            store(g_gain.at[0:2], gain_out)
    for copy in stores:
        copy.wait()
    for each in sums:
        each.clear()
    small.clear()

    for kind in range(4):
        held = sent.at[kind, pl.ds(0, balls * (near - 1) * block), :]
        pltpu.make_async_copy(held, held, send_sem.at[kind]).wait()


def finish_kernel(mixed, d_x, gain, qkv, out, mixed_out, points_out, gain_out, qkv_out, out_out, *rest):
    mixed_v, d_x_v, gain_v, qkv_v, out_v, qkv_f, out_f, load_sem, store_sem = rest
    rows = BALL
    moves = [(mixed, mixed_v, mixed_v, mixed_out), (d_x, d_x_v, d_x_v, points_out), (gain, gain_v, gain_v, gain_out)]
    for layer in range(qkv.shape[0]):
        for low in range(0, qkv.shape[1], rows):
            at = (layer, pl.ds(low, rows))
            moves.append((qkv.at[at], qkv_v.at[at], qkv_f.at[at], qkv_out.at[at]))
            moves.append((out.at[at], out_v.at[at], out_f.at[at], out_out.at[at]))
    moves = moves[3:] + moves[:3]
    loads = [pltpu.make_async_copy(m[0], m[1], load_sem.at[i]) for i, m in enumerate(moves)]
    stores = [pltpu.make_async_copy(m[2], m[3], store_sem.at[i]) for i, m in enumerate(moves)]
    for copy in loads:
        copy.start()
    for load, store, (_, held, ready, _) in zip(loads, stores, moves):
        load.wait()
        if held is not ready:
            ready[...] = held[...].astype(F32)
        store.start()
    for copy in stores:
        copy.wait()


def local(points, ball_lists, gains, w_qkv, w_out, cotangent):
    groups = lax.axis_size("seq")
    rows, width = points.shape[1:]
    balls = rows // BALL
    any_place = pl.BlockSpec(memory_space=pl.ANY)

    def saved(keep):
        return [
            pltpu.VMEM((width, rows), BF16),
            pltpu.VMEM((3 * width, rows), BF16),
            pltpu.VMEM((keep, HEADS, BALL, BALL), BF16),
            pltpu.VMEM((width, rows), BF16),
            pltpu.VMEM((keep, HEADS, BALL), F32),
        ]

    token = pltpu.VMEM((rows, width), BF16)

    def sums(columns):
        shapes = [(width, columns), (width, columns), (width // 2, columns), (2, width // 8, columns // 2)]
        shapes += [(2, width // 8, columns), (4, width // 32, columns), (4, width // 32, columns)]
        return [pltpu.VMEM(shape, BF16) for shape in shapes]

    parts = pl.pallas_call(
        kernel,
        out_shape=[
            jax.ShapeDtypeStruct(points.shape, BF16),
            jax.ShapeDtypeStruct(points.shape, BF16),
            jax.ShapeDtypeStruct(gains.shape, F32),
            jax.ShapeDtypeStruct(w_qkv.shape, BF16),
            jax.ShapeDtypeStruct(w_out.shape, BF16),
        ],
        in_specs=[any_place] * 6,
        out_specs=[any_place] * 5,
        scratch_shapes=[
            pltpu.VMEM((1, rows), jnp.int32),
            token,
            token,
            pltpu.VMEM(gains.shape, F32),
            pltpu.VMEM(w_qkv.shape, BF16),
            pltpu.VMEM(w_out.shape, BF16),
            pltpu.VMEM((2, 3 * width, width), BF16),
            pltpu.VMEM((rows, rows), BF16),
            token,
            *saved(balls),
            *saved(1),
            pltpu.VMEM((3 * width, rows), BF16),
            pltpu.VMEM((width, rows), BF16),
            pltpu.VMEM((4, rows, width), BF16),
            pltpu.VMEM((4, rows, width), BF16),
            token,
            pltpu.VMEM((8, width), F32),
            *[box for columns, _ in SUMS for box in sums(columns)],
            pltpu.VMEM((4, 4, 8, width), F32),
            pltpu.SemaphoreType.DMA((8,)),
            pltpu.SemaphoreType.DMA((16,)),
            pltpu.SemaphoreType.DMA((4,)),
            pltpu.SemaphoreType.DMA((4, balls)),
            pltpu.SemaphoreType.DMA((len(SUMS), 3)),
            pltpu.SemaphoreType.DMA((len(SUMS), 9)),
            pltpu.SemaphoreType.DMA((4,)),
            pltpu.SemaphoreType.DMA((4,)),
        ],
        compiler_params=pltpu.CompilerParams(
            vmem_limit_bytes=VMEM_BYTES, collective_id=0, has_side_effects=True
        ),
    )(points, ball_lists, gains, w_qkv, w_out, cotangent)
    results = [*parts[:3], *(jax.ShapeDtypeStruct(part.shape, F32) for part in parts[3:])]
    moves = 3 + 4 * width // BALL
    return pl.pallas_call(
        finish_kernel,
        out_shape=[jax.ShapeDtypeStruct(result.shape, result.dtype) for result in results],
        in_specs=[any_place] * 5,
        out_specs=[any_place] * 5,
        scratch_shapes=[
            *[pltpu.VMEM(part.shape, part.dtype) for part in parts],
            *[pltpu.VMEM(part.shape, F32) for part in parts[3:]],
            pltpu.SemaphoreType.DMA((moves,)),
            pltpu.SemaphoreType.DMA((moves,)),
        ],
        compiler_params=pltpu.CompilerParams(vmem_limit_bytes=VMEM_BYTES),
    )(*parts)


def solution(mesh):
    return jax.shard_map(
        local,
        mesh=mesh,
        in_specs=(P("dp", "seq", None), P("dp", "seq"), P(), P(), P(), P("dp", "seq", None)),
        out_specs=(P("dp", "seq", None), P("dp", "seq", None), P(), P(), P()),
        check_vma=False,
    )
```

```python
import jax
import jax.numpy as jnp
from jax import lax
from jax.experimental import pallas as pl
from jax.experimental.pallas import tpu as pltpu
from jax.sharding import PartitionSpec as P

MESH = pl.DeviceIdType.MESH
HEADS = 8
BALL = 256
EPS = 1e-05
F32 = jnp.float32
BF16 = jnp.bfloat16
VMEM_BYTES = 62 * 1024 * 1024


def dot(a, b, ca, cb):
    return lax.dot_general(a, b, (((ca,), (cb,)), ((), ())), preferred_element_type=F32)


def nn(a, b):
    return dot(a, b, 1, 0)


def nt(a, b):
    return dot(a, b, 1, 1)


def tn(a, b):
    return dot(a, b, 0, 0)


def cols(ball, count=1):
    return pl.ds(pl.multiple_of(ball * BALL, BALL), count * BALL)


def norm_scale(x):
    return lax.rsqrt(jnp.mean(x * x, axis=1, keepdims=True) + EPS)


def one_hot_to_rotated(order_row, first):
    rows = order_row.shape[1]
    lane = 128
    held = jnp.broadcast_to(order_row[:, pl.ds(pl.multiple_of(first, lane), lane)], (lane, lane)).T
    row = lax.broadcasted_iota(jnp.int32, (lane, lane), 1)
    parts = [jnp.where(held == row + low, 1.0, 0.0).astype(BF16) for low in range(0, rows, lane)]
    return jnp.concatenate(parts, axis=1)


def one_hot_to_tree(order_row, first, rows):
    tree = lax.broadcasted_iota(jnp.int32, (rows, order_row.shape[1]), 0) + first
    return jnp.where(order_row[...] == tree, 1.0, 0.0).astype(BF16)


def transpose_by_unit(wqkv, wqkv_t):
    unit = jnp.where(
        lax.broadcasted_iota(jnp.int32, (BALL, BALL), 0) == lax.broadcasted_iota(jnp.int32, (BALL, BALL), 1), 1.0, 0.0
    ).astype(BF16)
    for low in range(0, wqkv.shape[1], BALL):
        wqkv_t[low : low + BALL, :] = nt(unit, wqkv[:, low : low + BALL]).astype(BF16)


def forward_balls(ball, count, keep, x, gain, wqkv_t, h_t, qkv_t, p_t, att_t, inv):
    width = x.shape[1]
    size = width // HEADS
    here = cols(ball, count)
    values = x.astype(F32)
    hidden = (values * norm_scale(values) * gain).astype(BF16)
    hidden_t = hidden.T
    h_t[:, here] = hidden_t
    qkv_t[:, here] = nn(wqkv_t[...], hidden_t).astype(BF16)

    def score(item):
        nth, head = item
        low = head * size
        q = qkv_t[low : low + size, cols(ball + nth)] * size ** (-0.5)
        return tn(qkv_t[width + low : width + low + size, cols(ball + nth)], q)

    def weigh(item, scores):
        nth, head = item
        weights = jnp.exp(scores - jnp.max(scores, axis=0, keepdims=True))
        share = 1.0 / jnp.sum(weights, axis=0, keepdims=True)
        weights = weights.astype(BF16)
        p_t[keep + nth, head] = weights
        inv[keep + nth, head : head + 1, :] = share
        return weights, share

    def mix(item, weights, share):
        nth, head = item
        low = head * size
        v = qkv_t[2 * width + low : 2 * width + low + size, cols(ball + nth)]
        att_t[low : low + size, cols(ball + nth)] = (nn(v, weights) * share).astype(BF16)

    staggered([(nth, head) for nth in range(count) for head in range(HEADS)], score, weigh, mix)


def project(x, att_t, wout):
    return (x.astype(F32) + tn(att_t, wout[...])).astype(BF16)


def staggered(heads, *stages):
    heads = list(heads)
    held = {}
    for step in range(len(heads) + len(stages) - 1):
        for index, stage in enumerate(stages):
            if 0 <= step - index < len(heads):
                head = heads[step - index]
                given = held.pop((head, index), ())
                result = stage(head, *given)
                held[head, index + 1] = result if isinstance(result, tuple) else (result,)


def backward_heads(ball, keep, heads, d_att, qkv_t, p_t, att_t, inv, dqkv_t):
    width = d_att.shape[0]
    size = width // HEADS
    here = cols(ball)

    def weigh(head):
        low = head * size
        v = qkv_t[2 * width + low : 2 * width + low + size, here]
        d_out = d_att[low : low + size, here].astype(F32) * inv[keep, head : head + 1, :]
        delta = jnp.sum(d_out * att_t[low : low + size, here].astype(F32), axis=0, keepdims=True)
        d_out = d_out.astype(BF16)
        return d_out, delta, tn(v, d_out)

    def score(head, d_out, delta, d_weights):
        weights = p_t[keep, head]
        return d_out, weights, (weights.astype(F32) * (d_weights - delta)).astype(BF16)

    def spread(head, d_out, weights, d_scores):
        low = head * size
        q = qkv_t[low : low + size, here] * size ** (-0.5)
        k = qkv_t[width + low : width + low + size, here]
        dqkv_t[low : low + size, here] = (nn(k, d_scores) * size ** (-0.5)).astype(BF16)
        dqkv_t[width + low : width + low + size, here] = nt(q, d_scores).astype(BF16)
        dqkv_t[2 * width + low : 2 * width + low + size, here] = nt(d_out, weights).astype(BF16)

    staggered(heads, weigh, score, spread)


def backward_norm(ball, count, x, gain, dy, wqkv, dqkv_t):
    d_h = nn(wqkv[...], dqkv_t[:, cols(ball, count)]).T
    values = x.astype(F32)
    scale = norm_scale(values)
    unit = values * scale
    d_unit = d_h * gain
    d_n = scale * (d_unit - unit * jnp.mean(d_unit * unit, axis=1, keepdims=True))
    d_x = dy.astype(F32) + d_n.astype(BF16).astype(F32)
    return d_x.astype(BF16), jnp.sum(d_h * unit, axis=0, keepdims=True)


class Place:
    def __init__(self):
        dp, seq = lax.axis_index("dp"), lax.axis_index("seq")
        self.at = {"x": seq // 4, "y": dp // 4 * 2 + seq // 2 % 2, "z": dp % 4, "core": seq % 2}
        sizes = {"x": 4, "y": 4, "z": 4, "core": 2}
        self.peers = {
            axis: [(self.at[axis] + step) % size for step in range(1, size)] for axis, size in sizes.items()
        }
        self.devices = {
            axis: [(peer, self.other(axis, peer)) for peer in peers] for axis, peers in self.peers.items()
        }

    def device(self, axis, peer):
        for known, device in self.devices[axis]:
            if known is peer:
                return device
        return self.other(axis, peer)

    def other(self, axis, value):
        at = {**self.at, axis: value}
        return {"dp": at["y"] // 2 * 4 + at["z"], "seq": at["x"] * 4 + at["y"] % 2 * 2 + at["core"]}


STEPS = 10
HALVES, TURN, PASS, SPREAD, LAST, COLLECT, SHARE, RELAY, BACK = range(9)


class Sum:
    def __init__(self, place, slot, axes, part, total, halves, turns, quarters, pieces, lasts, send_sem, recv_sem):
        self.place, self.slot, self.axes = place, slot, axes
        self.part, self.total = part, total
        self.halves, self.turns, self.quarters, self.pieces, self.lasts = halves, turns, quarters, pieces, lasts
        self.send_sem, self.recv_sem = send_sem, recv_sem
        rows, columns = part.shape
        self.sizes = [rows, rows // 2, rows // 8, rows // 32]
        base, self.bases = 0, [0]
        for size, name in zip(self.sizes[1:], ("core", *axes)):
            base = base + place.at[name] * size
            self.bases.append(base)
        self.right, self.far, self.left = place.peers[axes[0]]
        self.sides = (pl.ds(0, columns // 2), pl.ds(columns // 2, columns // 2))
        self.done = 0

    def span(self, level, coordinate=None):
        base = self.bases[level] if coordinate is None else self.bases[level - 1] + coordinate * self.sizes[level]
        return pl.ds(pl.multiple_of(base, 16), self.sizes[level])

    def copy(self, source, target, send, recv, axis, peer):
        return pltpu.make_async_remote_copy(
            src_ref=source,
            dst_ref=target,
            send_sem=self.send_sem.at[self.slot, send],
            recv_sem=self.recv_sem.at[self.slot, recv],
            device_id=self.place.device(axis, peer),
            device_id_type=MESH,
        )

    def partner(self, kind):
        peer = self.place.peers["core"][0]
        if kind == HALVES:
            return self.copy(self.part.at[self.span(1, peer), :], self.halves, 0, kind, "core", peer)
        rows = self.total.at[self.span(1), :]
        return self.copy(rows, rows, 0, kind, "core", peer)

    def around(self, kind, way):
        peer = (self.right, self.left)[way]
        other = (self.left, self.right)[way]
        side = self.sides[way]
        if kind == TURN:
            source, target = self.part.at[self.span(2, self.far), side], self.turns.at[way]
        elif kind == PASS:
            source, target = self.part.at[self.span(2, peer), :], self.quarters.at[way]
        elif kind == SHARE:
            source = target = self.total.at[self.span(2), :]
        else:
            source = target = self.total.at[self.span(2, other), side]
        return self.copy(source, target, 1, kind, self.axes[0], peer)

    def along(self, kind, here, there):
        axis = self.axes[2] if kind == LAST else self.axes[1]
        if kind == SPREAD:
            source, target = self.part.at[self.span(3, there), :], self.pieces.at[here]
        elif kind == LAST:
            source = target = self.lasts.at[here]
        else:
            source = target = self.total.at[self.span(3, here), :]
        return self.copy(source, target, 2, kind, axis, there)

    def start_around(self, kind):
        for way in range(2):
            self.around(kind, way).start()

    def start_along(self, kind):
        axis = self.axes[2] if kind == LAST else self.axes[1]
        for peer in self.place.peers[axis]:
            self.along(kind, self.place.at[axis], peer).start()

    def arrive(self, kind):
        rows = self.part.shape[0]
        eighth, last = rows // 8, rows // 32
        held = {
            HALVES: self.halves,
            TURN: self.turns,
            PASS: self.quarters,
            SPREAD: self.pieces.at[pl.ds(0, 3)],
            LAST: self.lasts.at[pl.ds(0, 3)],
            COLLECT: self.total.at[pl.ds(0, 3 * last), :],
            SHARE: self.total.at[pl.ds(0, 2 * eighth), :],
            RELAY: self.total.at[pl.ds(0, eighth), :],
            BACK: self.total.at[pl.ds(0, rows // 2), :],
        }[kind]
        pltpu.make_async_copy(held, held, self.recv_sem.at[self.slot, kind]).wait()

    def add(self, rows, side, *arrived):
        value = self.part[rows, side].astype(F32)
        for each in arrived:
            value += each.astype(F32)
        return value.astype(BF16)

    def step(self):
        step, self.done = self.done, self.done + 1
        everything = pl.ds(0, self.part.shape[1])
        if step == 0:
            self.partner(HALVES).start()
        elif step == 1:
            self.arrive(HALVES)
            self.part[self.span(1), :] = self.add(self.span(1), everything, self.halves[...])
            self.start_around(TURN)
        elif step == 2:
            self.arrive(TURN)
            for way, peer in enumerate((self.right, self.left)):
                rows, side = self.span(2, peer), self.sides[way]
                self.part[rows, side] = self.add(rows, side, self.turns[way])
            self.start_around(PASS)
        elif step == 3:
            self.arrive(PASS)
            self.part[self.span(2), :] = self.add(self.span(2), everything, self.quarters[0], self.quarters[1])
            self.start_along(SPREAD)
        elif step == 4:
            self.arrive(SPREAD)
            mine = self.place.at[self.axes[2]]
            peers = self.place.peers[self.axes[1]]
            self.lasts[mine] = self.add(self.span(3), everything, *[self.pieces[peer] for peer in peers])
            self.start_along(LAST)
        elif step == 5:
            self.arrive(LAST)
            value = self.lasts[0].astype(F32)
            for peer in range(1, 4):
                value += self.lasts[peer].astype(F32)
            self.total[self.span(3), :] = value.astype(BF16)
            self.start_along(COLLECT)
        elif step == 6:
            self.arrive(COLLECT)
            self.start_around(SHARE)
        elif step == 7:
            self.arrive(SHARE)
            self.start_around(RELAY)
        elif step == 8:
            self.arrive(RELAY)
            self.partner(BACK).start()
        elif step == 9:
            self.arrive(BACK)

    def clear(self):
        rows = self.part.shape[0]
        for index, sent in enumerate((rows, 6 * rows // 8, 9 * rows // 32)):
            held = self.part.at[pl.ds(0, sent), :]
            pltpu.make_async_copy(held, held, self.send_sem.at[self.slot, index]).wait()


class SmallSum:
    axes = ("core", "x", "y", "z")

    def __init__(self, place, boxes, send_sem, recv_sem):
        self.place, self.boxes, self.send_sem, self.recv_sem = place, boxes, send_sem, recv_sem
        self.done = 0

    def hop(self, step, here, there):
        box = self.boxes.at[step, here]
        return pltpu.make_async_remote_copy(
            src_ref=box,
            dst_ref=box,
            send_sem=self.send_sem.at[step],
            recv_sem=self.recv_sem.at[step],
            device_id=self.place.device(self.axes[step], there),
            device_id_type=MESH,
        )

    def send(self, value):
        axis = self.axes[self.done]
        mine = self.place.at[axis]
        self.boxes[self.done, mine] = value
        for peer in self.place.peers[axis]:
            self.hop(self.done, mine, peer).start()

    def receive(self):
        axis = self.axes[self.done]
        self.wait(self.done, self.recv_sem)
        value = self.boxes[self.done, 0]
        for peer in range(1, len(self.place.peers[axis]) + 1):
            value += self.boxes[self.done, peer]
        self.done += 1
        return value

    def wait(self, step, sem):
        held = self.boxes.at[step, pl.ds(0, len(self.place.peers[self.axes[step]]))]
        pltpu.make_async_copy(held, held, sem.at[step]).wait()

    def clear(self):
        for step in range(len(self.axes)):
            self.wait(step, self.send_sem)


TO_X, TO_COT, BACK_R, BACK_D = range(4)
GROUPS = 2
PAIR = 2
SUMS = (
    (768, ("x", "z", "y")),
    (768, ("z", "x", "y")),
    (1024, ("x", "z", "y")),
    (768, ("z", "x", "y")),
    (256, ("x", "y", "z")),
    (256, ("z", "y", "x")),
    (256, ("y", "x", "z")),
)


def kernel(
    points, lists, gains, w_qkv, w_out, cotangent,
    mixed_out, points_out, gain_out, qkv_out, out_out,
    order, x, cot, gain, wqkv, wout, wqkv_t, onto, y,
    h0, qkv0, p0, att0, inv0, h1, qkv1, p1, att1, inv1, dqkv, d_att,
    sent, got, d_x, g_gain, *rest,
):
    sum_boxes, rest = rest[: 7 * len(SUMS)], rest[7 * len(SUMS) :]
    boxes, load_sem, store_sem, send_sem, recv_sem, sum_send, sum_recv, small_send, small_recv = rest
    groups = lax.axis_size("seq")
    me = lax.axis_index("seq")
    rows = x.shape[0]
    block = rows // groups
    balls = rows // BALL
    near = groups // balls
    home = me // near
    seat = me % near
    place = Place()
    sums = [
        Sum(place, slot, axes, *sum_boxes[7 * slot : 7 * slot + 7], sum_send, sum_recv)
        for slot, (columns, axes) in enumerate(SUMS)
    ]
    upper, sum_o, sum_q, last = sums[0:2], sums[2], sums[3], sums[4:7]
    small = SmallSum(place, boxes, small_send, small_recv)

    loads = []

    def load(source, target):
        copy = pltpu.make_async_copy(source, target, load_sem.at[len(loads)])
        copy.start()
        loads.append(copy)
        return copy

    lists_in = load(lists, order)
    cot_in = load(cotangent.at[0], cot)
    x_in = load(points.at[0], x)
    small_in = [load(gains, gain), load(w_qkv.at[0], wqkv.at[0]), load(w_out.at[0], wout.at[0])]
    late_in = [load(w_qkv.at[1], wqkv.at[1]), load(w_out.at[1], wout.at[1])]

    barrier = pltpu.get_barrier_semaphore()
    for step in range(1, near):
        pl.semaphore_signal(
            barrier, inc=1, device_id={"seq": home * near + (seat + step) % near}, device_id_type=MESH
        )
    for axis in ("x", "z"):
        for peer in place.peers[axis]:
            pl.semaphore_signal(barrier, inc=1, device_id=place.other(axis, peer), device_id_type=MESH)
    for step in range(2):
        far = (place.at["y"] // 2 * 2 + 2 + step) % 4
        pl.semaphore_signal(barrier, inc=1, device_id=place.other("y", far), device_id_type=MESH)

    def span(index):
        return pl.ds(pl.multiple_of(index * block, block), block)

    others = [(seat + step) % near for step in range(1, near)]

    def transfer(kind, ball, here, there):
        return pltpu.make_async_remote_copy(
            src_ref=sent.at[kind, span(ball * near + there), :],
            dst_ref=got.at[kind, span(ball * near + here), :],
            send_sem=send_sem.at[kind],
            recv_sem=recv_sem.at[kind, ball],
            device_id={"seq": home * near + there},
            device_id_type=MESH,
        )

    def send(kind, ball):
        for peer in others:
            transfer(kind, ball, seat, peer).start()
        own = span(ball * near + seat)
        got[kind, own, :] = sent[kind, own, :]

    def arrive(kind, ball):
        held = got.at[kind, pl.ds(0, (near - 1) * block), :]
        pltpu.make_async_copy(held, held, recv_sem.at[kind, ball]).wait()

    def gather(kind, source, ball):
        sent[kind, cols(ball, PAIR), :] = nn(onto[cols(ball, PAIR), :], source[...]).astype(BF16)

    lists_in.wait()

    @pl.loop(0, rows // 128)
    def _(part):
        first = pl.multiple_of(part * 128, 128)
        onto[pl.ds(first, 128), :] = one_hot_to_rotated(order, first)

    cot_in.wait()
    pl.semaphore_wait(barrier, near - 1 + 8)

    @pl.loop(0, balls, step=PAIR)
    def _(ball):
        gather(TO_COT, cot, ball)
        for nth in range(PAIR):
            send(TO_COT, ball + nth)

    x_in.wait()
    for copy in small_in:
        copy.wait()
    transpose_by_unit(wqkv.at[0], wqkv_t.at[0])

    @pl.loop(0, balls, step=PAIR)
    def _(ball):
        here = cols(ball, PAIR)
        forward_balls(ball, PAIR, ball, x[here, :], gain[0:1], wqkv_t.at[0], h0, qkv0, p0, att0, inv0)
        y[here, :] = project(x[here, :], att0[:, here], wout.at[0])

    @pl.loop(0, balls, step=PAIR)
    def _(ball):
        gather(TO_X, y, ball)
        for nth in range(PAIR):
            send(TO_X, ball + nth)

    for copy in late_in:
        copy.wait()
    transpose_by_unit(wqkv.at[1], wqkv_t.at[1])
    g_gain[...] = jnp.zeros_like(g_gain)

    @pl.loop(0, balls)
    def _(ball):
        arrive(TO_X, ball)
        forward_balls(
            ball, 1, 0, got[TO_X, cols(ball), :], gain[1:2], wqkv_t.at[1], h1, qkv1, p1, att1, inv1
        )
        arrive(TO_COT, ball)
        d_r = got[TO_COT, cols(ball), :]
        d_att[:, cols(ball)] = nt(wout[1], d_r).astype(BF16)
        backward_heads(ball, 0, range(HEADS), d_att, qkv1, p1, att1, inv1, dqkv)
        sent[BACK_D, cols(ball), :], gained = backward_norm(
            ball, 1, got[TO_X, cols(ball), :], gain[1:2], d_r, wqkv.at[1], dqkv
        )
        send(BACK_D, ball)
        g_gain[1:2] += gained

    stores = []

    def store(source, target):
        copy = pltpu.make_async_copy(source, target, store_sem.at[len(stores)])
        copy.start()
        stores.append(copy)
        return copy

    width = x.shape[1]
    def advance(*which):
        for each in which:
            each.step()

    half = 3 * width // 2
    for nth, each in enumerate(upper):
        each.part[...] = nt(h1[...], dqkv[nth * half : (nth + 1) * half, :]).astype(BF16)
        advance(each)

    @pl.loop(0, balls, step=PAIR)
    def _(ball):
        here = cols(ball, PAIR)
        sent[BACK_R, here, :] = project(got[TO_X, here, :], att1[:, here], wout.at[1])
        for nth in range(PAIR):
            send(BACK_R, ball + nth)

    sum_o.part[:, width:] = nn(att1[...], got[TO_COT]).astype(BF16)

    @pl.loop(0, balls)
    def _(ball):
        arrive(BACK_D, ball)

    @pl.loop(0, balls, step=PAIR)
    def _(ball):
        here = cols(ball, PAIR)
        y[here, :] = nn(one_hot_to_tree(order, ball * BALL, PAIR * BALL), got[BACK_D]).astype(BF16)
        d_att[:, here] = nt(wout[0], y[here, :]).astype(BF16)

        @pl.when(ball == 0)
        def _():
            advance(*upper)

    sum_o.part[:, :width] = nn(att0[...], y[...]).astype(BF16)
    advance(sum_o)
    span_q = width // GROUPS
    heads = HEADS // GROUPS
    for group in range(GROUPS):

        @pl.loop(0, balls)
        def _(ball):
            backward_heads(
                ball, ball, range(group * heads, (group + 1) * heads), d_att, qkv0, p0, att0, inv0, dqkv
            )

            @pl.when(ball == 2)
            def _():
                advance(sum_o)

        for kind in range(3):
            low = kind * width + group * span_q
            g = nt(h0[...], dqkv[low : low + span_q, :]).astype(BF16)
            if group == 0:
                sum_q.part[:, kind * span_q : (kind + 1) * span_q] = g
            else:
                last[kind].part[...] = g
                advance(last[kind])
        advance(*upper, sum_q)

    @pl.loop(0, balls, step=PAIR)
    def _(ball):
        here = cols(ball, PAIR)
        d_x[here, :], gained = backward_norm(
            ball, PAIR, x[here, :], gain[0:1], y[here, :], wqkv.at[0], dqkv
        )
        g_gain[0:1] += gained

        @pl.when(ball == 0)
        def _():
            advance(*last, sum_q, sum_o)

    small.send(g_gain[...])
    advance(*last, sum_q, *upper, sum_o)
    store(d_x, points_out.at[0])

    @pl.loop(0, balls)
    def _(ball):
        arrive(BACK_R, ball)

    @pl.loop(0, balls, step=PAIR)
    def _(ball):
        here = cols(ball, PAIR)
        cot[here, :] = nn(one_hot_to_tree(order, ball * BALL, PAIR * BALL), got[BACK_R]).astype(BF16)

        @pl.when(ball == 0)
        def _():
            advance(*last, sum_q, sum_o, *upper)

    store(cot, mixed_out.at[0])

    def store_total(each):
        if each in upper:
            store(each.total, qkv_out.at[1, :, pl.ds(upper.index(each) * half, half)])
        elif each is sum_o:
            store(each.total.at[:, :width], out_out.at[0])
            store(each.total.at[:, width:], out_out.at[1])
        elif each is sum_q:
            for kind in range(3):
                columns = pl.ds(kind * width, span_q)
                store(each.total.at[:, kind * span_q : (kind + 1) * span_q], qkv_out.at[0, :, columns])
        else:
            columns = pl.ds(last.index(each) * width + span_q, span_q)
            store(each.total, qkv_out.at[0, :, columns])

    while any(each.done < STEPS for each in sums):
        for each in (*last, sum_q, *upper, sum_o):
            if each.done < STEPS:
                each.step()
                if each.done == STEPS:
                    store_total(each)
        if small.done < 3:
            small.send(small.receive())
        elif small.done == 3:
            g_gain[...] = small.receive()
            store(g_gain.at[0:2], gain_out)
    for copy in stores:
        copy.wait()
    for each in sums:
        each.clear()
    small.clear()

    for kind in range(4):
        held = sent.at[kind, pl.ds(0, balls * (near - 1) * block), :]
        pltpu.make_async_copy(held, held, send_sem.at[kind]).wait()


def finish_kernel(mixed, d_x, gain, qkv, out, mixed_out, points_out, gain_out, qkv_out, out_out, *rest):
    mixed_v, d_x_v, gain_v, qkv_v, out_v, qkv_f, out_f, load_sem, store_sem = rest
    rows = BALL
    moves = [(mixed, mixed_v, mixed_v, mixed_out), (d_x, d_x_v, d_x_v, points_out), (gain, gain_v, gain_v, gain_out)]
    for layer in range(qkv.shape[0]):
        for low in range(0, qkv.shape[1], rows):
            at = (layer, pl.ds(low, rows))
            moves.append((qkv.at[at], qkv_v.at[at], qkv_f.at[at], qkv_out.at[at]))
            moves.append((out.at[at], out_v.at[at], out_f.at[at], out_out.at[at]))
    moves = moves[3:] + moves[:3]
    loads = [pltpu.make_async_copy(m[0], m[1], load_sem.at[i]) for i, m in enumerate(moves)]
    stores = [pltpu.make_async_copy(m[2], m[3], store_sem.at[i]) for i, m in enumerate(moves)]
    for copy in loads:
        copy.start()
    for load, store, (_, held, ready, _) in zip(loads, stores, moves):
        load.wait()
        if held is not ready:
            ready[...] = held[...].astype(F32)
        store.start()
    for copy in stores:
        copy.wait()


def local(points, ball_lists, gains, w_qkv, w_out, cotangent):
    groups = lax.axis_size("seq")
    rows, width = points.shape[1:]
    balls = rows // BALL
    any_place = pl.BlockSpec(memory_space=pl.ANY)

    def saved(keep):
        return [
            pltpu.VMEM((width, rows), BF16),
            pltpu.VMEM((3 * width, rows), BF16),
            pltpu.VMEM((keep, HEADS, BALL, BALL), BF16),
            pltpu.VMEM((width, rows), BF16),
            pltpu.VMEM((keep, HEADS, BALL), F32),
        ]

    token = pltpu.VMEM((rows, width), BF16)

    def sums(columns):
        shapes = [(width, columns), (width, columns), (width // 2, columns), (2, width // 8, columns // 2)]
        shapes += [(2, width // 8, columns), (4, width // 32, columns), (4, width // 32, columns)]
        return [pltpu.VMEM(shape, BF16) for shape in shapes]

    parts = pl.pallas_call(
        kernel,
        out_shape=[
            jax.ShapeDtypeStruct(points.shape, BF16),
            jax.ShapeDtypeStruct(points.shape, BF16),
            jax.ShapeDtypeStruct(gains.shape, F32),
            jax.ShapeDtypeStruct(w_qkv.shape, BF16),
            jax.ShapeDtypeStruct(w_out.shape, BF16),
        ],
        in_specs=[any_place] * 6,
        out_specs=[any_place] * 5,
        scratch_shapes=[
            pltpu.VMEM((1, rows), jnp.int32),
            token,
            token,
            pltpu.VMEM(gains.shape, F32),
            pltpu.VMEM(w_qkv.shape, BF16),
            pltpu.VMEM(w_out.shape, BF16),
            pltpu.VMEM((2, 3 * width, width), BF16),
            pltpu.VMEM((rows, rows), BF16),
            token,
            *saved(balls),
            *saved(1),
            pltpu.VMEM((3 * width, rows), BF16),
            pltpu.VMEM((width, rows), BF16),
            pltpu.VMEM((4, rows, width), BF16),
            pltpu.VMEM((4, rows, width), BF16),
            token,
            pltpu.VMEM((8, width), F32),
            *[box for columns, _ in SUMS for box in sums(columns)],
            pltpu.VMEM((4, 4, 8, width), F32),
            pltpu.SemaphoreType.DMA((8,)),
            pltpu.SemaphoreType.DMA((16,)),
            pltpu.SemaphoreType.DMA((4,)),
            pltpu.SemaphoreType.DMA((4, balls)),
            pltpu.SemaphoreType.DMA((len(SUMS), 3)),
            pltpu.SemaphoreType.DMA((len(SUMS), 9)),
            pltpu.SemaphoreType.DMA((4,)),
            pltpu.SemaphoreType.DMA((4,)),
        ],
        compiler_params=pltpu.CompilerParams(
            vmem_limit_bytes=VMEM_BYTES, collective_id=0, has_side_effects=True
        ),
    )(points, ball_lists, gains, w_qkv, w_out, cotangent)
    results = [*parts[:3], *(jax.ShapeDtypeStruct(part.shape, F32) for part in parts[3:])]
    moves = 3 + 4 * width // BALL
    return pl.pallas_call(
        finish_kernel,
        out_shape=[jax.ShapeDtypeStruct(result.shape, result.dtype) for result in results],
        in_specs=[any_place] * 5,
        out_specs=[any_place] * 5,
        scratch_shapes=[
            *[pltpu.VMEM(part.shape, part.dtype) for part in parts],
            *[pltpu.VMEM(part.shape, F32) for part in parts[3:]],
            pltpu.SemaphoreType.DMA((moves,)),
            pltpu.SemaphoreType.DMA((moves,)),
        ],
        compiler_params=pltpu.CompilerParams(vmem_limit_bytes=VMEM_BYTES),
    )(*parts)


def solution(mesh):
    return jax.shard_map(
        local,
        mesh=mesh,
        in_specs=(P("dp", "seq", None), P("dp", "seq"), P(), P(), P(), P("dp", "seq", None)),
        out_specs=(P("dp", "seq", None), P("dp", "seq", None), P(), P(), P()),
        check_vma=False,
    )
```

```python
import jax
import jax.numpy as jnp
from jax import lax
from jax.experimental import pallas as pl
from jax.experimental.pallas import tpu as pltpu
from jax.sharding import PartitionSpec as P

MESH = pl.DeviceIdType.MESH
HEADS = 8
BALL = 256
EPS = 1e-05
F32 = jnp.float32
BF16 = jnp.bfloat16
VMEM_BYTES = 62 * 1024 * 1024


def dot(a, b, ca, cb):
    return lax.dot_general(a, b, (((ca,), (cb,)), ((), ())), preferred_element_type=F32)


def nn(a, b):
    return dot(a, b, 1, 0)


def nt(a, b):
    return dot(a, b, 1, 1)


def tn(a, b):
    return dot(a, b, 0, 0)


def cols(ball, count=1):
    return pl.ds(pl.multiple_of(ball * BALL, BALL), count * BALL)


def norm_scale(x):
    return lax.rsqrt(jnp.mean(x * x, axis=1, keepdims=True) + EPS)


def one_hot_to_rotated(order_row, first):
    rows = order_row.shape[1]
    lane = 128
    held = jnp.broadcast_to(order_row[:, pl.ds(pl.multiple_of(first, lane), lane)], (lane, lane)).T
    row = lax.broadcasted_iota(jnp.int32, (lane, lane), 1)
    parts = [jnp.where(held == row + low, 1.0, 0.0).astype(BF16) for low in range(0, rows, lane)]
    return jnp.concatenate(parts, axis=1)


def one_hot_to_tree(order_row, first, rows):
    tree = lax.broadcasted_iota(jnp.int32, (rows, order_row.shape[1]), 0) + first
    return jnp.where(order_row[...] == tree, 1.0, 0.0).astype(BF16)


def transpose_by_unit(wqkv, wqkv_t):
    unit = jnp.where(
        lax.broadcasted_iota(jnp.int32, (BALL, BALL), 0) == lax.broadcasted_iota(jnp.int32, (BALL, BALL), 1), 1.0, 0.0
    ).astype(BF16)
    for low in range(0, wqkv.shape[1], BALL):
        wqkv_t[low : low + BALL, :] = nt(unit, wqkv[:, low : low + BALL]).astype(BF16)


def forward_balls(ball, count, keep, x, gain, wqkv_t, h_t, qkv_t, p_t, att_t, inv):
    width = x.shape[1]
    size = width // HEADS
    here = cols(ball, count)
    values = x.astype(F32)
    hidden = (values * norm_scale(values) * gain).astype(BF16)
    hidden_t = hidden.T
    h_t[:, here] = hidden_t
    qkv_t[:, here] = nn(wqkv_t[...], hidden_t).astype(BF16)

    def score(item):
        nth, head = item
        low = head * size
        q = qkv_t[low : low + size, cols(ball + nth)] * size ** (-0.5)
        return tn(qkv_t[width + low : width + low + size, cols(ball + nth)], q)

    def weigh(item, scores):
        nth, head = item
        weights = jnp.exp(scores - jnp.max(scores, axis=0, keepdims=True))
        share = 1.0 / jnp.sum(weights, axis=0, keepdims=True)
        weights = weights.astype(BF16)
        p_t[keep + nth, head] = weights
        inv[keep + nth, head : head + 1, :] = share
        return weights, share

    def mix(item, weights, share):
        nth, head = item
        low = head * size
        v = qkv_t[2 * width + low : 2 * width + low + size, cols(ball + nth)]
        att_t[low : low + size, cols(ball + nth)] = (nn(v, weights) * share).astype(BF16)

    staggered([(nth, head) for nth in range(count) for head in range(HEADS)], score, weigh, mix)


def project(x, att_t, wout):
    return (x.astype(F32) + tn(att_t, wout[...])).astype(BF16)


def staggered(heads, *stages):
    heads = list(heads)
    held = {}
    for step in range(len(heads) + len(stages) - 1):
        for index, stage in enumerate(stages):
            if 0 <= step - index < len(heads):
                head = heads[step - index]
                given = held.pop((head, index), ())
                result = stage(head, *given)
                held[head, index + 1] = result if isinstance(result, tuple) else (result,)


def backward_heads(ball, keep, heads, d_att, qkv_t, p_t, att_t, inv, dqkv_t):
    width = d_att.shape[0]
    size = width // HEADS
    here = cols(ball)

    def weigh(head):
        low = head * size
        v = qkv_t[2 * width + low : 2 * width + low + size, here]
        d_out = d_att[low : low + size, here].astype(F32) * inv[keep, head : head + 1, :]
        delta = jnp.sum(d_out * att_t[low : low + size, here].astype(F32), axis=0, keepdims=True)
        d_out = d_out.astype(BF16)
        return d_out, delta, tn(v, d_out)

    def score(head, d_out, delta, d_weights):
        weights = p_t[keep, head]
        return d_out, weights, (weights.astype(F32) * (d_weights - delta)).astype(BF16)

    def spread(head, d_out, weights, d_scores):
        low = head * size
        q = qkv_t[low : low + size, here] * size ** (-0.5)
        k = qkv_t[width + low : width + low + size, here]
        dqkv_t[low : low + size, here] = (nn(k, d_scores) * size ** (-0.5)).astype(BF16)
        dqkv_t[width + low : width + low + size, here] = nt(q, d_scores).astype(BF16)
        dqkv_t[2 * width + low : 2 * width + low + size, here] = nt(d_out, weights).astype(BF16)

    staggered(heads, weigh, score, spread)


def backward_norm(ball, count, x, gain, dy, wqkv, dqkv_t):
    d_h = nn(wqkv[...], dqkv_t[:, cols(ball, count)]).T
    values = x.astype(F32)
    scale = norm_scale(values)
    unit = values * scale
    d_unit = d_h * gain
    d_n = scale * (d_unit - unit * jnp.mean(d_unit * unit, axis=1, keepdims=True))
    d_x = dy.astype(F32) + d_n.astype(BF16).astype(F32)
    return d_x.astype(BF16), jnp.sum(d_h * unit, axis=0, keepdims=True)


class Place:
    def __init__(self):
        dp, seq = lax.axis_index("dp"), lax.axis_index("seq")
        self.at = {"x": seq // 4, "y": dp // 4 * 2 + seq // 2 % 2, "z": dp % 4, "core": seq % 2}
        sizes = {"x": 4, "y": 4, "z": 4, "core": 2}
        self.peers = {
            axis: [(self.at[axis] + step) % size for step in range(1, size)] for axis, size in sizes.items()
        }
        self.devices = {
            axis: [(peer, self.other(axis, peer)) for peer in peers] for axis, peers in self.peers.items()
        }

    def device(self, axis, peer):
        for known, device in self.devices[axis]:
            if known is peer:
                return device
        return self.other(axis, peer)

    def other(self, axis, value):
        at = {**self.at, axis: value}
        return {"dp": at["y"] // 2 * 4 + at["z"], "seq": at["x"] * 4 + at["y"] % 2 * 2 + at["core"]}


STEPS = 10
HALVES, TURN, PASS, SPREAD, LAST, COLLECT, SHARE, RELAY, BACK = range(9)


class Sum:
    def __init__(self, place, slot, axes, part, total, halves, turns, quarters, pieces, lasts, send_sem, recv_sem):
        self.place, self.slot, self.axes = place, slot, axes
        self.part, self.total = part, total
        self.halves, self.turns, self.quarters, self.pieces, self.lasts = halves, turns, quarters, pieces, lasts
        self.send_sem, self.recv_sem = send_sem, recv_sem
        rows, columns = part.shape
        self.sizes = [rows, rows // 2, rows // 8, rows // 32]
        base, self.bases = 0, [0]
        for size, name in zip(self.sizes[1:], ("core", *axes)):
            base = base + place.at[name] * size
            self.bases.append(base)
        self.right, self.far, self.left = place.peers[axes[0]]
        self.sides = (pl.ds(0, columns // 2), pl.ds(columns // 2, columns // 2))
        self.done = 0

    def span(self, level, coordinate=None):
        base = self.bases[level] if coordinate is None else self.bases[level - 1] + coordinate * self.sizes[level]
        return pl.ds(pl.multiple_of(base, 16), self.sizes[level])

    def copy(self, source, target, send, recv, axis, peer):
        return pltpu.make_async_remote_copy(
            src_ref=source,
            dst_ref=target,
            send_sem=self.send_sem.at[self.slot, send],
            recv_sem=self.recv_sem.at[self.slot, recv],
            device_id=self.place.device(axis, peer),
            device_id_type=MESH,
        )

    def partner(self, kind):
        peer = self.place.peers["core"][0]
        if kind == HALVES:
            return self.copy(self.part.at[self.span(1, peer), :], self.halves, 0, kind, "core", peer)
        rows = self.total.at[self.span(1), :]
        return self.copy(rows, rows, 0, kind, "core", peer)

    def around(self, kind, way):
        peer = (self.right, self.left)[way]
        other = (self.left, self.right)[way]
        side = self.sides[way]
        if kind == TURN:
            source, target = self.part.at[self.span(2, self.far), side], self.turns.at[way]
        elif kind == PASS:
            source, target = self.part.at[self.span(2, peer), :], self.quarters.at[way]
        elif kind == SHARE:
            source = target = self.total.at[self.span(2), :]
        else:
            source = target = self.total.at[self.span(2, other), side]
        return self.copy(source, target, 1, kind, self.axes[0], peer)

    def along(self, kind, here, there):
        axis = self.axes[2] if kind == LAST else self.axes[1]
        if kind == SPREAD:
            source, target = self.part.at[self.span(3, there), :], self.pieces.at[here]
        elif kind == LAST:
            source = target = self.lasts.at[here]
        else:
            source = target = self.total.at[self.span(3, here), :]
        return self.copy(source, target, 2, kind, axis, there)

    def start_around(self, kind):
        for way in range(2):
            self.around(kind, way).start()

    def start_along(self, kind):
        axis = self.axes[2] if kind == LAST else self.axes[1]
        for peer in self.place.peers[axis]:
            self.along(kind, self.place.at[axis], peer).start()

    def arrive(self, kind):
        rows = self.part.shape[0]
        eighth, last = rows // 8, rows // 32
        held = {
            HALVES: self.halves,
            TURN: self.turns,
            PASS: self.quarters,
            SPREAD: self.pieces.at[pl.ds(0, 3)],
            LAST: self.lasts.at[pl.ds(0, 3)],
            COLLECT: self.total.at[pl.ds(0, 3 * last), :],
            SHARE: self.total.at[pl.ds(0, 2 * eighth), :],
            RELAY: self.total.at[pl.ds(0, eighth), :],
            BACK: self.total.at[pl.ds(0, rows // 2), :],
        }[kind]
        pltpu.make_async_copy(held, held, self.recv_sem.at[self.slot, kind]).wait()

    def add(self, rows, side, *arrived):
        value = self.part[rows, side].astype(F32)
        for each in arrived:
            value += each.astype(F32)
        return value.astype(BF16)

    def step(self):
        step, self.done = self.done, self.done + 1
        everything = pl.ds(0, self.part.shape[1])
        if step == 0:
            self.partner(HALVES).start()
        elif step == 1:
            self.arrive(HALVES)
            self.part[self.span(1), :] = self.add(self.span(1), everything, self.halves[...])
            self.start_around(TURN)
        elif step == 2:
            self.arrive(TURN)
            for way, peer in enumerate((self.right, self.left)):
                rows, side = self.span(2, peer), self.sides[way]
                self.part[rows, side] = self.add(rows, side, self.turns[way])
            self.start_around(PASS)
        elif step == 3:
            self.arrive(PASS)
            self.part[self.span(2), :] = self.add(self.span(2), everything, self.quarters[0], self.quarters[1])
            self.start_along(SPREAD)
        elif step == 4:
            self.arrive(SPREAD)
            mine = self.place.at[self.axes[2]]
            peers = self.place.peers[self.axes[1]]
            self.lasts[mine] = self.add(self.span(3), everything, *[self.pieces[peer] for peer in peers])
            self.start_along(LAST)
        elif step == 5:
            self.arrive(LAST)
            value = self.lasts[0].astype(F32)
            for peer in range(1, 4):
                value += self.lasts[peer].astype(F32)
            self.total[self.span(3), :] = value.astype(BF16)
            self.start_along(COLLECT)
        elif step == 6:
            self.arrive(COLLECT)
            self.start_around(SHARE)
        elif step == 7:
            self.arrive(SHARE)
            self.start_around(RELAY)
        elif step == 8:
            self.arrive(RELAY)
            self.partner(BACK).start()
        elif step == 9:
            self.arrive(BACK)

    def clear(self):
        rows = self.part.shape[0]
        for index, sent in enumerate((rows, 6 * rows // 8, 9 * rows // 32)):
            held = self.part.at[pl.ds(0, sent), :]
            pltpu.make_async_copy(held, held, self.send_sem.at[self.slot, index]).wait()


class SmallSum:
    axes = ("core", "x", "y", "z")

    def __init__(self, place, boxes, send_sem, recv_sem):
        self.place, self.boxes, self.send_sem, self.recv_sem = place, boxes, send_sem, recv_sem
        self.done = 0

    def hop(self, step, here, there):
        box = self.boxes.at[step, here]
        return pltpu.make_async_remote_copy(
            src_ref=box,
            dst_ref=box,
            send_sem=self.send_sem.at[step],
            recv_sem=self.recv_sem.at[step],
            device_id=self.place.device(self.axes[step], there),
            device_id_type=MESH,
        )

    def send(self, value):
        axis = self.axes[self.done]
        mine = self.place.at[axis]
        self.boxes[self.done, mine] = value
        for peer in self.place.peers[axis]:
            self.hop(self.done, mine, peer).start()

    def receive(self):
        axis = self.axes[self.done]
        self.wait(self.done, self.recv_sem)
        value = self.boxes[self.done, 0]
        for peer in range(1, len(self.place.peers[axis]) + 1):
            value += self.boxes[self.done, peer]
        self.done += 1
        return value

    def wait(self, step, sem):
        held = self.boxes.at[step, pl.ds(0, len(self.place.peers[self.axes[step]]))]
        pltpu.make_async_copy(held, held, sem.at[step]).wait()

    def clear(self):
        for step in range(len(self.axes)):
            self.wait(step, self.send_sem)


TO_X, TO_COT, BACK_R, BACK_D = range(4)
GROUPS = 2
PAIR = 2
MIXED_TURNS = (3, 4)
SUMS = (
    (768, ("x", "z", "y")),
    (768, ("z", "x", "y")),
    (1024, ("x", "z", "y")),
    (768, ("z", "x", "y")),
    (256, ("x", "y", "z")),
    (256, ("z", "y", "x")),
    (256, ("y", "x", "z")),
)


def kernel(
    points, lists, gains, w_qkv, w_out, cotangent,
    mixed_out, points_out, gain_out, qkv_out, out_out,
    order, x, cot, gain, wqkv, wout, wqkv_t, onto, y,
    h0, qkv0, p0, att0, inv0, h1, qkv1, p1, att1, inv1, dqkv, d_att,
    sent, got, d_x, g_gain, *rest,
):
    sum_boxes, rest = rest[: 7 * len(SUMS)], rest[7 * len(SUMS) :]
    boxes, load_sem, store_sem, send_sem, recv_sem, sum_send, sum_recv, small_send, small_recv = rest
    groups = lax.axis_size("seq")
    me = lax.axis_index("seq")
    rows = x.shape[0]
    block = rows // groups
    balls = rows // BALL
    near = groups // balls
    home = me // near
    seat = me % near
    place = Place()
    sums = [
        Sum(place, slot, axes, *sum_boxes[7 * slot : 7 * slot + 7], sum_send, sum_recv)
        for slot, (columns, axes) in enumerate(SUMS)
    ]
    upper, sum_o, sum_q, last = sums[0:2], sums[2], sums[3], sums[4:7]
    small = SmallSum(place, boxes, small_send, small_recv)

    loads = []

    def load(source, target):
        copy = pltpu.make_async_copy(source, target, load_sem.at[len(loads)])
        copy.start()
        loads.append(copy)
        return copy

    lists_in = load(lists, order)
    cot_in = load(cotangent.at[0], cot)
    x_in = load(points.at[0], x)
    small_in = [load(gains, gain), load(w_qkv.at[0], wqkv.at[0]), load(w_out.at[0], wout.at[0])]
    late_in = [load(w_qkv.at[1], wqkv.at[1]), load(w_out.at[1], wout.at[1])]

    barrier = pltpu.get_barrier_semaphore()
    for step in range(1, near):
        pl.semaphore_signal(
            barrier, inc=1, device_id={"seq": home * near + (seat + step) % near}, device_id_type=MESH
        )
    for axis in ("x", "z"):
        for peer in place.peers[axis]:
            pl.semaphore_signal(barrier, inc=1, device_id=place.other(axis, peer), device_id_type=MESH)
    for step in range(2):
        far = (place.at["y"] // 2 * 2 + 2 + step) % 4
        pl.semaphore_signal(barrier, inc=1, device_id=place.other("y", far), device_id_type=MESH)

    def span(index):
        return pl.ds(pl.multiple_of(index * block, block), block)

    others = [(seat + step) % near for step in range(1, near)]

    def transfer(kind, ball, here, there):
        return pltpu.make_async_remote_copy(
            src_ref=sent.at[kind, span(ball * near + there), :],
            dst_ref=got.at[kind, span(ball * near + here), :],
            send_sem=send_sem.at[kind],
            recv_sem=recv_sem.at[kind, ball],
            device_id={"seq": home * near + there},
            device_id_type=MESH,
        )

    def send(kind, ball):
        for peer in others:
            transfer(kind, ball, seat, peer).start()
        own = span(ball * near + seat)
        got[kind, own, :] = sent[kind, own, :]

    def arrive(kind, ball):
        held = got.at[kind, pl.ds(0, (near - 1) * block), :]
        pltpu.make_async_copy(held, held, recv_sem.at[kind, ball]).wait()

    def gather(kind, source, ball):
        sent[kind, cols(ball, PAIR), :] = nn(onto[cols(ball, PAIR), :], source[...]).astype(BF16)

    lists_in.wait()

    @pl.loop(0, rows // 128)
    def _(part):
        first = pl.multiple_of(part * 128, 128)
        onto[pl.ds(first, 128), :] = one_hot_to_rotated(order, first)

    cot_in.wait()
    pl.semaphore_wait(barrier, near - 1 + 8)

    for ball in range(0, balls, PAIR):
        gather(TO_COT, cot, ball)
        for nth in range(PAIR):
            if ball + nth < balls - 1:
                send(TO_COT, ball + nth)

    x_in.wait()
    for copy in small_in:
        copy.wait()
    transpose_by_unit(wqkv.at[0], wqkv_t.at[0])

    @pl.loop(0, balls, step=PAIR)
    def _(ball):
        here = cols(ball, PAIR)
        forward_balls(ball, PAIR, ball, x[here, :], gain[0:1], wqkv_t.at[0], h0, qkv0, p0, att0, inv0)
        y[here, :] = project(x[here, :], att0[:, here], wout.at[0])

    @pl.loop(0, balls, step=PAIR)
    def _(ball):
        gather(TO_X, y, ball)
        for nth in range(PAIR):
            send(TO_X, ball + nth)

    send(TO_COT, balls - 1)

    for copy in late_in:
        copy.wait()
    transpose_by_unit(wqkv.at[1], wqkv_t.at[1])
    g_gain[...] = jnp.zeros_like(g_gain)

    for ball, count in ((0, 1), (1, balls - 2), (balls - 1, 1)):
        here = cols(ball, count)
        for nth in range(count):
            arrive(TO_X, ball + nth)
        forward_balls(ball, count, 0, got[TO_X, here, :], gain[1:2], wqkv_t.at[1], h1, qkv1, p1, att1, inv1)
        for nth in range(count):
            arrive(TO_COT, ball + nth)
        d_r = got[TO_COT, here, :]
        d_att[:, here] = nt(wout[1], d_r).astype(BF16)
        for nth in range(count):
            backward_heads(ball + nth, nth, range(HEADS), d_att, qkv1, p1, att1, inv1, dqkv)
        sent[BACK_D, here, :], gained = backward_norm(
            ball, count, got[TO_X, here, :], gain[1:2], d_r, wqkv.at[1], dqkv
        )
        for nth in range(count):
            send(BACK_D, ball + nth)
        g_gain[1:2] += gained

    stores = []

    def store(source, target):
        copy = pltpu.make_async_copy(source, target, store_sem.at[len(stores)])
        copy.start()
        stores.append(copy)
        return copy

    width = x.shape[1]
    def advance(*which):
        for each in which:
            each.step()

    half = 3 * width // 2
    for nth, each in enumerate(upper):
        each.part[...] = nt(h1[...], dqkv[nth * half : (nth + 1) * half, :]).astype(BF16)
        advance(each)

    @pl.loop(0, balls)
    def _(ball):
        arrive(BACK_D, ball)

    @pl.loop(0, balls, step=PAIR)
    def _(ball):
        here = cols(ball, PAIR)
        y[here, :] = nn(one_hot_to_tree(order, ball * BALL, PAIR * BALL), got[BACK_D]).astype(BF16)
        d_att[:, here] = nt(wout[0], y[here, :]).astype(BF16)

        @pl.when(ball == 0)
        def _():
            advance(*upper)

    span_q = width // GROUPS
    heads = HEADS // GROUPS
    for group in range(GROUPS):

        @pl.loop(0, balls)
        def _(ball):
            backward_heads(
                ball, ball, range(group * heads, (group + 1) * heads), d_att, qkv0, p0, att0, inv0, dqkv
            )

        for kind in range(3):
            low = kind * width + group * span_q
            g = nt(h0[...], dqkv[low : low + span_q, :]).astype(BF16)
            if group == 0:
                sum_q.part[:, kind * span_q : (kind + 1) * span_q] = g
            else:
                last[kind].part[...] = g
                advance(last[kind])
        advance(*upper, sum_q)
        if group == 0:
            sum_o.part[:, :width] = nn(att0[...], y[...]).astype(BF16)
            sum_o.part[:, width:] = nn(att1[...], got[TO_COT]).astype(BF16)
        advance(sum_o)

    @pl.loop(0, balls, step=PAIR)
    def _(ball):
        here = cols(ball, PAIR)
        sent[BACK_R, here, :] = project(got[TO_X, here, :], att1[:, here], wout.at[1])
        for nth in range(PAIR):
            send(BACK_R, ball + nth)

    @pl.loop(0, balls, step=PAIR)
    def _(ball):
        here = cols(ball, PAIR)
        d_x[here, :], gained = backward_norm(
            ball, PAIR, x[here, :], gain[0:1], y[here, :], wqkv.at[0], dqkv
        )
        g_gain[0:1] += gained

        @pl.when(ball == 0)
        def _():
            advance(*last, sum_q, sum_o)

    small.send(g_gain[...])
    advance(*last, sum_q, *upper, sum_o)
    store(d_x, points_out.at[0])

    def store_total(each):
        if each in upper:
            store(each.total, qkv_out.at[1, :, pl.ds(upper.index(each) * half, half)])
        elif each is sum_o:
            store(each.total.at[:, :width], out_out.at[0])
            store(each.total.at[:, width:], out_out.at[1])
        elif each is sum_q:
            for kind in range(3):
                columns = pl.ds(kind * width, span_q)
                store(each.total.at[:, kind * span_q : (kind + 1) * span_q], qkv_out.at[0, :, columns])
        else:
            columns = pl.ds(last.index(each) * width + span_q, span_q)
            store(each.total, qkv_out.at[0, :, columns])

    turn = 0
    while any(each.done < STEPS for each in sums):
        for each in (*last, sum_q, *upper, sum_o):
            if each.done < STEPS:
                each.step()
                if each.done == STEPS:
                    store_total(each)
        if small.done < 3:
            small.send(small.receive())
        elif small.done == 3:
            g_gain[...] = small.receive()
            store(g_gain.at[0:2], gain_out)
        if turn in MIXED_TURNS:
            ball = MIXED_TURNS.index(turn) * PAIR
            if ball == 0:
                for each in range(balls):
                    arrive(BACK_R, each)
            here = cols(ball, PAIR)
            cot[here, :] = nn(one_hot_to_tree(order, ball * BALL, PAIR * BALL), got[BACK_R]).astype(BF16)
            store(cot.at[here, :], mixed_out.at[0, here, :])
        turn += 1
    for copy in stores:
        copy.wait()
    for each in sums:
        each.clear()
    small.clear()

    for kind in range(4):
        held = sent.at[kind, pl.ds(0, balls * (near - 1) * block), :]
        pltpu.make_async_copy(held, held, send_sem.at[kind]).wait()


def finish_kernel(mixed, d_x, gain, qkv, out, mixed_out, points_out, gain_out, qkv_out, out_out, *rest):
    mixed_v, d_x_v, gain_v, qkv_v, out_v, qkv_f, out_f, load_sem, store_sem = rest
    rows = BALL
    moves = [(mixed, mixed_v, mixed_v, mixed_out), (d_x, d_x_v, d_x_v, points_out), (gain, gain_v, gain_v, gain_out)]
    for layer in range(qkv.shape[0]):
        for low in range(0, qkv.shape[1], rows):
            at = (layer, pl.ds(low, rows))
            moves.append((qkv.at[at], qkv_v.at[at], qkv_f.at[at], qkv_out.at[at]))
            moves.append((out.at[at], out_v.at[at], out_f.at[at], out_out.at[at]))
    moves = moves[3:] + moves[:3]
    loads = [pltpu.make_async_copy(m[0], m[1], load_sem.at[i]) for i, m in enumerate(moves)]
    stores = [pltpu.make_async_copy(m[2], m[3], store_sem.at[i]) for i, m in enumerate(moves)]
    for copy in loads:
        copy.start()
    for load, store, (_, held, ready, _) in zip(loads, stores, moves):
        load.wait()
        if held is not ready:
            ready[...] = held[...].astype(F32)
        store.start()
    for copy in stores:
        copy.wait()


def local(points, ball_lists, gains, w_qkv, w_out, cotangent):
    groups = lax.axis_size("seq")
    rows, width = points.shape[1:]
    balls = rows // BALL
    any_place = pl.BlockSpec(memory_space=pl.ANY)

    def saved(keep):
        return [
            pltpu.VMEM((width, rows), BF16),
            pltpu.VMEM((3 * width, rows), BF16),
            pltpu.VMEM((keep, HEADS, BALL, BALL), BF16),
            pltpu.VMEM((width, rows), BF16),
            pltpu.VMEM((keep, HEADS, BALL), F32),
        ]

    token = pltpu.VMEM((rows, width), BF16)

    def sums(columns):
        shapes = [(width, columns), (width, columns), (width // 2, columns), (2, width // 8, columns // 2)]
        shapes += [(2, width // 8, columns), (4, width // 32, columns), (4, width // 32, columns)]
        return [pltpu.VMEM(shape, BF16) for shape in shapes]

    parts = pl.pallas_call(
        kernel,
        out_shape=[
            jax.ShapeDtypeStruct(points.shape, BF16),
            jax.ShapeDtypeStruct(points.shape, BF16),
            jax.ShapeDtypeStruct(gains.shape, F32),
            jax.ShapeDtypeStruct(w_qkv.shape, BF16),
            jax.ShapeDtypeStruct(w_out.shape, BF16),
        ],
        in_specs=[any_place] * 6,
        out_specs=[any_place] * 5,
        scratch_shapes=[
            pltpu.VMEM((1, rows), jnp.int32),
            token,
            token,
            pltpu.VMEM(gains.shape, F32),
            pltpu.VMEM(w_qkv.shape, BF16),
            pltpu.VMEM(w_out.shape, BF16),
            pltpu.VMEM((2, 3 * width, width), BF16),
            pltpu.VMEM((rows, rows), BF16),
            token,
            *saved(balls),
            *saved(balls - 2),
            pltpu.VMEM((3 * width, rows), BF16),
            pltpu.VMEM((width, rows), BF16),
            pltpu.VMEM((4, rows, width), BF16),
            pltpu.VMEM((4, rows, width), BF16),
            token,
            pltpu.VMEM((8, width), F32),
            *[box for columns, _ in SUMS for box in sums(columns)],
            pltpu.VMEM((4, 4, 8, width), F32),
            pltpu.SemaphoreType.DMA((8,)),
            pltpu.SemaphoreType.DMA((16,)),
            pltpu.SemaphoreType.DMA((4,)),
            pltpu.SemaphoreType.DMA((4, balls)),
            pltpu.SemaphoreType.DMA((len(SUMS), 3)),
            pltpu.SemaphoreType.DMA((len(SUMS), 9)),
            pltpu.SemaphoreType.DMA((4,)),
            pltpu.SemaphoreType.DMA((4,)),
        ],
        compiler_params=pltpu.CompilerParams(
            vmem_limit_bytes=VMEM_BYTES, collective_id=0, has_side_effects=True
        ),
    )(points, ball_lists, gains, w_qkv, w_out, cotangent)
    results = [*parts[:3], *(jax.ShapeDtypeStruct(part.shape, F32) for part in parts[3:])]
    moves = 3 + 4 * width // BALL
    return pl.pallas_call(
        finish_kernel,
        out_shape=[jax.ShapeDtypeStruct(result.shape, result.dtype) for result in results],
        in_specs=[any_place] * 5,
        out_specs=[any_place] * 5,
        scratch_shapes=[
            *[pltpu.VMEM(part.shape, part.dtype) for part in parts],
            *[pltpu.VMEM(part.shape, F32) for part in parts[3:]],
            pltpu.SemaphoreType.DMA((moves,)),
            pltpu.SemaphoreType.DMA((moves,)),
        ],
        compiler_params=pltpu.CompilerParams(vmem_limit_bytes=VMEM_BYTES),
    )(*parts)


def solution(mesh):
    return jax.shard_map(
        local,
        mesh=mesh,
        in_specs=(P("dp", "seq", None), P("dp", "seq"), P(), P(), P(), P("dp", "seq", None)),
        out_specs=(P("dp", "seq", None), P("dp", "seq", None), P(), P(), P()),
        check_vma=False,
    )
```

```python
import jax
import jax.numpy as jnp
from jax import lax
from jax.experimental import pallas as pl
from jax.experimental.pallas import tpu as pltpu
from jax.sharding import PartitionSpec as P

MESH = pl.DeviceIdType.MESH
HEADS = 8
BALL = 256
EPS = 1e-05
F32 = jnp.float32
BF16 = jnp.bfloat16
VMEM_BYTES = 62 * 1024 * 1024


def dot(a, b, ca, cb):
    return lax.dot_general(a, b, (((ca,), (cb,)), ((), ())), preferred_element_type=F32)


def nn(a, b):
    return dot(a, b, 1, 0)


def nt(a, b):
    return dot(a, b, 1, 1)


def tn(a, b):
    return dot(a, b, 0, 0)


def cols(ball, count=1):
    return pl.ds(pl.multiple_of(ball * BALL, BALL), count * BALL)


def norm_scale(x):
    return lax.rsqrt(jnp.mean(x * x, axis=1, keepdims=True) + EPS)


def one_hot_to_rotated(order_row, first):
    rows = order_row.shape[1]
    lane = 128
    held = jnp.broadcast_to(order_row[:, pl.ds(pl.multiple_of(first, lane), lane)], (lane, lane)).T
    row = lax.broadcasted_iota(jnp.int32, (lane, lane), 1)
    parts = [jnp.where(held == row + low, 1.0, 0.0).astype(BF16) for low in range(0, rows, lane)]
    return jnp.concatenate(parts, axis=1)


def one_hot_to_tree(order_row, first, rows):
    tree = lax.broadcasted_iota(jnp.int32, (rows, order_row.shape[1]), 0) + first
    return jnp.where(order_row[...] == tree, 1.0, 0.0).astype(BF16)


def transpose_by_unit(wqkv, wqkv_t):
    unit = jnp.where(
        lax.broadcasted_iota(jnp.int32, (BALL, BALL), 0) == lax.broadcasted_iota(jnp.int32, (BALL, BALL), 1), 1.0, 0.0
    ).astype(BF16)

    @pl.loop(0, wqkv.shape[1] // BALL)
    def _(tile):
        wqkv_t[cols(tile), :] = nt(unit, wqkv[:, cols(tile)]).astype(BF16)


def forward_balls(ball, count, keep, x, gain, wqkv_t, wout, h_t, qkv_t, p_t, att_t, inv):
    width = x.shape[1]
    size = width // HEADS
    here = cols(ball, count)
    values = x.astype(F32)
    hidden = (values * norm_scale(values) * gain).astype(BF16)
    hidden_t = hidden.T
    h_t[:, here] = hidden_t
    qkv_t[:, here] = nn(wqkv_t[...], hidden_t).astype(BF16)

    def score(item):
        nth, head = item
        q = qkv_t[rows_of(head, 0, width), cols(ball + nth)] * size ** (-0.5)
        return tn(qkv_t[rows_of(head, 1, width), cols(ball + nth)], q)

    def weigh(item, scores):
        nth, head = item
        weights = jnp.exp(scores - jnp.max(scores, axis=0, keepdims=True))
        share = 1.0 / jnp.sum(weights, axis=0, keepdims=True)
        weights = weights.astype(BF16)
        p_t[keep + nth, head] = weights
        inv[keep + nth, pl.ds(head, 1), :] = share
        return weights, share

    def mix(item, weights, share):
        nth, head = item
        v = qkv_t[rows_of(head, 2, width), cols(ball + nth)]
        att_t[rows_of(head, 0, width), cols(ball + nth)] = (nn(v, weights) * share).astype(BF16)

    @pl.loop(0, count * HEADS, step=ROLL)
    def _(first):
        staggered([(first // HEADS, first % HEADS + each) for each in range(ROLL)], score, weigh, mix)

    return values + tn(att_t[:, here], wout[...])


def rows_of(head, part, width):
    size = width // HEADS
    return pl.ds(pl.multiple_of(part * width + head * size, size), size)


def staggered(heads, *stages):
    heads = list(heads)
    held = {}
    for step in range(len(heads) + len(stages) - 1):
        for index, stage in enumerate(stages):
            if 0 <= step - index < len(heads):
                given = held.pop((step - index, index), ())
                result = stage(heads[step - index], *given)
                held[step - index, index + 1] = result if isinstance(result, tuple) else (result,)


def backward_heads(ball, keep, heads, d_att, qkv_t, p_t, att_t, inv, dqkv_t):
    width = d_att.shape[0]
    size = width // HEADS
    here = cols(ball)

    def weigh(head):
        rows = rows_of(head, 0, width)
        d_out = d_att[rows, here].astype(F32) * inv[keep, pl.ds(head, 1), :]
        delta = jnp.sum(d_out * att_t[rows, here].astype(F32), axis=0, keepdims=True)
        d_out = d_out.astype(BF16)
        return d_out, delta, tn(qkv_t[rows_of(head, 2, width), here], d_out)

    def score(head, d_out, delta, d_weights):
        weights = p_t[keep, head]
        return d_out, weights, (weights.astype(F32) * (d_weights - delta)).astype(BF16)

    def spread(head, d_out, weights, d_scores):
        q = qkv_t[rows_of(head, 0, width), here] * size ** (-0.5)
        k = qkv_t[rows_of(head, 1, width), here]
        dqkv_t[rows_of(head, 0, width), here] = (nn(k, d_scores) * size ** (-0.5)).astype(BF16)
        dqkv_t[rows_of(head, 1, width), here] = nt(q, d_scores).astype(BF16)
        dqkv_t[rows_of(head, 2, width), here] = nt(d_out, weights).astype(BF16)

    @pl.loop(heads.start, heads.stop, step=ROLL)
    def _(first):
        staggered([first + each for each in range(ROLL)], weigh, score, spread)


def backward_norm(ball, count, x, gain, dy, wqkv, dqkv_t):
    d_h = nn(wqkv[...], dqkv_t[:, cols(ball, count)]).T
    values = x.astype(F32)
    scale = norm_scale(values)
    unit = values * scale
    d_unit = d_h * gain
    d_n = scale * (d_unit - unit * jnp.mean(d_unit * unit, axis=1, keepdims=True))
    d_x = dy.astype(F32) + d_n.astype(BF16).astype(F32)
    return d_x.astype(BF16), jnp.sum(d_h * unit, axis=0, keepdims=True)


class Place:
    def __init__(self):
        dp, seq = lax.axis_index("dp"), lax.axis_index("seq")
        self.at = {"x": seq // 4, "y": dp // 4 * 2 + seq // 2 % 2, "z": dp % 4, "core": seq % 2}
        sizes = {"x": 4, "y": 4, "z": 4, "core": 2}
        self.peers = {
            axis: [(self.at[axis] + step) % size for step in range(1, size)] for axis, size in sizes.items()
        }
        self.devices = {
            axis: [(peer, self.other(axis, peer)) for peer in peers] for axis, peers in self.peers.items()
        }

    def device(self, axis, peer):
        for known, device in self.devices[axis]:
            if known is peer:
                return device
        return self.other(axis, peer)

    def other(self, axis, value):
        at = {**self.at, axis: value}
        return {"dp": at["y"] // 2 * 4 + at["z"], "seq": at["x"] * 4 + at["y"] % 2 * 2 + at["core"]}


STEPS = 10
HALVES, TURN, PASS, SPREAD, LAST, COLLECT, SHARE, RELAY, BACK = range(9)


class Sum:
    def __init__(self, place, slot, axes, part, total, halves, turns, quarters, pieces, lasts, send_sem, recv_sem):
        self.place, self.slot, self.axes = place, slot, axes
        self.part, self.total = part, total
        self.halves, self.turns, self.quarters, self.pieces, self.lasts = halves, turns, quarters, pieces, lasts
        self.send_sem, self.recv_sem = send_sem, recv_sem
        rows, columns = part.shape
        self.sizes = [rows, rows // 2, rows // 8, rows // 32]
        base, self.bases = 0, [0]
        for size, name in zip(self.sizes[1:], ("core", *axes)):
            base = base + place.at[name] * size
            self.bases.append(base)
        self.right, self.far, self.left = place.peers[axes[0]]
        self.sides = (pl.ds(0, columns // 2), pl.ds(columns // 2, columns // 2))
        self.done = 0

    def span(self, level, coordinate=None):
        base = self.bases[level] if coordinate is None else self.bases[level - 1] + coordinate * self.sizes[level]
        return pl.ds(pl.multiple_of(base, 16), self.sizes[level])

    def copy(self, source, target, send, recv, axis, peer):
        return pltpu.make_async_remote_copy(
            src_ref=source,
            dst_ref=target,
            send_sem=self.send_sem.at[self.slot, send],
            recv_sem=self.recv_sem.at[self.slot, recv],
            device_id=self.place.device(axis, peer),
            device_id_type=MESH,
        )

    def partner(self, kind):
        peer = self.place.peers["core"][0]
        if kind == HALVES:
            return self.copy(self.part.at[self.span(1, peer), :], self.halves, 0, kind, "core", peer)
        rows = self.total.at[self.span(1), :]
        return self.copy(rows, rows, 0, kind, "core", peer)

    def around(self, kind, way):
        peer = (self.right, self.left)[way]
        other = (self.left, self.right)[way]
        side = self.sides[way]
        if kind == TURN:
            source, target = self.part.at[self.span(2, self.far), side], self.turns.at[way]
        elif kind == PASS:
            source, target = self.part.at[self.span(2, peer), :], self.quarters.at[way]
        elif kind == SHARE:
            source = target = self.total.at[self.span(2), :]
        else:
            source = target = self.total.at[self.span(2, other), side]
        return self.copy(source, target, 1, kind, self.axes[0], peer)

    def along(self, kind, here, there):
        axis = self.axes[2] if kind == LAST else self.axes[1]
        if kind == SPREAD:
            source, target = self.part.at[self.span(3, there), :], self.pieces.at[here]
        elif kind == LAST:
            source = target = self.lasts.at[here]
        else:
            source = target = self.total.at[self.span(3, here), :]
        return self.copy(source, target, 2, kind, axis, there)

    def start_around(self, kind):
        for way in range(2):
            self.around(kind, way).start()

    def start_along(self, kind):
        axis = self.axes[2] if kind == LAST else self.axes[1]
        for peer in self.place.peers[axis]:
            self.along(kind, self.place.at[axis], peer).start()

    def arrive(self, kind):
        rows = self.part.shape[0]
        eighth, last = rows // 8, rows // 32
        held = {
            HALVES: self.halves,
            TURN: self.turns,
            PASS: self.quarters,
            SPREAD: self.pieces.at[pl.ds(0, 3)],
            LAST: self.lasts.at[pl.ds(0, 3)],
            COLLECT: self.total.at[pl.ds(0, 3 * last), :],
            SHARE: self.total.at[pl.ds(0, 2 * eighth), :],
            RELAY: self.total.at[pl.ds(0, eighth), :],
            BACK: self.total.at[pl.ds(0, rows // 2), :],
        }[kind]
        pltpu.make_async_copy(held, held, self.recv_sem.at[self.slot, kind]).wait()

    def add(self, rows, side, *arrived):
        value = self.part[rows, side].astype(F32)
        for each in arrived:
            value += each.astype(F32)
        return value.astype(BF16)

    def step(self):
        step, self.done = self.done, self.done + 1
        everything = pl.ds(0, self.part.shape[1])
        if step == 0:
            self.partner(HALVES).start()
        elif step == 1:
            self.arrive(HALVES)
            base = self.bases[1]

            @pl.loop(0, self.sizes[1] // 32)
            def _(tile):
                rows = pl.ds(pl.multiple_of(base + tile * 32, 32), 32)
                held = pl.ds(pl.multiple_of(tile * 32, 32), 32)
                self.part[rows, :] = self.add(rows, everything, self.halves[held, :])

            self.start_around(TURN)
        elif step == 2:
            self.arrive(TURN)
            for way, peer in enumerate((self.right, self.left)):
                rows, side = self.span(2, peer), self.sides[way]
                self.part[rows, side] = self.add(rows, side, self.turns[way])
            self.start_around(PASS)
        elif step == 3:
            self.arrive(PASS)
            self.part[self.span(2), :] = self.add(self.span(2), everything, self.quarters[0], self.quarters[1])
            self.start_along(SPREAD)
        elif step == 4:
            self.arrive(SPREAD)
            mine = self.place.at[self.axes[2]]
            peers = self.place.peers[self.axes[1]]
            self.lasts[mine] = self.add(self.span(3), everything, *[self.pieces[peer] for peer in peers])
            self.start_along(LAST)
        elif step == 5:
            self.arrive(LAST)
            value = self.lasts[0].astype(F32)
            for peer in range(1, 4):
                value += self.lasts[peer].astype(F32)
            self.total[self.span(3), :] = value.astype(BF16)
            self.start_along(COLLECT)
        elif step == 6:
            self.arrive(COLLECT)
            self.start_around(SHARE)
        elif step == 7:
            self.arrive(SHARE)
            self.start_around(RELAY)
        elif step == 8:
            self.arrive(RELAY)
            self.partner(BACK).start()
        elif step == 9:
            self.arrive(BACK)

    def clear(self):
        rows = self.part.shape[0]
        for index, sent in enumerate((rows, 6 * rows // 8, 9 * rows // 32)):
            held = self.part.at[pl.ds(0, sent), :]
            pltpu.make_async_copy(held, held, self.send_sem.at[self.slot, index]).wait()


class SmallSum:
    axes = ("core", "x", "y", "z")

    def __init__(self, place, boxes, send_sem, recv_sem):
        self.place, self.boxes, self.send_sem, self.recv_sem = place, boxes, send_sem, recv_sem
        self.done = 0

    def hop(self, step, here, there):
        box = self.boxes.at[step, here]
        return pltpu.make_async_remote_copy(
            src_ref=box,
            dst_ref=box,
            send_sem=self.send_sem.at[step],
            recv_sem=self.recv_sem.at[step],
            device_id=self.place.device(self.axes[step], there),
            device_id_type=MESH,
        )

    def send(self, value):
        axis = self.axes[self.done]
        mine = self.place.at[axis]
        self.boxes[self.done, mine] = value
        for peer in self.place.peers[axis]:
            self.hop(self.done, mine, peer).start()

    def receive(self):
        axis = self.axes[self.done]
        self.wait(self.done, self.recv_sem)
        value = self.boxes[self.done, 0]
        for peer in range(1, len(self.place.peers[axis]) + 1):
            value += self.boxes[self.done, peer]
        self.done += 1
        return value

    def wait(self, step, sem):
        held = self.boxes.at[step, pl.ds(0, len(self.place.peers[self.axes[step]]))]
        pltpu.make_async_copy(held, held, sem.at[step]).wait()

    def clear(self):
        for step in range(len(self.axes)):
            self.wait(step, self.send_sem)


TO_X, TO_COT, BACK_R, BACK_D = range(4)
GROUPS = 2
PAIR = 2
ROLL = 4
SUMS = (
    (1024, ("x", "z", "y")),
    (1024, ("z", "x", "y")),
    (512, ("x", "z", "y")),
    (768, ("z", "x", "y")),
    (256, ("x", "y", "z")),
    (256, ("z", "y", "x")),
    (256, ("y", "x", "z")),
)


def kernel(
    points, lists, gains, w_qkv, w_out, cotangent,
    mixed_out, points_out, gain_out, qkv_out, out_out,
    order, x, cot, gain, wqkv, wout, wqkv_t, onto, y,
    h0, qkv0, p0, att0, inv0, h1, qkv1, p1, att1, inv1, dqkv, d_att,
    sent, got, d_x, g_gain, *rest,
):
    sum_boxes, rest = rest[: 7 * len(SUMS)], rest[7 * len(SUMS) :]
    boxes, load_sem, store_sem, send_sem, recv_sem, sum_send, sum_recv, small_send, small_recv = rest
    groups = lax.axis_size("seq")
    me = lax.axis_index("seq")
    rows = x.shape[0]
    block = rows // groups
    balls = rows // BALL
    near = groups // balls
    home = me // near
    seat = me % near
    place = Place()
    sums = [
        Sum(place, slot, axes, *sum_boxes[7 * slot : 7 * slot + 7], sum_send, sum_recv)
        for slot, (columns, axes) in enumerate(SUMS)
    ]
    upper, sum_o, sum_q, last = sums[0:2], sums[2], sums[3], sums[4:7]
    small = SmallSum(place, boxes, small_send, small_recv)

    loads = []

    def load(source, target):
        copy = pltpu.make_async_copy(source, target, load_sem.at[len(loads)])
        copy.start()
        loads.append(copy)
        return copy

    lists_in = load(lists, order)
    cot_in = load(cotangent.at[0], cot)
    x_in = load(points.at[0], x)
    small_in = [load(gains, gain), load(w_qkv.at[0], wqkv.at[0]), load(w_out.at[0], wout.at[0])]
    late_in = [load(w_qkv.at[1], wqkv.at[1]), load(w_out.at[1], wout.at[1])]

    barrier = pltpu.get_barrier_semaphore()
    for step in range(1, near):
        pl.semaphore_signal(
            barrier, inc=1, device_id={"seq": home * near + (seat + step) % near}, device_id_type=MESH
        )
    for axis in ("x", "z"):
        for peer in place.peers[axis]:
            pl.semaphore_signal(barrier, inc=1, device_id=place.other(axis, peer), device_id_type=MESH)
    for step in range(2):
        far = (place.at["y"] // 2 * 2 + 2 + step) % 4
        pl.semaphore_signal(barrier, inc=1, device_id=place.other("y", far), device_id_type=MESH)

    def span(index):
        return pl.ds(pl.multiple_of(index * block, block), block)

    others = [(seat + step) % near for step in range(1, near)]

    def transfer(kind, ball, here, there):
        return pltpu.make_async_remote_copy(
            src_ref=sent.at[kind, span(ball * near + there), :],
            dst_ref=got.at[kind, span(ball * near + here), :],
            send_sem=send_sem.at[kind],
            recv_sem=recv_sem.at[kind, ball],
            device_id={"seq": home * near + there},
            device_id_type=MESH,
        )

    def send(kind, ball):
        for peer in others:
            transfer(kind, ball, seat, peer).start()
        own = span(ball * near + seat)
        got[kind, own, :] = sent[kind, own, :]

    def arrive(kind, ball):
        held = got.at[kind, pl.ds(0, (near - 1) * block), :]
        pltpu.make_async_copy(held, held, recv_sem.at[kind, ball]).wait()

    def gather(kind, source, ball):
        sent[kind, cols(ball, PAIR), :] = nn(onto[cols(ball, PAIR), :], source[...]).astype(BF16)

    lists_in.wait()

    @pl.loop(0, rows // 128)
    def _(part):
        first = pl.multiple_of(part * 128, 128)
        onto[pl.ds(first, 128), :] = one_hot_to_rotated(order, first)

    cot_in.wait()
    pl.semaphore_wait(barrier, near - 1 + 8)

    @pl.loop(0, balls, step=PAIR)
    def _(ball):
        gather(TO_COT, cot, ball)
        for nth in range(PAIR):
            send(TO_COT, ball + nth)

    x_in.wait()
    for copy in small_in:
        copy.wait()
    transpose_by_unit(wqkv.at[0], wqkv_t.at[0])

    @pl.loop(0, balls, step=PAIR)
    def _(ball):
        here = cols(ball, PAIR)
        y[here, :] = forward_balls(
            ball, PAIR, ball, x[here, :], gain[0:1], wqkv_t.at[0], wout.at[0], h0, qkv0, p0, att0, inv0
        ).astype(BF16)

    @pl.loop(0, balls, step=PAIR)
    def _(ball):
        gather(TO_X, y, ball)
        for nth in range(PAIR):
            send(TO_X, ball + nth)

    for copy in late_in:
        copy.wait()
    transpose_by_unit(wqkv.at[1], wqkv_t.at[1])
    g_gain[...] = jnp.zeros_like(g_gain)

    @pl.loop(0, balls)
    def _(ball):
        arrive(TO_X, ball)
        rows_x = got[TO_X, cols(ball), :]
        sent[BACK_R, cols(ball), :] = forward_balls(
            ball, 1, 0, rows_x, gain[1:2], wqkv_t.at[1], wout.at[1], h1, qkv1, p1, att1, inv1
        ).astype(BF16)
        arrive(TO_COT, ball)
        d_r = got[TO_COT, cols(ball), :]
        d_att[:, cols(ball)] = nt(wout[1], d_r).astype(BF16)
        backward_heads(ball, 0, range(HEADS), d_att, qkv1, p1, att1, inv1, dqkv)
        sent[BACK_D, cols(ball), :], gained = backward_norm(
            ball, 1, got[TO_X, cols(ball), :], gain[1:2], d_r, wqkv.at[1], dqkv
        )
        send(BACK_D, ball)
        g_gain[1:2] += gained

    @pl.loop(0, balls)
    def _(ball):
        send(BACK_R, ball)

    stores = []

    def store(source, target):
        copy = pltpu.make_async_copy(source, target, store_sem.at[len(stores)])
        copy.start()
        stores.append(copy)
        return copy

    width = x.shape[1]
    first, second = upper[0].part, upper[1].part

    @pl.loop(0, 2 * width // BALL)
    def _(tile):
        first[:, cols(tile)] = nt(h1[...], dqkv[cols(tile), :]).astype(BF16)

    @pl.loop(0, width // BALL)
    def _(tile):
        second[:, cols(tile)] = nt(h1[...], dqkv[cols(2 * width // BALL + tile), :]).astype(BF16)

    second[:, width:] = nn(att1[...], got[TO_COT]).astype(BF16)

    def advance(*which):
        for each in which:
            each.step()

    advance(*upper)

    @pl.loop(0, balls)
    def _(ball):
        arrive(BACK_D, ball)

    @pl.loop(0, balls, step=PAIR)
    def _(ball):
        here = cols(ball, PAIR)
        y[here, :] = nn(one_hot_to_tree(order, ball * BALL, PAIR * BALL), got[BACK_D]).astype(BF16)
        d_att[:, here] = nt(wout[0], y[here, :]).astype(BF16)

        @pl.when(ball == 0)
        def _():
            advance(*upper)

    sum_o.part[...] = nn(att0[...], y[...]).astype(BF16)
    advance(sum_o)
    span_q = width // GROUPS
    heads = HEADS // GROUPS
    for group in range(GROUPS):

        @pl.loop(0, balls)
        def _(ball):
            backward_heads(
                ball, ball, range(group * heads, (group + 1) * heads), d_att, qkv0, p0, att0, inv0, dqkv
            )

            @pl.when(ball == 2)
            def _():
                advance(sum_o)

        if group == 0:

            @pl.loop(0, 3)
            def _(kind):
                rows = cols(kind * (width // BALL))
                sum_q.part[:, cols(kind)] = nt(h0[...], dqkv[rows, :]).astype(BF16)

        else:
            for kind in range(3):
                rows = cols(kind * (width // BALL) + 1)
                last[kind].part[...] = nt(h0[...], dqkv[rows, :]).astype(BF16)
                advance(last[kind])
        advance(*upper, sum_q)

    @pl.loop(0, balls, step=PAIR)
    def _(ball):
        here = cols(ball, PAIR)
        d_x[here, :], gained = backward_norm(
            ball, PAIR, x[here, :], gain[0:1], y[here, :], wqkv.at[0], dqkv
        )
        g_gain[0:1] += gained

        @pl.when(ball == 0)
        def _():
            advance(*last, sum_q, sum_o)

    small.send(g_gain[...])
    advance(*last, sum_q, *upper, sum_o)
    store(d_x, points_out.at[0])

    @pl.loop(0, balls)
    def _(ball):
        arrive(BACK_R, ball)

    @pl.loop(0, balls, step=PAIR)
    def _(ball):
        here = cols(ball, PAIR)
        cot[here, :] = nn(one_hot_to_tree(order, ball * BALL, PAIR * BALL), got[BACK_R]).astype(BF16)

        @pl.when(ball == 0)
        def _():
            advance(*last, sum_q, sum_o, *upper)

    store(cot, mixed_out.at[0])

    def store_total(each):
        if each is upper[0]:
            store(each.total, qkv_out.at[1, :, : 2 * width])
        elif each is upper[1]:
            store(each.total.at[:, :width], qkv_out.at[1, :, 2 * width :])
            store(each.total.at[:, width:], out_out.at[1])
        elif each is sum_o:
            store(each.total, out_out.at[0])
        elif each is sum_q:
            for kind in range(3):
                columns = pl.ds(kind * width, span_q)
                store(each.total.at[:, kind * span_q : (kind + 1) * span_q], qkv_out.at[0, :, columns])
        else:
            columns = pl.ds(last.index(each) * width + span_q, span_q)
            store(each.total, qkv_out.at[0, :, columns])

    while any(each.done < STEPS for each in sums):
        for each in (*last, sum_q, *upper, sum_o):
            if each.done < STEPS:
                each.step()
                if each.done == STEPS:
                    store_total(each)
        if small.done < 3:
            small.send(small.receive())
        elif small.done == 3:
            g_gain[...] = small.receive()
            store(g_gain.at[0:2], gain_out)
    for copy in stores:
        copy.wait()
    for each in sums:
        each.clear()
    small.clear()

    for kind in range(4):
        held = sent.at[kind, pl.ds(0, balls * (near - 1) * block), :]
        pltpu.make_async_copy(held, held, send_sem.at[kind]).wait()


def finish_kernel(mixed, d_x, gain, qkv, out, mixed_out, points_out, gain_out, qkv_out, out_out, *rest):
    mixed_v, d_x_v, gain_v, qkv_v, out_v, qkv_f, out_f, load_sem, store_sem = rest
    rows = BALL
    moves = [(mixed, mixed_v, mixed_v, mixed_out), (d_x, d_x_v, d_x_v, points_out), (gain, gain_v, gain_v, gain_out)]
    for layer in range(qkv.shape[0]):
        for low in range(0, qkv.shape[1], rows):
            at = (layer, pl.ds(low, rows))
            moves.append((qkv.at[at], qkv_v.at[at], qkv_f.at[at], qkv_out.at[at]))
            moves.append((out.at[at], out_v.at[at], out_f.at[at], out_out.at[at]))
    moves = moves[3:] + moves[:3]
    loads = [pltpu.make_async_copy(m[0], m[1], load_sem.at[i]) for i, m in enumerate(moves)]
    stores = [pltpu.make_async_copy(m[2], m[3], store_sem.at[i]) for i, m in enumerate(moves)]
    for copy in loads:
        copy.start()
    for load, store, (_, held, ready, _) in zip(loads, stores, moves):
        load.wait()
        if held is not ready:
            ready[...] = held[...].astype(F32)
        store.start()
    for copy in stores:
        copy.wait()


def local(points, ball_lists, gains, w_qkv, w_out, cotangent):
    groups = lax.axis_size("seq")
    rows, width = points.shape[1:]
    balls = rows // BALL
    any_place = pl.BlockSpec(memory_space=pl.ANY)

    def saved(keep):
        return [
            pltpu.VMEM((width, rows), BF16),
            pltpu.VMEM((3 * width, rows), BF16),
            pltpu.VMEM((keep, HEADS, BALL, BALL), BF16),
            pltpu.VMEM((width, rows), BF16),
            pltpu.VMEM((keep, HEADS, BALL), F32),
        ]

    token = pltpu.VMEM((rows, width), BF16)

    def sums(columns):
        shapes = [(width, columns), (width, columns), (width // 2, columns), (2, width // 8, columns // 2)]
        shapes += [(2, width // 8, columns), (4, width // 32, columns), (4, width // 32, columns)]
        return [pltpu.VMEM(shape, BF16) for shape in shapes]

    parts = pl.pallas_call(
        kernel,
        out_shape=[
            jax.ShapeDtypeStruct(points.shape, BF16),
            jax.ShapeDtypeStruct(points.shape, BF16),
            jax.ShapeDtypeStruct(gains.shape, F32),
            jax.ShapeDtypeStruct(w_qkv.shape, BF16),
            jax.ShapeDtypeStruct(w_out.shape, BF16),
        ],
        in_specs=[any_place] * 6,
        out_specs=[any_place] * 5,
        scratch_shapes=[
            pltpu.VMEM((1, rows), jnp.int32),
            token,
            token,
            pltpu.VMEM(gains.shape, F32),
            pltpu.VMEM(w_qkv.shape, BF16),
            pltpu.VMEM(w_out.shape, BF16),
            pltpu.VMEM((2, 3 * width, width), BF16),
            pltpu.VMEM((rows, rows), BF16),
            token,
            *saved(balls),
            *saved(1),
            pltpu.VMEM((3 * width, rows), BF16),
            pltpu.VMEM((width, rows), BF16),
            pltpu.VMEM((4, rows, width), BF16),
            pltpu.VMEM((4, rows, width), BF16),
            token,
            pltpu.VMEM((8, width), F32),
            *[box for columns, _ in SUMS for box in sums(columns)],
            pltpu.VMEM((4, 4, 8, width), F32),
            pltpu.SemaphoreType.DMA((8,)),
            pltpu.SemaphoreType.DMA((16,)),
            pltpu.SemaphoreType.DMA((4,)),
            pltpu.SemaphoreType.DMA((4, balls)),
            pltpu.SemaphoreType.DMA((len(SUMS), 3)),
            pltpu.SemaphoreType.DMA((len(SUMS), 9)),
            pltpu.SemaphoreType.DMA((4,)),
            pltpu.SemaphoreType.DMA((4,)),
        ],
        compiler_params=pltpu.CompilerParams(
            vmem_limit_bytes=VMEM_BYTES, collective_id=0, has_side_effects=True
        ),
    )(points, ball_lists, gains, w_qkv, w_out, cotangent)
    results = [*parts[:3], *(jax.ShapeDtypeStruct(part.shape, F32) for part in parts[3:])]
    moves = 3 + 4 * width // BALL
    return pl.pallas_call(
        finish_kernel,
        out_shape=[jax.ShapeDtypeStruct(result.shape, result.dtype) for result in results],
        in_specs=[any_place] * 5,
        out_specs=[any_place] * 5,
        scratch_shapes=[
            *[pltpu.VMEM(part.shape, part.dtype) for part in parts],
            *[pltpu.VMEM(part.shape, F32) for part in parts[3:]],
            pltpu.SemaphoreType.DMA((moves,)),
            pltpu.SemaphoreType.DMA((moves,)),
        ],
        compiler_params=pltpu.CompilerParams(vmem_limit_bytes=VMEM_BYTES),
    )(*parts)


def solution(mesh):
    return jax.shard_map(
        local,
        mesh=mesh,
        in_specs=(P("dp", "seq", None), P("dp", "seq"), P(), P(), P(), P("dp", "seq", None)),
        out_specs=(P("dp", "seq", None), P("dp", "seq", None), P(), P(), P()),
        check_vma=False,
    )
```

```python
import jax
import jax.numpy as jnp
from jax import lax
from jax.experimental import pallas as pl
from jax.experimental.pallas import tpu as pltpu
from jax.sharding import PartitionSpec as P

MESH = pl.DeviceIdType.MESH
HEADS = 8
BALL = 256
EPS = 1e-05
F32 = jnp.float32
BF16 = jnp.bfloat16
VMEM_BYTES = 62 * 1024 * 1024


def dot(a, b, ca, cb):
    return lax.dot_general(a, b, (((ca,), (cb,)), ((), ())), preferred_element_type=F32)


def nn(a, b):
    return dot(a, b, 1, 0)


def nt(a, b):
    return dot(a, b, 1, 1)


def tn(a, b):
    return dot(a, b, 0, 0)


def cols(ball, count=1):
    return pl.ds(pl.multiple_of(ball * BALL, BALL), count * BALL)


def norm_scale(x):
    return lax.rsqrt(jnp.mean(x * x, axis=1, keepdims=True) + EPS)


def one_hot_to_rotated(order_row, first):
    rows = order_row.shape[1]
    lane = 128
    held = jnp.broadcast_to(order_row[:, pl.ds(pl.multiple_of(first, lane), lane)], (lane, lane)).T
    row = lax.broadcasted_iota(jnp.int32, (lane, lane), 1)
    parts = [jnp.where(held == row + low, 1.0, 0.0).astype(BF16) for low in range(0, rows, lane)]
    return jnp.concatenate(parts, axis=1)


def one_hot_to_tree(order_row, first, rows):
    tree = lax.broadcasted_iota(jnp.int32, (rows, order_row.shape[1]), 0) + first
    return jnp.where(order_row[...] == tree, 1.0, 0.0).astype(BF16)


def transpose_by_unit(wqkv, wqkv_t):
    unit = jnp.where(
        lax.broadcasted_iota(jnp.int32, (BALL, BALL), 0) == lax.broadcasted_iota(jnp.int32, (BALL, BALL), 1), 1.0, 0.0
    ).astype(BF16)
    for low in range(0, wqkv.shape[1], BALL):
        wqkv_t[low : low + BALL, :] = nt(unit, wqkv[:, low : low + BALL]).astype(BF16)


def forward_balls(ball, count, keep, x, gain, wqkv_t, wout, h_t, qkv_t, p_t, att_t, inv):
    width = x.shape[1]
    size = width // HEADS
    here = cols(ball, count)
    values = x.astype(F32)
    hidden = (values * norm_scale(values) * gain).astype(BF16)
    hidden_t = hidden.T
    h_t[:, here] = hidden_t
    qkv_t[:, here] = nn(wqkv_t[...], hidden_t).astype(BF16)

    def score(item):
        nth, head = item
        low = head * size
        q = qkv_t[low : low + size, cols(ball + nth)] * size ** (-0.5)
        return tn(qkv_t[width + low : width + low + size, cols(ball + nth)], q)

    def weigh(item, scores):
        nth, head = item
        weights = jnp.exp(scores - jnp.max(scores, axis=0, keepdims=True))
        share = 1.0 / jnp.sum(weights, axis=0, keepdims=True)
        weights = weights.astype(BF16)
        p_t[keep + nth, head] = weights
        inv[keep + nth, head : head + 1, :] = share
        return weights, share

    def mix(item, weights, share):
        nth, head = item
        low = head * size
        v = qkv_t[2 * width + low : 2 * width + low + size, cols(ball + nth)]
        att_t[low : low + size, cols(ball + nth)] = (nn(v, weights) * share).astype(BF16)

    staggered([(nth, head) for nth in range(count) for head in range(HEADS)], score, weigh, mix)
    return values + tn(att_t[:, here], wout[...])


def staggered(heads, *stages):
    heads = list(heads)
    held = {}
    for step in range(len(heads) + len(stages) - 1):
        for index, stage in enumerate(stages):
            if 0 <= step - index < len(heads):
                head = heads[step - index]
                given = held.pop((head, index), ())
                result = stage(head, *given)
                held[head, index + 1] = result if isinstance(result, tuple) else (result,)


def backward_heads(ball, keep, heads, d_att, qkv_t, p_t, att_t, inv, dqkv_t):
    width = d_att.shape[0]
    size = width // HEADS
    here = cols(ball)

    def weigh(head):
        low = head * size
        v = qkv_t[2 * width + low : 2 * width + low + size, here]
        d_out = d_att[low : low + size, here].astype(F32) * inv[keep, head : head + 1, :]
        delta = jnp.sum(d_out * att_t[low : low + size, here].astype(F32), axis=0, keepdims=True)
        d_out = d_out.astype(BF16)
        return d_out, delta, tn(v, d_out)

    def score(head, d_out, delta, d_weights):
        weights = p_t[keep, head]
        return d_out, weights, (weights.astype(F32) * (d_weights - delta)).astype(BF16)

    def spread(head, d_out, weights, d_scores):
        low = head * size
        q = qkv_t[low : low + size, here] * size ** (-0.5)
        k = qkv_t[width + low : width + low + size, here]
        dqkv_t[low : low + size, here] = (nn(k, d_scores) * size ** (-0.5)).astype(BF16)
        dqkv_t[width + low : width + low + size, here] = nt(q, d_scores).astype(BF16)
        dqkv_t[2 * width + low : 2 * width + low + size, here] = nt(d_out, weights).astype(BF16)

    staggered(heads, weigh, score, spread)


def backward_norm(ball, count, x, gain, dy, wqkv, dqkv_t):
    d_h = nn(wqkv[...], dqkv_t[:, cols(ball, count)]).T
    values = x.astype(F32)
    scale = norm_scale(values)
    unit = values * scale
    d_unit = d_h * gain
    d_n = scale * (d_unit - unit * jnp.mean(d_unit * unit, axis=1, keepdims=True))
    d_x = dy.astype(F32) + d_n.astype(BF16).astype(F32)
    return d_x.astype(BF16), jnp.sum(d_h * unit, axis=0, keepdims=True)


class Place:
    def __init__(self):
        dp, seq = lax.axis_index("dp"), lax.axis_index("seq")
        self.at = {"x": seq // 4, "y": dp // 4 * 2 + seq // 2 % 2, "z": dp % 4, "core": seq % 2}
        sizes = {"x": 4, "y": 4, "z": 4, "core": 2}
        self.peers = {
            axis: [(self.at[axis] + step) % size for step in range(1, size)] for axis, size in sizes.items()
        }
        self.devices = {
            axis: [(peer, self.other(axis, peer)) for peer in peers] for axis, peers in self.peers.items()
        }

    def device(self, axis, peer):
        for known, device in self.devices[axis]:
            if known is peer:
                return device
        return self.other(axis, peer)

    def other(self, axis, value):
        at = {**self.at, axis: value}
        return {"dp": at["y"] // 2 * 4 + at["z"], "seq": at["x"] * 4 + at["y"] % 2 * 2 + at["core"]}


STEPS = 10
HALVES, TURN, PASS, SPREAD, LAST, COLLECT, SHARE, RELAY, BACK = range(9)


class Sum:
    def __init__(self, place, slot, axes, part, total, halves, turns, quarters, pieces, lasts, send_sem, recv_sem):
        self.place, self.slot, self.axes = place, slot, axes
        self.part, self.total = part, total
        self.halves, self.turns, self.quarters, self.pieces, self.lasts = halves, turns, quarters, pieces, lasts
        self.send_sem, self.recv_sem = send_sem, recv_sem
        rows, columns = part.shape
        self.sizes = [rows, rows // 2, rows // 8, rows // 32]
        base, self.bases = 0, [0]
        for size, name in zip(self.sizes[1:], ("core", *axes)):
            base = base + place.at[name] * size
            self.bases.append(base)
        self.right, self.far, self.left = place.peers[axes[0]]
        self.sides = (pl.ds(0, columns // 2), pl.ds(columns // 2, columns // 2))
        self.done = 0

    def span(self, level, coordinate=None):
        base = self.bases[level] if coordinate is None else self.bases[level - 1] + coordinate * self.sizes[level]
        return pl.ds(pl.multiple_of(base, 16), self.sizes[level])

    def copy(self, source, target, send, recv, axis, peer):
        return pltpu.make_async_remote_copy(
            src_ref=source,
            dst_ref=target,
            send_sem=self.send_sem.at[self.slot, send],
            recv_sem=self.recv_sem.at[self.slot, recv],
            device_id=self.place.device(axis, peer),
            device_id_type=MESH,
        )

    def partner(self, kind):
        peer = self.place.peers["core"][0]
        if kind == HALVES:
            return self.copy(self.part.at[self.span(1, peer), :], self.halves, 0, kind, "core", peer)
        rows = self.total.at[self.span(1), :]
        return self.copy(rows, rows, 0, kind, "core", peer)

    def around(self, kind, way):
        peer = (self.right, self.left)[way]
        other = (self.left, self.right)[way]
        side = self.sides[way]
        if kind == TURN:
            source, target = self.part.at[self.span(2, self.far), side], self.turns.at[way]
        elif kind == PASS:
            source, target = self.part.at[self.span(2, peer), :], self.quarters.at[way]
        elif kind == SHARE:
            source = target = self.total.at[self.span(2), :]
        else:
            source = target = self.total.at[self.span(2, other), side]
        return self.copy(source, target, 1, kind, self.axes[0], peer)

    def along(self, kind, here, there):
        axis = self.axes[2] if kind == LAST else self.axes[1]
        if kind == SPREAD:
            source, target = self.part.at[self.span(3, there), :], self.pieces.at[here]
        elif kind == LAST:
            source = target = self.lasts.at[here]
        else:
            source = target = self.total.at[self.span(3, here), :]
        return self.copy(source, target, 2, kind, axis, there)

    def start_around(self, kind):
        for way in range(2):
            self.around(kind, way).start()

    def start_along(self, kind):
        axis = self.axes[2] if kind == LAST else self.axes[1]
        for peer in self.place.peers[axis]:
            self.along(kind, self.place.at[axis], peer).start()

    def arrive(self, kind):
        rows = self.part.shape[0]
        eighth, last = rows // 8, rows // 32
        held = {
            HALVES: self.halves,
            TURN: self.turns,
            PASS: self.quarters,
            SPREAD: self.pieces.at[pl.ds(0, 3)],
            LAST: self.lasts.at[pl.ds(0, 3)],
            COLLECT: self.total.at[pl.ds(0, 3 * last), :],
            SHARE: self.total.at[pl.ds(0, 2 * eighth), :],
            RELAY: self.total.at[pl.ds(0, eighth), :],
            BACK: self.total.at[pl.ds(0, rows // 2), :],
        }[kind]
        pltpu.make_async_copy(held, held, self.recv_sem.at[self.slot, kind]).wait()

    def add(self, rows, side, *arrived):
        value = self.part[rows, side].astype(F32)
        for each in arrived:
            value += each.astype(F32)
        return value.astype(BF16)

    def step(self):
        step, self.done = self.done, self.done + 1
        everything = pl.ds(0, self.part.shape[1])
        if step == 0:
            self.partner(HALVES).start()
        elif step == 1:
            self.arrive(HALVES)
            self.part[self.span(1), :] = self.add(self.span(1), everything, self.halves[...])
            self.start_around(TURN)
        elif step == 2:
            self.arrive(TURN)
            for way, peer in enumerate((self.right, self.left)):
                rows, side = self.span(2, peer), self.sides[way]
                self.part[rows, side] = self.add(rows, side, self.turns[way])
            self.start_around(PASS)
        elif step == 3:
            self.arrive(PASS)
            self.part[self.span(2), :] = self.add(self.span(2), everything, self.quarters[0], self.quarters[1])
            self.start_along(SPREAD)
        elif step == 4:
            self.arrive(SPREAD)
            mine = self.place.at[self.axes[2]]
            peers = self.place.peers[self.axes[1]]
            self.lasts[mine] = self.add(self.span(3), everything, *[self.pieces[peer] for peer in peers])
            self.start_along(LAST)
        elif step == 5:
            self.arrive(LAST)
            value = self.lasts[0].astype(F32)
            for peer in range(1, 4):
                value += self.lasts[peer].astype(F32)
            self.total[self.span(3), :] = value.astype(BF16)
            self.start_along(COLLECT)
        elif step == 6:
            self.arrive(COLLECT)
            self.start_around(SHARE)
        elif step == 7:
            self.arrive(SHARE)
            self.start_around(RELAY)
        elif step == 8:
            self.arrive(RELAY)
            self.partner(BACK).start()
        elif step == 9:
            self.arrive(BACK)

    def clear(self):
        rows = self.part.shape[0]
        for index, sent in enumerate((rows, 6 * rows // 8, 9 * rows // 32)):
            held = self.part.at[pl.ds(0, sent), :]
            pltpu.make_async_copy(held, held, self.send_sem.at[self.slot, index]).wait()


class SmallSum:
    axes = ("core", "x", "y", "z")

    def __init__(self, place, boxes, send_sem, recv_sem):
        self.place, self.boxes, self.send_sem, self.recv_sem = place, boxes, send_sem, recv_sem
        self.done = 0

    def hop(self, step, here, there):
        box = self.boxes.at[step, here]
        return pltpu.make_async_remote_copy(
            src_ref=box,
            dst_ref=box,
            send_sem=self.send_sem.at[step],
            recv_sem=self.recv_sem.at[step],
            device_id=self.place.device(self.axes[step], there),
            device_id_type=MESH,
        )

    def send(self, value):
        axis = self.axes[self.done]
        mine = self.place.at[axis]
        self.boxes[self.done, mine] = value
        for peer in self.place.peers[axis]:
            self.hop(self.done, mine, peer).start()

    def receive(self):
        axis = self.axes[self.done]
        self.wait(self.done, self.recv_sem)
        value = self.boxes[self.done, 0]
        for peer in range(1, len(self.place.peers[axis]) + 1):
            value += self.boxes[self.done, peer]
        self.done += 1
        return value

    def wait(self, step, sem):
        held = self.boxes.at[step, pl.ds(0, len(self.place.peers[self.axes[step]]))]
        pltpu.make_async_copy(held, held, sem.at[step]).wait()

    def clear(self):
        for step in range(len(self.axes)):
            self.wait(step, self.send_sem)


TO_X, TO_COT, BACK_R, BACK_D = range(4)
GROUPS = 2
PAIR = 2
SUMS = (
    (1024, ("x", "z", "y")),
    (1024, ("z", "x", "y")),
    (512, ("x", "z", "y")),
    (768, ("z", "x", "y")),
    (256, ("x", "y", "z")),
    (256, ("z", "y", "x")),
    (256, ("y", "x", "z")),
)


def kernel(
    points, lists, gains, w_qkv, w_out, cotangent,
    mixed_out, points_out, gain_out, qkv_out, out_out,
    order, x, cot, gain, wqkv, wout, wqkv_t, onto, y,
    h0, qkv0, p0, att0, inv0, h1, qkv1, p1, att1, inv1, dqkv, d_att,
    sent, got, d_x, g_gain, *rest,
):
    sum_boxes, rest = rest[: 7 * len(SUMS)], rest[7 * len(SUMS) :]
    boxes, load_sem, store_sem, send_sem, recv_sem, sum_send, sum_recv, small_send, small_recv = rest
    groups = lax.axis_size("seq")
    me = lax.axis_index("seq")
    rows = x.shape[0]
    block = rows // groups
    balls = rows // BALL
    near = groups // balls
    home = me // near
    seat = me % near
    place = Place()
    sums = [
        Sum(place, slot, axes, *sum_boxes[7 * slot : 7 * slot + 7], sum_send, sum_recv)
        for slot, (columns, axes) in enumerate(SUMS)
    ]
    upper, sum_o, sum_q, last = sums[0:2], sums[2], sums[3], sums[4:7]
    small = SmallSum(place, boxes, small_send, small_recv)

    loads = []

    def load(source, target):
        copy = pltpu.make_async_copy(source, target, load_sem.at[len(loads)])
        copy.start()
        loads.append(copy)
        return copy

    lists_in = load(lists, order)
    cot_in = load(cotangent.at[0], cot)
    x_in = load(points.at[0], x)
    small_in = [load(gains, gain), load(w_qkv.at[0], wqkv.at[0]), load(w_out.at[0], wout.at[0])]
    late_in = [load(w_qkv.at[1], wqkv.at[1]), load(w_out.at[1], wout.at[1])]

    barrier = pltpu.get_barrier_semaphore()
    for step in range(1, near):
        pl.semaphore_signal(
            barrier, inc=1, device_id={"seq": home * near + (seat + step) % near}, device_id_type=MESH
        )
    for axis in ("x", "z"):
        for peer in place.peers[axis]:
            pl.semaphore_signal(barrier, inc=1, device_id=place.other(axis, peer), device_id_type=MESH)
    for step in range(2):
        far = (place.at["y"] // 2 * 2 + 2 + step) % 4
        pl.semaphore_signal(barrier, inc=1, device_id=place.other("y", far), device_id_type=MESH)

    def span(index):
        return pl.ds(pl.multiple_of(index * block, block), block)

    others = [(seat + step) % near for step in range(1, near)]

    def transfer(kind, ball, here, there):
        return pltpu.make_async_remote_copy(
            src_ref=sent.at[kind, span(ball * near + there), :],
            dst_ref=got.at[kind, span(ball * near + here), :],
            send_sem=send_sem.at[kind],
            recv_sem=recv_sem.at[kind, ball],
            device_id={"seq": home * near + there},
            device_id_type=MESH,
        )

    def send(kind, ball):
        for peer in others:
            transfer(kind, ball, seat, peer).start()
        own = span(ball * near + seat)
        got[kind, own, :] = sent[kind, own, :]

    def arrive(kind, ball):
        held = got.at[kind, pl.ds(0, (near - 1) * block), :]
        pltpu.make_async_copy(held, held, recv_sem.at[kind, ball]).wait()

    def gather(kind, source, ball):
        sent[kind, cols(ball, PAIR), :] = nn(onto[cols(ball, PAIR), :], source[...]).astype(BF16)

    lists_in.wait()

    @pl.loop(0, rows // 128)
    def _(part):
        first = pl.multiple_of(part * 128, 128)
        onto[pl.ds(first, 128), :] = one_hot_to_rotated(order, first)

    cot_in.wait()
    pl.semaphore_wait(barrier, near - 1 + 8)

    @pl.loop(0, balls, step=PAIR)
    def _(ball):
        gather(TO_COT, cot, ball)
        for nth in range(PAIR):
            send(TO_COT, ball + nth)

    x_in.wait()
    for copy in small_in:
        copy.wait()
    transpose_by_unit(wqkv.at[0], wqkv_t.at[0])

    @pl.loop(0, balls, step=PAIR)
    def _(ball):
        here = cols(ball, PAIR)
        y[here, :] = forward_balls(
            ball, PAIR, ball, x[here, :], gain[0:1], wqkv_t.at[0], wout.at[0], h0, qkv0, p0, att0, inv0
        ).astype(BF16)

    @pl.loop(0, balls, step=PAIR)
    def _(ball):
        gather(TO_X, y, ball)
        for nth in range(PAIR):
            send(TO_X, ball + nth)

    for copy in late_in:
        copy.wait()
    transpose_by_unit(wqkv.at[1], wqkv_t.at[1])
    g_gain[...] = jnp.zeros_like(g_gain)

    for ball, count in ((0, 1), (1, balls - 2), (balls - 1, 1)):
        here = cols(ball, count)
        for nth in range(count):
            arrive(TO_X, ball + nth)
        sent[BACK_R, here, :] = forward_balls(
            ball, count, 0, got[TO_X, here, :], gain[1:2], wqkv_t.at[1], wout.at[1], h1, qkv1, p1, att1, inv1
        ).astype(BF16)
        for nth in range(count):
            arrive(TO_COT, ball + nth)
        d_r = got[TO_COT, here, :]
        d_att[:, here] = nt(wout[1], d_r).astype(BF16)
        for nth in range(count):
            backward_heads(ball + nth, nth, range(HEADS), d_att, qkv1, p1, att1, inv1, dqkv)
        sent[BACK_D, here, :], gained = backward_norm(
            ball, count, got[TO_X, here, :], gain[1:2], d_r, wqkv.at[1], dqkv
        )
        for nth in range(count):
            send(BACK_D, ball + nth)
        g_gain[1:2] += gained

    @pl.loop(0, balls)
    def _(ball):
        send(BACK_R, ball)

    stores = []

    def store(source, target):
        copy = pltpu.make_async_copy(source, target, store_sem.at[len(stores)])
        copy.start()
        stores.append(copy)
        return copy

    width = x.shape[1]
    first, second = upper[0].part, upper[1].part
    second[:, width:] = nn(att1[...], got[TO_COT]).astype(BF16)
    first[...] = nt(h1[...], dqkv[: 2 * width, :]).astype(BF16)
    second[:, :width] = nt(h1[...], dqkv[2 * width :, :]).astype(BF16)

    def advance(*which):
        for each in which:
            each.step()

    advance(*upper)

    @pl.loop(0, balls)
    def _(ball):
        arrive(BACK_D, ball)

    @pl.loop(0, balls, step=PAIR)
    def _(ball):
        here = cols(ball, PAIR)
        y[here, :] = nn(one_hot_to_tree(order, ball * BALL, PAIR * BALL), got[BACK_D]).astype(BF16)
        d_att[:, here] = nt(wout[0], y[here, :]).astype(BF16)

        @pl.when(ball == 0)
        def _():
            advance(*upper)

    sum_o.part[...] = nn(att0[...], y[...]).astype(BF16)
    advance(sum_o)
    span_q = width // GROUPS
    heads = HEADS // GROUPS
    for group in range(GROUPS):

        @pl.loop(0, balls)
        def _(ball):
            backward_heads(
                ball, ball, range(group * heads, (group + 1) * heads), d_att, qkv0, p0, att0, inv0, dqkv
            )

            @pl.when(ball == 2)
            def _():
                advance(sum_o)

        for kind in range(3):
            low = kind * width + group * span_q
            g = nt(h0[...], dqkv[low : low + span_q, :]).astype(BF16)
            if group == 0:
                sum_q.part[:, kind * span_q : (kind + 1) * span_q] = g
            else:
                last[kind].part[...] = g
                advance(last[kind])
        advance(*upper, sum_q)

    @pl.loop(0, balls, step=PAIR)
    def _(ball):
        here = cols(ball, PAIR)
        d_x[here, :], gained = backward_norm(
            ball, PAIR, x[here, :], gain[0:1], y[here, :], wqkv.at[0], dqkv
        )
        g_gain[0:1] += gained

        @pl.when(ball == 0)
        def _():
            advance(*last, sum_q, sum_o)

    small.send(g_gain[...])
    advance(*last, sum_q, *upper, sum_o)
    store(d_x, points_out.at[0])

    @pl.loop(0, balls)
    def _(ball):
        arrive(BACK_R, ball)

    @pl.loop(0, balls, step=PAIR)
    def _(ball):
        here = cols(ball, PAIR)
        cot[here, :] = nn(one_hot_to_tree(order, ball * BALL, PAIR * BALL), got[BACK_R]).astype(BF16)

        @pl.when(ball == 0)
        def _():
            advance(*last, sum_q, sum_o, *upper)

    store(cot, mixed_out.at[0])

    def store_total(each):
        if each is upper[0]:
            store(each.total, qkv_out.at[1, :, : 2 * width])
        elif each is upper[1]:
            store(each.total.at[:, :width], qkv_out.at[1, :, 2 * width :])
            store(each.total.at[:, width:], out_out.at[1])
        elif each is sum_o:
            store(each.total, out_out.at[0])
        elif each is sum_q:
            for kind in range(3):
                columns = pl.ds(kind * width, span_q)
                store(each.total.at[:, kind * span_q : (kind + 1) * span_q], qkv_out.at[0, :, columns])
        else:
            columns = pl.ds(last.index(each) * width + span_q, span_q)
            store(each.total, qkv_out.at[0, :, columns])

    while any(each.done < STEPS for each in sums):
        for each in (*last, sum_q, *upper, sum_o):
            if each.done < STEPS:
                each.step()
                if each.done == STEPS:
                    store_total(each)
        if small.done < 3:
            small.send(small.receive())
        elif small.done == 3:
            g_gain[...] = small.receive()
            store(g_gain.at[0:2], gain_out)
    for copy in stores:
        copy.wait()
    for each in sums:
        each.clear()
    small.clear()

    for kind in range(4):
        held = sent.at[kind, pl.ds(0, balls * (near - 1) * block), :]
        pltpu.make_async_copy(held, held, send_sem.at[kind]).wait()


def finish_kernel(mixed, d_x, gain, qkv, out, mixed_out, points_out, gain_out, qkv_out, out_out, *rest):
    mixed_v, d_x_v, gain_v, qkv_v, out_v, qkv_f, out_f, load_sem, store_sem = rest
    rows = BALL
    moves = [(mixed, mixed_v, mixed_v, mixed_out), (d_x, d_x_v, d_x_v, points_out), (gain, gain_v, gain_v, gain_out)]
    for layer in range(qkv.shape[0]):
        for low in range(0, qkv.shape[1], rows):
            at = (layer, pl.ds(low, rows))
            moves.append((qkv.at[at], qkv_v.at[at], qkv_f.at[at], qkv_out.at[at]))
            moves.append((out.at[at], out_v.at[at], out_f.at[at], out_out.at[at]))
    moves = moves[3:] + moves[:3]
    loads = [pltpu.make_async_copy(m[0], m[1], load_sem.at[i]) for i, m in enumerate(moves)]
    stores = [pltpu.make_async_copy(m[2], m[3], store_sem.at[i]) for i, m in enumerate(moves)]
    for copy in loads:
        copy.start()
    for load, store, (_, held, ready, _) in zip(loads, stores, moves):
        load.wait()
        if held is not ready:
            ready[...] = held[...].astype(F32)
        store.start()
    for copy in stores:
        copy.wait()


def local(points, ball_lists, gains, w_qkv, w_out, cotangent):
    groups = lax.axis_size("seq")
    rows, width = points.shape[1:]
    balls = rows // BALL
    any_place = pl.BlockSpec(memory_space=pl.ANY)

    def saved(keep):
        return [
            pltpu.VMEM((width, rows), BF16),
            pltpu.VMEM((3 * width, rows), BF16),
            pltpu.VMEM((keep, HEADS, BALL, BALL), BF16),
            pltpu.VMEM((width, rows), BF16),
            pltpu.VMEM((keep, HEADS, BALL), F32),
        ]

    token = pltpu.VMEM((rows, width), BF16)

    def sums(columns):
        shapes = [(width, columns), (width, columns), (width // 2, columns), (2, width // 8, columns // 2)]
        shapes += [(2, width // 8, columns), (4, width // 32, columns), (4, width // 32, columns)]
        return [pltpu.VMEM(shape, BF16) for shape in shapes]

    parts = pl.pallas_call(
        kernel,
        out_shape=[
            jax.ShapeDtypeStruct(points.shape, BF16),
            jax.ShapeDtypeStruct(points.shape, BF16),
            jax.ShapeDtypeStruct(gains.shape, F32),
            jax.ShapeDtypeStruct(w_qkv.shape, BF16),
            jax.ShapeDtypeStruct(w_out.shape, BF16),
        ],
        in_specs=[any_place] * 6,
        out_specs=[any_place] * 5,
        scratch_shapes=[
            pltpu.VMEM((1, rows), jnp.int32),
            token,
            token,
            pltpu.VMEM(gains.shape, F32),
            pltpu.VMEM(w_qkv.shape, BF16),
            pltpu.VMEM(w_out.shape, BF16),
            pltpu.VMEM((2, 3 * width, width), BF16),
            pltpu.VMEM((rows, rows), BF16),
            token,
            *saved(balls),
            *saved(balls - 2),
            pltpu.VMEM((3 * width, rows), BF16),
            pltpu.VMEM((width, rows), BF16),
            pltpu.VMEM((4, rows, width), BF16),
            pltpu.VMEM((4, rows, width), BF16),
            token,
            pltpu.VMEM((8, width), F32),
            *[box for columns, _ in SUMS for box in sums(columns)],
            pltpu.VMEM((4, 4, 8, width), F32),
            pltpu.SemaphoreType.DMA((8,)),
            pltpu.SemaphoreType.DMA((16,)),
            pltpu.SemaphoreType.DMA((4,)),
            pltpu.SemaphoreType.DMA((4, balls)),
            pltpu.SemaphoreType.DMA((len(SUMS), 3)),
            pltpu.SemaphoreType.DMA((len(SUMS), 9)),
            pltpu.SemaphoreType.DMA((4,)),
            pltpu.SemaphoreType.DMA((4,)),
        ],
        compiler_params=pltpu.CompilerParams(
            vmem_limit_bytes=VMEM_BYTES, collective_id=0, has_side_effects=True
        ),
    )(points, ball_lists, gains, w_qkv, w_out, cotangent)
    results = [*parts[:3], *(jax.ShapeDtypeStruct(part.shape, F32) for part in parts[3:])]
    moves = 3 + 4 * width // BALL
    return pl.pallas_call(
        finish_kernel,
        out_shape=[jax.ShapeDtypeStruct(result.shape, result.dtype) for result in results],
        in_specs=[any_place] * 5,
        out_specs=[any_place] * 5,
        scratch_shapes=[
            *[pltpu.VMEM(part.shape, part.dtype) for part in parts],
            *[pltpu.VMEM(part.shape, F32) for part in parts[3:]],
            pltpu.SemaphoreType.DMA((moves,)),
            pltpu.SemaphoreType.DMA((moves,)),
        ],
        compiler_params=pltpu.CompilerParams(vmem_limit_bytes=VMEM_BYTES),
    )(*parts)


def solution(mesh):
    return jax.shard_map(
        local,
        mesh=mesh,
        in_specs=(P("dp", "seq", None), P("dp", "seq"), P(), P(), P(), P("dp", "seq", None)),
        out_specs=(P("dp", "seq", None), P("dp", "seq", None), P(), P(), P()),
        check_vma=False,
    )
```
